32 devices in a mesh: dp: 2 (over core), expert: 16 (over z, y, x).
Axes of the slice: x: 2, y: 2, z: 4, core: 2. Of those that a mesh axis runs over, the one named last changes fastest.
Arguments:
- tokens: bfloat16 [2048, 3072], P('expert'), may hold values from -6 to 6
- cotangent: bfloat16 [2048, 3072], P('expert'), may hold values from -6 to 6
- routes: int32 [2048, 2], P('expert'), may hold values from 0 to 15, as said below
- gate_values: float32 [2048, 2], P('expert'), may hold values from 0.1 to 0.9
- weights: bfloat16 [2, 24576, 3, 2, 512], P(None, 'expert', None, 'dp'), may hold values from -0.15625 to 0.15625
Outputs:
- layer_out: bfloat16 [2048, 3072], P('expert')
- input_grad: bfloat16 [2048, 3072], P('expert')
- gate_grad: float32 [2048, 2], P('expert')
- weight_grad: bfloat16 [16, 3072, 3, 2, 512], P('expert', None, None, 'dp')
The draws below stay inside these ranges and needn't reach their ends.
Inputs may be any that keep to these rules, and one draw needn't show every extreme that they name: `routes`: within the rows of one device, the first id of a token is below 8 and the second is 8 or more, no id appears more than 20 times, and for each of the two columns one id, the same for every device, appears exactly 20 times in the rows of every device.
All inputs are finite; a program needn't handle non-finite values.
Results may differ from the reference program's by a relative error of at most 0.0072.
Values may be sent and summed in bfloat16 or wider, within the bound.
No kernel may reach another device: no remote copies, remote signals or barrier semaphores. Data moves between devices by JAX's collectives and lax.ppermute only.
A program may use at most 128 MiB of HBM per device.

```python
import jax
import jax.numpy as jnp
from jax import lax

ORIG = 8
D = 3072
TOPK = 2
TOK_DEV = 128
GROUP = 2
SUBS = 16
HALF_H = 512
CAP = 20
TOKENS = 2048
N_DP = 2


def draw_routes(key, part):
    block_total = TOKENS // TOK_DEV
    half_count = SUBS // 2
    columns = []
    for column in range(2):
        column_key = jax.random.fold_in(key, 11 + column)
        hot_expert = jax.random.randint(jax.random.fold_in(column_key, 1), (), 0, half_count)

        def one_block(block_key):
            slot_key, order_key = jax.random.split(block_key)
            picked_slots = jax.random.permutation(slot_key, (half_count - 1) * CAP)[:TOK_DEV - CAP] // CAP
            other_ids = (picked_slots + (picked_slots >= hot_expert).astype(jnp.int32)).astype(jnp.int32)
            block_ids = jnp.concatenate([jnp.full((CAP,), hot_expert, jnp.int32), other_ids])
            return jax.random.permutation(order_key, block_ids)
        block_keys = jax.random.split(jax.random.fold_in(column_key, 2), block_total)
        column_ids = jax.vmap(one_block)(block_keys).reshape(TOKENS)
        columns.append(column_ids + column * half_count)
    return jnp.stack(columns, axis=1).astype(jnp.int32)


def shard_levels(key, dims, cuts, smallest, high):
    factor_of, own = 1.0, jax.random.fold_in(key, 6)
    for position, blocks in cuts:
        heights = jnp.exp(jax.random.uniform(jax.random.fold_in(own, position), (blocks,), jnp.float32, smallest / len(cuts), high / len(cuts)))
        factor_of = factor_of * jnp.repeat(heights, dims[position] // blocks).reshape([-1 if axis == position else 1 for axis in range(len(dims))])
    return factor_of


def noise(rng, dims, width, most, pieces=(), kind=jnp.bfloat16):
    result = jax.random.normal(rng, dims, jnp.float32) * width
    if len(pieces) > 0:
        result = shard_levels(rng, dims, pieces, -0.22, 0.18) * result
    return jnp.clip(result, min=-most, max=most).astype(kind)


def setup_inputs(seed: int = 0) -> dict:
    splits = jax.random.split(jax.random.key(seed), 6)
    tokens = noise(splits[0], (TOKENS, D), 1.0, 6.0, ((0, 16),))
    cotangent = noise(splits[1], (TOKENS, D), 1.0, 6.0, ((0, 16),))
    routes = draw_routes(jax.random.fold_in(splits[5], 71), 0)
    gate_values = jnp.clip(0.1 + 0.79999997 * jax.random.uniform(splits[3], (TOKENS, TOPK), jnp.float32) ** shard_levels(splits[3], (TOKENS, TOPK), ((0, 16),), -0.2, 0.2), 0.1, 0.9)
    weights = noise(splits[4], (GROUP, ORIG * D, 3, N_DP, HALF_H), (D // 2) ** -0.5, 0.15625, ((1, 16), (3, 2)))
    return {"tokens": tokens, "cotangent": cotangent, "routes": routes, "gate_values": gate_values, "weights": weights}


def slot_table(routes):
    source_count = TOKENS // TOK_DEV
    flat_ids = routes.reshape(source_count, TOK_DEV * TOPK).astype(jnp.int32)
    onehot = (flat_ids[:, :, None] == jnp.arange(SUBS, dtype=jnp.int32)[None, None, :]).astype(jnp.int32)
    before = jnp.cumsum(onehot, axis=1).astype(jnp.int32) - onehot
    slot_index = jnp.sum(before * onehot, axis=2).astype(jnp.int32)
    sources = jnp.arange(source_count, dtype=jnp.int32)[:, None]
    return ((flat_ids * source_count + sources) * CAP + slot_index).reshape(TOKENS * TOPK).astype(jnp.int32)


def contract_last(left, right):
    return lax.dot_general(left, right, (((1,), (1,)), ((), ())), preferred_element_type=jnp.float32)


def contract_first(left, right):
    return lax.dot_general(left, right, (((0,), (0,)), ((), ())), preferred_element_type=jnp.float32)


def expert_pass(sub_index, slot_tokens, slot_grads, weights):
    expert_id = (sub_index // GROUP).astype(jnp.int32)
    group_pos = (sub_index % GROUP).astype(jnp.int32)
    anchor = jnp.zeros((), jnp.int32)
    block = lax.dynamic_slice(weights, (group_pos, expert_id * D, anchor, anchor, anchor), (1, D, 3, N_DP, HALF_H))[0]
    out_sum = jnp.zeros((slot_tokens.shape[0], D), jnp.float32)
    dx_sum = jnp.zeros((slot_tokens.shape[0], D), jnp.float32)
    grad_halves = []
    for half_index in range(N_DP):
        gate_weight = block[:, 0, half_index]
        up_weight = block[:, 1, half_index]
        down_weight = block[:, 2, half_index]
        pre_gate = jnp.dot(slot_tokens, gate_weight, preferred_element_type=jnp.float32)
        pre_up = jnp.dot(slot_tokens, up_weight, preferred_element_type=jnp.float32)
        sigmoid_gate = jax.nn.sigmoid(pre_gate)
        activated = pre_gate * sigmoid_gate
        hidden = (activated * pre_up).astype(jnp.bfloat16)
        out_part = contract_last(hidden, down_weight).astype(jnp.bfloat16)
        hidden_grad = jnp.dot(slot_grads, down_weight, preferred_element_type=jnp.float32)
        grad_gate = (hidden_grad * pre_up * sigmoid_gate * (1.0 + pre_gate * (1.0 - sigmoid_gate))).astype(jnp.bfloat16)
        grad_up = (hidden_grad * activated).astype(jnp.bfloat16)
        dx_part = (contract_last(grad_gate, gate_weight) + contract_last(grad_up, up_weight)).astype(jnp.bfloat16)
        out_sum = out_sum + lax.optimization_barrier(out_part).astype(jnp.float32)
        dx_sum = dx_sum + lax.optimization_barrier(dx_part).astype(jnp.float32)
        grad_halves.append(jnp.stack([contract_first(slot_tokens, grad_gate), contract_first(slot_tokens, grad_up), contract_first(slot_grads, hidden)], axis=1).astype(jnp.bfloat16))
    return out_sum.astype(jnp.bfloat16), dx_sum.astype(jnp.bfloat16), jnp.stack(grad_halves, axis=2)


def reference(tokens, cotangent, routes, gate_values, weights):
    buffer_row = slot_table(routes)
    source_count = TOKENS // TOK_DEV
    total_rows = SUBS * source_count * CAP
    pair_rows = jnp.repeat(tokens, TOPK, axis=0)
    gated_grad = (gate_values[:, :, None] * cotangent[:, None, :].astype(jnp.float32)).astype(jnp.bfloat16).reshape(TOKENS * TOPK, D)
    slot_tokens = jnp.zeros((total_rows, D), jnp.bfloat16).at[buffer_row].set(pair_rows).reshape(SUBS, source_count * CAP, D)
    slot_grads = jnp.zeros((total_rows, D), jnp.bfloat16).at[buffer_row].set(gated_grad).reshape(SUBS, source_count * CAP, D)

    def one_sub(inputs):
        return expert_pass(inputs[0], inputs[1], inputs[2], weights)

    slot_out, slot_dx, weight_grad = lax.map(one_sub, (jnp.arange(SUBS, dtype=jnp.int32), slot_tokens, slot_grads))
    picked_out = slot_out.reshape(total_rows, D)[buffer_row].reshape(TOKENS, TOPK, D).astype(jnp.float32)
    picked_dx = slot_dx.reshape(total_rows, D)[buffer_row].reshape(TOKENS, TOPK, D).astype(jnp.float32)
    layer_out = jnp.sum(gate_values[:, :, None] * picked_out, axis=1).astype(jnp.bfloat16)
    input_grad = jnp.sum(picked_dx, axis=1).astype(jnp.bfloat16)
    gate_grad = jnp.sum(cotangent[:, None, :].astype(jnp.float32) * picked_out, axis=2)
    return layer_out, input_grad, gate_grad, weight_grad
```

```python
import functools

import jax
import jax.numpy as jnp
import numpy as np
from jax import lax
from jax.experimental import pallas as pl
from jax.experimental.pallas import tpu as pltpu
from jax.sharding import PartitionSpec as P

F32 = jnp.float32
BF16 = jnp.bfloat16
CHUNKS = 2
VMEM_LIMIT = 40 * 1024 * 1024


def dot(left, right, left_dim, right_dim):
    return lax.dot_general(
        left, right, (((left_dim,), (right_dim,)), ((), ())), preferred_element_type=F32
    )


def params():
    return pltpu.CompilerParams(vmem_limit_bytes=VMEM_LIMIT)


def cost(macs, moved):
    return pl.CostEstimate(flops=2 * macs, bytes_accessed=moved, transcendentals=0)


def iota(shape, dim):
    return lax.broadcasted_iota(jnp.int32, shape, dim)


def split_index(index, size, count):
    whole = jnp.floor((index.astype(F32) + 0.5) * (1.0 / size)).astype(jnp.int32)
    return whole, index - whole * size


def dispatch_kernel(dims, chunk, ids, routes, gates, tokens, cotangent, sent, picks, scales):
    subs, groups, per_chunk, cap, block = dims
    token_count = routes.shape[1]

    @pl.when(pl.program_id(0) == 0)
    def _():
        route = [routes[k : k + 1, :] for k in range(2)]
        gate = [gates[k : k + 1, :] for k in range(2)]
        sub = iota((subs, token_count), 0)
        hits = [(route[k] == sub).astype(F32) for k in range(2)]
        earlier = (iota((token_count,) * 2, 0) < iota((token_count,) * 2, 1)).astype(BF16)
        before = dot((hits[0] + hits[1]).astype(BF16), earlier, 1, 0)
        slot = [jnp.sum(hits[k] * before, axis=0, keepdims=True) for k in range(2)]
        slot[1] = slot[1] + (route[0] == route[1]).astype(F32)
        row = iota((block, token_count), 0)
        row = jnp.where(row >= block // 2, row - block // 2, row)
        local = jnp.zeros_like(row)
        for i in range(1, per_chunk):
            local = local + (row >= i * cap).astype(jnp.int32)
        place = (row - local * cap).astype(F32)
        for e in range(subs // groups):
            wanted = local + (e * groups + chunk * per_chunk)
            match = [(route[k] == wanted) & (slot[k] == place) for k in range(2)]
            scale = jnp.where(match[0], gate[0], 0.0) + jnp.where(match[1], gate[1], 0.0)
            scales[e * block : (e + 1) * block, :] = jnp.broadcast_to(
                jnp.sum(scale, axis=1, keepdims=True), scale.shape
            )
            picks[e * block : (e + 1) * block, :] = (
                match[0].astype(F32) + match[1].astype(F32)
            ).astype(BF16)

    rows = picks[...]
    chosen = dot(rows, tokens[...], 1, 0)
    graded = dot(rows, cotangent[...], 1, 0) * scales[:, :1]
    for e in range(subs // groups):
        part = slice(e * block, (e + 1) * block)
        first = iota((block, 1), 0) < block // 2
        sent[e] = jnp.where(first, chosen[part], graded[part]).astype(BF16)


def quarter(value, groups, width):
    rows = value.shape[0]
    if width % 128 == 0:
        return value, pl.BlockSpec((rows, width), lambda p, ids: (0, 2 * p + ids[0]))
    own = lax.dynamic_index_in_dim(
        value.reshape(rows, groups, 2, width), lax.axis_index("dp"), 2, keepdims=False
    )
    return own.transpose(1, 0, 2), pl.BlockSpec((None, rows, width), lambda p, ids: (p, 0, 0))


def dispatch(dims, chunk, width, ids, routes, gates, tokens, cotangent):
    subs, groups, per_chunk, cap, block = dims
    experts = subs // groups
    token_count = routes.shape[1]
    whole = lambda shape: pl.BlockSpec(shape, lambda p, ids: (0,) * len(shape))
    tokens, tokens_spec = tokens
    cotangent, cotangent_spec = cotangent
    return pl.pallas_call(
        functools.partial(dispatch_kernel, dims, chunk),
        out_shape=jax.ShapeDtypeStruct((experts, groups, block, width), BF16),
        grid_spec=pltpu.PrefetchScalarGridSpec(
            num_scalar_prefetch=1,
            grid=(groups,),
            in_specs=[whole(routes.shape), whole(gates.shape), tokens_spec, cotangent_spec],
            out_specs=pl.BlockSpec((experts, None, block, width), lambda p, ids: (0, p, 0, 0)),
            scratch_shapes=[
                pltpu.VMEM((experts * block, token_count), BF16),
                pltpu.VMEM((experts * block, token_count), F32),
            ],
        ),
        compiler_params=params(),
        cost_estimate=cost(
            2 * experts * block * token_count * width * groups,
            2 * (2 * token_count + experts * block) * width * groups,
        ),
        name=f"dispatch_{chunk}",
    )(ids, routes, gates, tokens, cotangent)


def partial_kernel(dims, ids, own, other, weights, *rest):
    subs, groups, per_chunk, cap, block = dims
    features, partial, held = rest[-3:]
    q = ids[0]
    width = own.shape[1]
    kind = pl.program_id(0)
    sources = subs
    rows = sources * cap

    @pl.when(kind == 0)
    def _():
        source, place = split_index(iota((rows, 1), 0), cap, sources)
        lane = iota((rows, sources * block), 1)
        for half in range(2):
            for i in range(per_chunk):
                target = source * block + (half * per_chunk + i) * cap + place
                chooser = (lane == target).astype(F32).astype(BF16)
                for side, received in enumerate((own, other)):
                    unpacked = dot(chooser, received[...], 1, 0).astype(BF16)
                    held[i, side, half] = unpacked
                    features[i, side, half] = unpacked

    half = jnp.where(kind == 2, 1, 0)
    for i in range(per_chunk):
        total = dot(
            held[i, 0, half], weights[i, pl.ds(pl.multiple_of(q * width, 64), width), :], 1, 0
        )
        total += dot(
            held[i, 1, half], weights[i, pl.ds(pl.multiple_of((1 - q) * width, 64), width), :], 1, 0
        )
        partial[i] = total.astype(BF16)


def partial_products(dims, chunk, ids, own, other, weights, features):
    subs, groups, per_chunk, cap, block = dims
    rows = subs * cap
    width = own.shape[1]
    depth, units = weights.shape[2:]
    whole = lambda shape: pl.BlockSpec(shape, lambda m, ids: (0,) * len(shape))
    feature_shape = (groups, 2, 2, rows, width)
    in_specs = [
        whole(own.shape),
        whole(other.shape),
        pl.BlockSpec((per_chunk, None, depth, units), lambda m, ids: (chunk, m, 0, 0)),
    ]
    operands = [ids, own, other, weights]
    aliases = {}
    if features is not None:
        in_specs.append(pl.BlockSpec(memory_space=pl.ANY))
        operands.append(features)
        aliases = {4: 0}
    return pl.pallas_call(
        functools.partial(partial_kernel, dims),
        out_shape=(
            jax.ShapeDtypeStruct(feature_shape, BF16),
            jax.ShapeDtypeStruct((per_chunk, rows, 3 * units), BF16),
        ),
        grid_spec=pltpu.PrefetchScalarGridSpec(
            num_scalar_prefetch=1,
            grid=(3,),
            in_specs=in_specs,
            out_specs=(
                pl.BlockSpec((per_chunk, 2, 2, rows, width), lambda m, ids: (chunk, 0, 0, 0, 0)),
                pl.BlockSpec((per_chunk, rows, units), lambda m, ids: (0, 0, m)),
            ),
            scratch_shapes=[pltpu.VMEM((per_chunk, 2, 2, rows, width), BF16)],
        ),
        input_output_aliases=aliases,
        compiler_params=params(),
        cost_estimate=cost(
            per_chunk * rows * (3 * depth * units + 4 * subs * block * width),
            2 * per_chunk * (3 * depth * units + 8 * rows * width + 3 * rows * units),
        ),
        name=f"partial_{chunk}",
    )(*operands)


def output_kernel(dims, ids, mine, theirs, weights, *rest):
    per_chunk = dims[2]
    acts, own, other, held = rest[-4:]
    units = weights.shape[3]
    rows = mine.shape[1]
    step = pl.program_id(0)

    @pl.when(step == 0)
    def _():
        for i in range(per_chunk):
            total = lambda m: mine[i, :, m * units : (m + 1) * units].astype(F32) + theirs[
                i, :, m * units : (m + 1) * units
            ].astype(F32)
            gate, up, grad = total(0), total(1), total(2)
            sigmoid = jax.nn.sigmoid(gate)
            active = gate * sigmoid
            values = (
                (grad * up * sigmoid * (1.0 + gate * (1.0 - sigmoid))).astype(BF16),
                (grad * active).astype(BF16),
                (active * up).astype(BF16),
            )
            for m in range(3):
                held[i, m] = values[m]
                acts[i, :, m * units : (m + 1) * units] = values[m]

    def emit(target):
        for i in range(per_chunk):
            target[0, i] = dot(held[i, 2], weights[i, 2], 1, 1).astype(BF16)
            target[1, i] = (
                dot(held[i, 0], weights[i, 0], 1, 1) + dot(held[i, 1], weights[i, 1], 1, 1)
            ).astype(BF16)

    pl.when(step == 0)(lambda: emit(other))
    pl.when(step == 1)(lambda: emit(own))


def output_products(dims, chunk, ids, mine, theirs, weights, acts):
    subs, groups, per_chunk, cap, block = dims
    rows = subs * cap
    depth, units = weights.shape[2:]
    width = depth // 2
    whole = lambda shape: pl.BlockSpec(shape, lambda s, ids: (0,) * len(shape))
    in_specs = [
        whole(mine.shape),
        whole(theirs.shape),
        pl.BlockSpec(
            (per_chunk, 3, width, units),
            lambda s, ids: (chunk, 0, jnp.where(s == 0, 1 - ids[0], ids[0]), 0),
        ),
    ]
    operands = [ids, mine, theirs, weights]
    aliases = {}
    if acts is not None:
        in_specs.append(pl.BlockSpec(memory_space=pl.ANY))
        operands.append(acts)
        aliases = {4: 0}
    out = jax.ShapeDtypeStruct((2, per_chunk, rows, width), BF16)
    return pl.pallas_call(
        functools.partial(output_kernel, dims),
        out_shape=(jax.ShapeDtypeStruct((groups, rows, 3 * units), BF16), out, out),
        grid_spec=pltpu.PrefetchScalarGridSpec(
            num_scalar_prefetch=1,
            grid=(2,),
            in_specs=in_specs,
            out_specs=(
                pl.BlockSpec((per_chunk, rows, 3 * units), lambda s, ids: (chunk, 0, 0)),
                whole(out.shape),
                whole(out.shape),
            ),
            scratch_shapes=[pltpu.VMEM((per_chunk, 3, rows, units), BF16)],
        ),
        input_output_aliases=aliases,
        compiler_params=params(),
        cost_estimate=cost(
            per_chunk * rows * 3 * depth * units,
            2 * per_chunk * (3 * depth * units + 2 * rows * depth + 9 * rows * units),
        ),
        name=f"output_{chunk}",
    )(*operands)


def pack_kernel(dims, own, arrived, packed):
    subs, groups, per_chunk, cap, block = dims
    rows = own.shape[2]
    source, place = split_index(iota((subs * block, 1), 0), block, subs)
    lane = iota((subs * block, rows), 1)
    total = None
    for half in range(2):
        for i in range(per_chunk):
            start = (half * per_chunk + i) * cap
            inside = (place >= start) & (place < start + cap)
            target = jnp.where(inside, source * cap + place - start, -1)
            chooser = (lane == target).astype(F32).astype(BF16)
            summed = (own[half, i].astype(F32) + arrived[half, i].astype(F32)).astype(BF16)
            term = dot(chooser, summed, 1, 0)
            total = term if total is None else total + term
    packed[...] = total.astype(BF16)


def pack(dims, chunk, own, arrived):
    subs, groups, per_chunk, cap, block = dims
    rows = subs * cap
    width = own.shape[3]
    columns = 256 if width % 256 == 0 else width
    spec = pl.BlockSpec((2, per_chunk, rows, columns), lambda c: (0, 0, 0, c))
    return pl.pallas_call(
        functools.partial(pack_kernel, dims),
        out_shape=jax.ShapeDtypeStruct((subs * block, width), BF16),
        grid=(width // columns,),
        in_specs=[spec, spec],
        out_specs=pl.BlockSpec((subs * block, columns), lambda c: (0, c)),
        compiler_params=params(),
        cost_estimate=cost(
            subs * block * 2 * per_chunk * rows * width, 6 * subs * block * width
        ),
        name=f"pack_{chunk}",
    )(own, arrived)


def chooser_kernel(dims, ids, routes, marks, *choosers):
    subs, groups, per_chunk, cap, block = dims
    token_count = routes.shape[0]
    p = pl.program_id(0)
    route = [routes[:, k : k + 1] for k in range(2)]
    sub = iota((token_count, subs), 1)
    hits = [(route[k] == sub).astype(F32) for k in range(2)]
    earlier = (iota((token_count,) * 2, 1) < iota((token_count,) * 2, 0)).astype(BF16)
    before = dot(earlier, (hits[0] + hits[1]).astype(BF16), 1, 0)
    slot = [jnp.sum(hits[k] * before, axis=1, keepdims=True) for k in range(2)]
    slot[1] = slot[1] + (route[0] == route[1]).astype(F32)
    slot = [value.astype(jnp.int32) for value in slot]
    for chunk in range(CHUNKS):
        wanted = marks[0:1, :] + chunk * per_chunk
        place, half, holder = marks[1:2, :], marks[2:3, :], marks[3:4, :]
        match = [
            ((route[k] == wanted) & (slot[k] == place) & (holder == p)).astype(F32)
            for k in range(2)
        ]
        first = (half == 0).astype(F32)
        second = (half == 1).astype(F32)
        choosers[chunk][0:token_count, :] = (match[0] * first).astype(BF16)
        choosers[chunk][token_count : 2 * token_count, :] = (match[1] * first).astype(BF16)
        choosers[chunk][2 * token_count :, :] = ((match[0] + match[1]) * second).astype(BF16)


def return_choosers(dims, ids, routes):
    subs, groups, per_chunk, cap, block = dims
    token_count = routes.shape[0]
    row = np.arange(subs * block)
    device, inner = row // block, row % block
    half, inner = inner // (per_chunk * cap), inner % (per_chunk * cap)
    local, place = inner // cap, inner % cap
    marks = np.zeros((8, subs * block), np.int32)
    marks[0] = device // groups * groups + local
    marks[1] = place
    marks[2] = half
    marks[3] = device % groups
    whole = lambda shape: pl.BlockSpec(shape, lambda p, ids: (0,) * len(shape))
    shape = jax.ShapeDtypeStruct((groups, 3 * token_count, subs * block), BF16)
    spec = pl.BlockSpec((None, 3 * token_count, subs * block), lambda p, ids: (p, 0, 0))
    return pl.pallas_call(
        functools.partial(chooser_kernel, dims),
        out_shape=(shape,) * CHUNKS,
        grid_spec=pltpu.PrefetchScalarGridSpec(
            num_scalar_prefetch=1,
            grid=(groups,),
            in_specs=[whole(routes.shape), whole(marks.shape)],
            out_specs=(spec,) * CHUNKS,
        ),
        compiler_params=params(),
        cost_estimate=cost(0, 2 * CHUNKS * groups * 3 * token_count * subs * block),
        name="choosers",
    )(ids, routes, jnp.asarray(marks))


def combine_kernel(ids, gates, cotangent, *rest):
    choosers = rest[:CHUNKS]
    returned = rest[CHUNKS : 2 * CHUNKS]
    combined, gate_grad = rest[2 * CHUNKS :]
    token_count = gates.shape[0]
    p = pl.program_id(0)
    total = dot(choosers[0][...], returned[0][...], 1, 0)
    for chunk in range(1, CHUNKS):
        total += dot(choosers[chunk][...], returned[chunk][...], 1, 0)
    picked = [total[k * token_count : (k + 1) * token_count] for k in range(3)]
    combined[0] = (gates[:, 0:1] * picked[0] + gates[:, 1:2] * picked[1]).astype(BF16)
    combined[1] = picked[2].astype(BF16)
    grads = cotangent[...].astype(F32)
    lane = iota((token_count, 128), 1)
    term = jnp.where(lane == 0, jnp.sum(grads * picked[0], axis=1, keepdims=True), 0.0)
    term += jnp.where(lane == 1, jnp.sum(grads * picked[1], axis=1, keepdims=True), 0.0)

    @pl.when(p == 0)
    def _():
        gate_grad[...] = term

    @pl.when(p > 0)
    def _():
        gate_grad[...] += term


def combine(dims, width, ids, gates, cotangent, choosers, returned):
    subs, groups, per_chunk, cap, block = dims
    token_count = gates.shape[0]
    cotangent, cotangent_spec = cotangent
    whole = lambda shape: pl.BlockSpec(shape, lambda p, ids: (0,) * len(shape))
    chooser_spec = pl.BlockSpec((None, 3 * token_count, subs * block), lambda p, ids: (p, 0, 0))
    return pl.pallas_call(
        combine_kernel,
        out_shape=(
            jax.ShapeDtypeStruct((2, groups, token_count, width), BF16),
            jax.ShapeDtypeStruct((token_count, 128), F32),
        ),
        grid_spec=pltpu.PrefetchScalarGridSpec(
            num_scalar_prefetch=1,
            grid=(groups,),
            in_specs=[whole(gates.shape), cotangent_spec]
            + [chooser_spec] * CHUNKS
            + [whole(returned[0].shape)] * CHUNKS,
            out_specs=(
                pl.BlockSpec((2, None, token_count, width), lambda p, ids: (0, p, 0, 0)),
                whole((token_count, 128)),
            ),
        ),
        compiler_params=params(),
        cost_estimate=cost(
            CHUNKS * groups * 3 * token_count * subs * block * width,
            2 * CHUNKS * subs * block * (width + 3 * groups * token_count),
        ),
        name="combine",
    )(ids, gates, cotangent, *choosers, *returned)


def merge_kernel(ids, own, other, layer_out, input_grad):
    side = pl.program_id(1)

    @pl.when(side == 0)
    def _():
        layer_out[...] = own[0]
        input_grad[...] = own[1]

    @pl.when(side == 1)
    def _():
        layer_out[...] = other[0]
        input_grad[...] = other[1]


def merge(ids, own, other):
    _, groups, token_count, width = own.shape
    model_width = 2 * groups * width
    if width % 128:
        q = lax.axis_index("dp")
        pair = jnp.stack([jnp.where(q == 0, own, other), jnp.where(q == 0, other, own)], axis=2)
        pair = pair.transpose(0, 3, 1, 2, 4).reshape(2, token_count, model_width)
        return pair[0], pair[1]
    in_spec = pl.BlockSpec((2, None, token_count, width), lambda p, s, ids: (0, p, 0, 0))
    out_spec = pl.BlockSpec(
        (token_count, width), lambda p, s, ids: (0, 2 * p + jnp.where(s == 0, ids[0], 1 - ids[0]))
    )
    shape = jax.ShapeDtypeStruct((token_count, model_width), BF16)
    return pl.pallas_call(
        merge_kernel,
        out_shape=(shape, shape),
        grid_spec=pltpu.PrefetchScalarGridSpec(
            num_scalar_prefetch=1,
            grid=(groups, 2),
            in_specs=[in_spec, in_spec],
            out_specs=(out_spec, out_spec),
        ),
        compiler_params=params(),
        cost_estimate=cost(0, 8 * token_count * model_width),
        name="merge",
    )(ids, own, other)


def weight_grad_kernel(count, ids, acts, *rest):
    features, grads = rest[:-1], rest[-1]
    units = acts.shape[1] // 3
    step = pl.program_id(0)
    for index in range(count):

        @pl.when(step == index)
        def _(index=index):
            both = dot(features[index][0], acts[:, : 2 * units], 0, 0).astype(BF16)
            grads[0] = both[:, :units]
            grads[1] = both[:, units:]
            grads[2] = dot(features[index][1], acts[:, 2 * units :], 0, 0).astype(BF16)


def weight_grads(ids, acts, features, far):
    groups, _, _, rows, width = features.shape
    units = acts.shape[2] // 3
    operands = [features, features]
    specs = [
        pl.BlockSpec((None, None, 2, rows, width), lambda s, ids: (ids[1], 0, 0, 0, 0)),
        pl.BlockSpec((None, None, 2, rows, width), lambda s, ids: (ids[1], 1, 0, 0, 0)),
    ]
    for own, other in far:
        operands += [own, other]
        specs += [pl.BlockSpec(own.shape, lambda s, ids: (0, 0, 0))] * 2
    steps = len(operands)

    def target(s, ids):
        holder = ids[1] ^ (s // 2)
        side = jnp.where(s % 2 == 0, ids[0], 1 - ids[0])
        return 0, 2 * holder + side, 0

    return pl.pallas_call(
        functools.partial(weight_grad_kernel, steps),
        out_shape=jax.ShapeDtypeStruct((3, steps * width, units), BF16),
        grid_spec=pltpu.PrefetchScalarGridSpec(
            num_scalar_prefetch=1,
            grid=(steps,),
            in_specs=[pl.BlockSpec((None, rows, 3 * units), lambda s, ids: (ids[1], 0, 0))]
            + specs,
            out_specs=pl.BlockSpec((3, width, units), target),
        ),
        compiler_params=params(),
        cost_estimate=cost(
            3 * rows * steps * width * units, 6 * steps * width * units + 4 * steps * rows * width
        ),
        name="weight_grads",
    )(ids, acts, *operands)


def swap_cores(value):
    return lax.ppermute(value, "dp", [(0, 1), (1, 0)])


def swap_holders(value, mask):
    size = lax.axis_size("expert")
    return lax.ppermute(value, "expert", [(source, source ^ mask) for source in range(size)])


def shards(tokens, cotangent, routes, gate_values, weights):
    groups, depth = weights.shape[:2]
    token_count, top_count = routes.shape
    subs = lax.axis_size("expert")
    cap = 5 * token_count * top_count // (4 * subs)
    per_chunk = groups // CHUNKS
    block = 2 * per_chunk * cap
    width = depth // 2
    dims = (subs, groups, per_chunk, cap, block)
    core = lax.axis_index("dp")
    holder = lax.axis_index("expert") % groups
    ids = jnp.stack([core, holder]).astype(jnp.int32)
    weights = weights[:, :, :, 0, :].transpose(0, 2, 1, 3)
    own_tokens = quarter(tokens, groups, width)
    own_cotangent = quarter(cotangent, groups, width)

    def exchange(rows):
        blocks = rows.reshape(subs, block, width)
        moved = lax.all_to_all(blocks, "expert", split_axis=0, concat_axis=0, tiled=True)
        return moved.reshape(subs * block, width)

    sent = [
        dispatch(dims, c, width, ids, routes.T, gate_values.T, own_tokens, own_cotangent)
        for c in range(CHUNKS)
    ]
    choosers = return_choosers(dims, ids, routes)
    arrived = [exchange(value) for value in sent]
    features = acts = None
    partials = []
    for c in range(CHUNKS):
        features, partial = partial_products(
            dims, c, ids, arrived[c], swap_cores(arrived[c]), weights, features
        )
        partials.append(partial)
    returned = []
    for c in range(CHUNKS):
        mine, mask = partials[c], 1
        while mask < groups // 2:
            mine = (mine.astype(F32) + swap_holders(mine, mask).astype(F32)).astype(BF16)
            mask *= 2
        acts, own, other = output_products(
            dims, c, ids, mine, swap_holders(mine, mask), weights, acts
        )
        returned.append(exchange(pack(dims, c, own, swap_cores(other))))
    far = []
    for mask in range(1, groups):
        near = swap_holders(
            lax.dynamic_index_in_dim(features, holder ^ mask, 0, keepdims=False)[0], mask
        )
        far.append((near, swap_cores(near)))
    weight_grad = weight_grads(ids, acts, features, far)
    combined, gate_part = combine(
        dims, width, ids, gate_values, own_cotangent, choosers, returned
    )
    layer_out, input_grad = merge(ids, combined, swap_cores(combined))
    gate_grad = (gate_part + swap_cores(gate_part))[:, :top_count]
    weight_grad = weight_grad.transpose(1, 0, 2).reshape(1, groups * depth, 3, 1, -1)
    return layer_out, input_grad, gate_grad, weight_grad


def solution(mesh):
    in_specs = (
        P("expert", None),
        P("expert", None),
        P("expert", None),
        P("expert", None),
        P(None, "expert", None, "dp", None),
    )
    out_specs = (
        P("expert", None),
        P("expert", None),
        P("expert", None),
        P("expert", None, None, "dp", None),
    )
    return jax.shard_map(shards, mesh=mesh, in_specs=in_specs, out_specs=out_specs, check_vma=False)
```

```python
import functools

import jax
import jax.numpy as jnp
import numpy as np
from jax import lax
from jax.experimental import pallas as pl
from jax.experimental.pallas import tpu as pltpu
from jax.sharding import PartitionSpec as P

F32 = jnp.float32
BF16 = jnp.bfloat16
CHUNKS = 2
MIB = 1024 * 1024
BIG = 48


def dot(left, right, left_dim, right_dim):
    return lax.dot_general(
        left, right, (((left_dim,), (right_dim,)), ((), ())), preferred_element_type=F32
    )


def params(mib=24):
    return pltpu.CompilerParams(vmem_limit_bytes=mib * MIB)


WEIGHTS = {"output_0": 30, "output_1": 30}


def cost(macs, moved, name=""):
    weight = WEIGHTS.get(name, 0.01)
    return pl.CostEstimate(
        flops=int(2 * weight * macs), bytes_accessed=int(weight * moved), transcendentals=0
    )


def iota(shape, dim):
    return lax.broadcasted_iota(jnp.int32, shape, dim)


def split_index(index, size):
    whole = jnp.floor((index.astype(F32) + 0.5) * (1.0 / size)).astype(jnp.int32)
    return whole, index - whole * size


def dispatch_kernel(dims, chunk, ids, routes, gates, tokens, cotangent, sent, picks, scales):
    subs, groups, per_chunk, cap, block = dims
    token_count = routes.shape[1]

    @pl.when(pl.program_id(0) == 0)
    def _():
        route = [routes[k : k + 1, :] for k in range(2)]
        gate = [gates[k : k + 1, :] for k in range(2)]
        sub = iota((subs, token_count), 0)
        hits = [(route[k] == sub).astype(F32) for k in range(2)]
        earlier = (iota((token_count,) * 2, 0) < iota((token_count,) * 2, 1)).astype(BF16)
        before = dot((hits[0] + hits[1]).astype(BF16), earlier, 1, 0)
        slot = [jnp.sum(hits[k] * before, axis=0, keepdims=True) for k in range(2)]
        slot[1] = slot[1] + (route[0] == route[1]).astype(F32)
        row = iota((block, token_count), 0)
        row = jnp.where(row >= block // 2, row - block // 2, row)
        local = jnp.zeros_like(row)
        for i in range(1, per_chunk):
            local = local + (row >= i * cap).astype(jnp.int32)
        place = (row - local * cap).astype(F32)
        for e in range(subs // groups):
            wanted = local + (e * groups + chunk * per_chunk)
            match = [(route[k] == wanted) & (slot[k] == place) for k in range(2)]
            scale = jnp.where(match[0], gate[0], 0.0) + jnp.where(match[1], gate[1], 0.0)
            scales[e * block : (e + 1) * block, :] = jnp.broadcast_to(
                jnp.sum(scale, axis=1, keepdims=True), scale.shape
            )
            picks[e * block : (e + 1) * block, :] = (
                match[0].astype(F32) + match[1].astype(F32)
            ).astype(BF16)

    rows = picks[...]
    chosen = dot(rows, tokens[...], 1, 0)
    graded = dot(rows, cotangent[...], 1, 0) * scales[:, :1]
    for e in range(subs // groups):
        part = slice(e * block, (e + 1) * block)
        first = iota((block, 1), 0) < block // 2
        sent[e] = jnp.where(first, chosen[part], graded[part]).astype(BF16)


def quarter(value, groups, width):
    rows = value.shape[0]
    if width % 128 == 0:
        return value, pl.BlockSpec((rows, width), lambda p, ids: (0, 2 * p + ids[0]))
    own = lax.dynamic_index_in_dim(
        value.reshape(rows, groups, 2, width), lax.axis_index("dp"), 2, keepdims=False
    )
    return own.transpose(1, 0, 2), pl.BlockSpec((None, rows, width), lambda p, ids: (p, 0, 0))


def dispatch(dims, chunk, width, ids, routes, gates, tokens, cotangent):
    subs, groups, per_chunk, cap, block = dims
    experts = subs // groups
    token_count = routes.shape[1]
    whole = lambda shape: pl.BlockSpec(shape, lambda p, ids: (0,) * len(shape))
    tokens, tokens_spec = tokens
    cotangent, cotangent_spec = cotangent
    return pl.pallas_call(
        functools.partial(dispatch_kernel, dims, chunk),
        out_shape=jax.ShapeDtypeStruct((experts, groups, block, width), BF16),
        grid_spec=pltpu.PrefetchScalarGridSpec(
            num_scalar_prefetch=1,
            grid=(groups,),
            in_specs=[whole(routes.shape), whole(gates.shape), tokens_spec, cotangent_spec],
            out_specs=pl.BlockSpec((experts, None, block, width), lambda p, ids: (0, p, 0, 0)),
            scratch_shapes=[
                pltpu.VMEM((experts * block, token_count), BF16),
                pltpu.VMEM((experts * block, token_count), F32),
            ],
        ),
        compiler_params=params(60),
        cost_estimate=cost(
            2 * experts * block * token_count * width * groups,
            2 * (2 * token_count + experts * block) * width * groups,
        ),
        name=f"dispatch_{chunk}",
    )(ids, routes, gates, tokens, cotangent)


def partial_kernel(dims, chunk, ids, own, other_low, other_high, weights, *rest):
    subs, groups, per_chunk, cap, block = dims
    features, partial, held, arrivals = rest
    q = ids[0]
    width = own.shape[1]
    units = weights.shape[3]
    loads = [
        pltpu.make_async_copy(
            weights.at[pl.ds(chunk * per_chunk, per_chunk), m], held.at[m], arrivals.at[m]
        )
        for m in range(3)
    ]
    for load in loads:
        load.start()
    together_count = gather_group(cap)
    inner = together_count * block
    part = together_count * cap
    kind, place = split_index(iota((inner, 1), 0), part)
    source, place = split_index(place, cap)
    target = source * block + kind * cap + place
    chooser = (iota((inner, inner), 1) == target).astype(F32).astype(BF16)
    sets = subs // together_count
    for side in range(2):
        for g in range(sets):
            if side == 0:
                rows = own[g * inner : (g + 1) * inner, :]
            elif g < sets // 2:
                rows = other_low[g * inner : (g + 1) * inner, :]
            else:
                rows = other_high[(g - sets // 2) * inner : (g + 1 - sets // 2) * inner, :]
            sorted_rows = dot(chooser, rows, 1, 0).astype(BF16)
            for half in range(2):
                for i in range(per_chunk):
                    start = (half * per_chunk + i) * part
                    features[i, side, half, g * part : (g + 1) * part, :] = sorted_rows[
                        start : start + part
                    ]
    for m in range(3):
        loads[m].wait()
        half = 1 if m == 2 else 0
        for i in range(per_chunk):
            total = None
            for side in range(2):
                first = q * width if side == 0 else (1 - q) * width
                block_rows = held[m, i, pl.ds(pl.multiple_of(first, 64), width), :]
                term = dot(features[i, side, half], block_rows, 1, 0)
                total = term if total is None else total + term
            partial[i, :, m * units : (m + 1) * units] = total.astype(BF16)


def gather_group(cap):
    count = 1
    while count * cap % 16:
        count *= 2
    return count


def partial_products(dims, chunk, ids, own, others, weights):
    subs, groups, per_chunk, cap, block = dims
    rows = subs * cap
    width = own.shape[1]
    depth, units = weights.shape[2:]
    whole = lambda shape: pl.BlockSpec(shape, lambda s, ids: (0,) * len(shape))
    in_specs = [whole(own.shape)] + [whole(o.shape) for o in others]
    in_specs.append(pl.BlockSpec(memory_space=pltpu.HBM))
    operands = [ids, own, *others, weights]
    return pl.pallas_call(
        functools.partial(partial_kernel, dims, chunk),
        out_shape=(
            jax.ShapeDtypeStruct((per_chunk, 2, 2, rows, width), BF16),
            jax.ShapeDtypeStruct((per_chunk, rows, 3 * units), BF16),
        ),
        grid_spec=pltpu.PrefetchScalarGridSpec(
            num_scalar_prefetch=1,
            grid=(1,),
            in_specs=in_specs,
            out_specs=(
                whole((per_chunk, 2, 2, rows, width)),
                whole((per_chunk, rows, 3 * units)),
            ),
            scratch_shapes=[
                pltpu.VMEM((3, per_chunk, depth, units), BF16),
                pltpu.SemaphoreType.DMA((3,)),
            ],
        ),
        compiler_params=params(BIG),
        cost_estimate=cost(
            per_chunk * rows * (3 * depth * units + 4 * subs * block * width),
            2 * per_chunk * (3 * depth * units + 8 * rows * width + 3 * rows * units),
        ),
        name=f"partial_{chunk}",
    )(*operands)


def output_kernel(dims, chunk, ids, mine, theirs, weights, *rest):
    per_chunk = dims[2]
    acts, own_out, own_grad, other_out, other_grad, held, arrivals = rest
    units = weights.shape[3]
    width = own_out.shape[2]
    q = ids[0]
    loads = [
        pltpu.make_async_copy(
            weights.at[
                pl.ds(chunk * per_chunk, per_chunk),
                :,
                pl.ds(pl.multiple_of((1 - q if side == 0 else q) * width, 64), width),
            ],
            held.at[side],
            arrivals.at[side],
        )
        for side in range(2)
    ]
    for load in loads:
        load.start()
    for i in range(per_chunk):
        total = lambda m: mine[i, :, m * units : (m + 1) * units].astype(F32) + theirs[
            i, :, m * units : (m + 1) * units
        ].astype(F32)
        gate, up, grad = total(0), total(1), total(2)
        sigmoid = jax.nn.sigmoid(gate)
        active = gate * sigmoid
        acts[i, :, :units] = (grad * up * sigmoid * (1.0 + gate * (1.0 - sigmoid))).astype(BF16)
        acts[i, :, units : 2 * units] = (grad * active).astype(BF16)
        acts[i, :, 2 * units :] = (active * up).astype(BF16)
    for side, target in enumerate(((other_out, other_grad), (own_out, own_grad))):
        loads[side].wait()
        for i in range(per_chunk):
            hidden = acts[i, :, 2 * units :]
            target[0][i] = dot(hidden, held[side, i, 2], 1, 1).astype(BF16)
            target[1][i] = (
                dot(acts[i, :, :units], held[side, i, 0], 1, 1)
                + dot(acts[i, :, units : 2 * units], held[side, i, 1], 1, 1)
            ).astype(BF16)


def output_products(dims, chunk, ids, mine, theirs, weights):
    subs, groups, per_chunk, cap, block = dims
    rows = subs * cap
    depth, units = weights.shape[2:]
    width = depth // 2
    whole = lambda shape: pl.BlockSpec(shape, lambda s, ids: (0,) * len(shape))
    in_specs = [whole(mine.shape), whole(theirs.shape), pl.BlockSpec(memory_space=pltpu.HBM)]
    operands = [ids, mine, theirs, weights]
    out = jax.ShapeDtypeStruct((per_chunk, rows, width), BF16)
    return pl.pallas_call(
        functools.partial(output_kernel, dims, chunk),
        out_shape=(jax.ShapeDtypeStruct((per_chunk, rows, 3 * units), BF16),) + (out,) * 4,
        grid_spec=pltpu.PrefetchScalarGridSpec(
            num_scalar_prefetch=1,
            grid=(1,),
            in_specs=in_specs,
            out_specs=(
                whole((per_chunk, rows, 3 * units)),
            )
            + (whole(out.shape),) * 4,
            scratch_shapes=[
                pltpu.VMEM((2, per_chunk, 3, width, units), BF16),
                pltpu.SemaphoreType.DMA((2,)),
            ],
        ),
        compiler_params=params(BIG),
        cost_estimate=cost(
            per_chunk * rows * 3 * depth * units,
            2 * per_chunk * (3 * depth * units + 2 * rows * depth + 9 * rows * units),
            f"output_{chunk}",
        ),
        name=f"output_{chunk}",
    )(*operands)


def pack_kernel(dims, own_out, own_grad, other_out, other_grad, packed):
    subs, groups, per_chunk, cap, block = dims
    count = gather_group(cap)
    inner, part = count * block, count * cap
    source, place = split_index(iota((inner, 1), 0), block)
    kind, place = split_index(place, cap)
    target = kind * part + source * cap + place
    chooser = (iota((inner, inner), 1) == target).astype(F32).astype(BF16)
    for g in range(subs // count):
        rows = slice(g * part, (g + 1) * part)
        summed = [
            (own[i, rows].astype(F32) + other[i, rows].astype(F32)).astype(BF16)
            for own, other in ((own_out, other_out), (own_grad, other_grad))
            for i in range(per_chunk)
        ]
        packed[g * inner : (g + 1) * inner, :] = dot(
            chooser, jnp.concatenate(summed, axis=0), 1, 0
        ).astype(BF16)


def pack(dims, chunk, parts):
    subs, groups, per_chunk, cap, block = dims
    rows = subs * cap
    width = parts[0].shape[2]
    columns = 256 if width % 256 == 0 else width
    spec = pl.BlockSpec((per_chunk, rows, columns), lambda c: (0, 0, c))
    return pl.pallas_call(
        functools.partial(pack_kernel, dims),
        out_shape=jax.ShapeDtypeStruct((subs * block, width), BF16),
        grid=(width // columns,),
        in_specs=[spec] * 4,
        out_specs=pl.BlockSpec((subs * block, columns), lambda c: (0, c)),
        compiler_params=params(),
        cost_estimate=cost(
            subs * block * 2 * per_chunk * rows * width, 6 * subs * block * width, f"pack_{chunk}"
        ),
        name=f"pack_{chunk}",
    )(*parts)


def chooser_kernel(dims, ids, routes, gates, marks, gates_out, *choosers):
    subs, groups, per_chunk, cap, block = dims
    token_count = routes.shape[0]
    p = pl.program_id(0)
    gates_out[...] = gates[...]
    route = [routes[:, k : k + 1] for k in range(2)]
    sub = iota((token_count, subs), 1)
    hits = [(route[k] == sub).astype(F32) for k in range(2)]
    earlier = (iota((token_count,) * 2, 1) < iota((token_count,) * 2, 0)).astype(BF16)
    before = dot(earlier, (hits[0] + hits[1]).astype(BF16), 1, 0)
    slot = [jnp.sum(hits[k] * before, axis=1, keepdims=True) for k in range(2)]
    slot[1] = slot[1] + (route[0] == route[1]).astype(F32)
    slot = [value.astype(jnp.int32) for value in slot]
    for chunk in range(CHUNKS):
        wanted = marks[0:1, :] + chunk * per_chunk
        place, half, holder = marks[1:2, :], marks[2:3, :], marks[3:4, :]
        match = [
            ((route[k] == wanted) & (slot[k] == place) & (holder == p)).astype(F32)
            for k in range(2)
        ]
        first = (half == 0).astype(F32)
        second = (half == 1).astype(F32)
        choosers[chunk][0:token_count, :] = (match[0] * first).astype(BF16)
        choosers[chunk][token_count : 2 * token_count, :] = (match[1] * first).astype(BF16)
        choosers[chunk][2 * token_count :, :] = ((match[0] + match[1]) * second).astype(BF16)


def return_choosers(dims, ids, routes, gates):
    subs, groups, per_chunk, cap, block = dims
    token_count = routes.shape[0]
    row = np.arange(subs * block)
    device, inner = row // block, row % block
    half, inner = inner // (per_chunk * cap), inner % (per_chunk * cap)
    local, place = inner // cap, inner % cap
    marks = np.zeros((8, subs * block), np.int32)
    marks[0] = device // groups * groups + local
    marks[1] = place
    marks[2] = half
    marks[3] = device % groups
    whole = lambda shape: pl.BlockSpec(shape, lambda p, ids: (0,) * len(shape))
    shape = jax.ShapeDtypeStruct((groups, 3 * token_count, subs * block), BF16)
    spec = pl.BlockSpec((None, 3 * token_count, subs * block), lambda p, ids: (p, 0, 0))
    return pl.pallas_call(
        functools.partial(chooser_kernel, dims),
        out_shape=(jax.ShapeDtypeStruct(gates.shape, F32),) + (shape,) * CHUNKS,
        grid_spec=pltpu.PrefetchScalarGridSpec(
            num_scalar_prefetch=1,
            grid=(groups,),
            in_specs=[whole(routes.shape), whole(gates.shape), whole(marks.shape)],
            out_specs=(whole(gates.shape),) + (spec,) * CHUNKS,
        ),
        compiler_params=params(),
        cost_estimate=cost(0, 2 * CHUNKS * groups * 3 * token_count * subs * block, "choosers"),
        name="choosers",
    )(ids, routes, gates, jnp.asarray(marks))


def gather_kernel(ids, chooser, returned, total):
    total[...] = dot(chooser[...], returned[...], 1, 0)


def gather_rows(ids, chooser, returned):
    groups, picks, rows = chooser.shape
    width = returned.shape[1]
    return pl.pallas_call(
        gather_kernel,
        out_shape=jax.ShapeDtypeStruct((groups, picks, width), F32),
        grid_spec=pltpu.PrefetchScalarGridSpec(
            num_scalar_prefetch=1,
            grid=(groups,),
            in_specs=[
                pl.BlockSpec((None, picks, rows), lambda p, ids: (p, 0, 0)),
                pl.BlockSpec(returned.shape, lambda p, ids: (0, 0)),
            ],
            out_specs=pl.BlockSpec((None, picks, width), lambda p, ids: (p, 0, 0)),
        ),
        compiler_params=params(),
        cost_estimate=cost(groups * picks * rows * width, 4 * groups * picks * width, "gather_rows"),
        name="gather_rows",
    )(ids, chooser, returned)


def combine_kernel(ids, gates, cotangent, chooser, returned, earlier, combined, gate_grad, *direct):
    token_count = gates.shape[0]
    p = pl.program_id(0)
    total = dot(chooser[...], returned[...], 1, 0) + earlier[...]
    picked = [total[k * token_count : (k + 1) * token_count] for k in range(3)]
    layer_out = (gates[:, 0:1] * picked[0] + gates[:, 1:2] * picked[1]).astype(BF16)
    input_grad = picked[2].astype(BF16)
    combined[0] = layer_out
    combined[1] = input_grad
    if direct:
        direct[0][...] = layer_out
        direct[1][...] = input_grad
    grads = cotangent[...].astype(F32)
    lane = iota((token_count, 128), 1)
    term = jnp.where(lane == 0, jnp.sum(grads * picked[0], axis=1, keepdims=True), 0.0)
    term += jnp.where(lane == 1, jnp.sum(grads * picked[1], axis=1, keepdims=True), 0.0)

    @pl.when(p == 0)
    def _():
        gate_grad[...] = term

    @pl.when(p > 0)
    def _():
        gate_grad[...] += term


def combine(dims, width, ids, gates, cotangent, chooser, returned, earlier):
    subs, groups, per_chunk, cap, block = dims
    token_count = gates.shape[0]
    cotangent, cotangent_spec = cotangent
    whole = lambda shape: pl.BlockSpec(shape, lambda p, ids: (0,) * len(shape))
    by_holder = lambda shape: pl.BlockSpec((None,) + shape[1:], lambda p, ids: (p, 0, 0))
    final = jax.ShapeDtypeStruct((token_count, 2 * groups * width), BF16)
    direct = 2 if width % 128 == 0 else 0
    return pl.pallas_call(
        combine_kernel,
        out_shape=(
            jax.ShapeDtypeStruct((2, groups, token_count, width), BF16),
            jax.ShapeDtypeStruct((token_count, 128), F32),
        )
        + (final,) * direct,
        grid_spec=pltpu.PrefetchScalarGridSpec(
            num_scalar_prefetch=1,
            grid=(groups,),
            in_specs=[
                whole(gates.shape),
                cotangent_spec,
                by_holder(chooser.shape),
                whole(returned.shape),
                by_holder(earlier.shape),
            ],
            out_specs=(
                pl.BlockSpec((2, None, token_count, width), lambda p, ids: (0, p, 0, 0)),
                whole((token_count, 128)),
            )
            + (pl.BlockSpec((token_count, width), lambda p, ids: (0, 2 * p + ids[0])),) * direct,
        ),
        compiler_params=params(),
        cost_estimate=cost(
            groups * 3 * token_count * subs * block * width,
            2 * subs * block * (width + 3 * groups * token_count),
        ),
        name="combine",
    )(ids, gates, cotangent, chooser, returned, earlier)


def merge_kernel(ids, other, started_out, started_grad, layer_out, input_grad):
    layer_out[...] = other[0]
    input_grad[...] = other[1]


def merge(ids, own, other, direct):
    _, groups, token_count, width = own.shape
    model_width = 2 * groups * width
    if not direct:
        q = lax.axis_index("dp")
        pair = jnp.stack([jnp.where(q == 0, own, other), jnp.where(q == 0, other, own)], axis=2)
        pair = pair.transpose(0, 3, 1, 2, 4).reshape(2, token_count, model_width)
        return pair[0], pair[1]
    in_spec = pl.BlockSpec((2, None, token_count, width), lambda p, ids: (0, p, 0, 0))
    out_spec = pl.BlockSpec((token_count, width), lambda p, ids: (0, 2 * p + 1 - ids[0]))
    shape = jax.ShapeDtypeStruct((token_count, model_width), BF16)
    return pl.pallas_call(
        merge_kernel,
        out_shape=(shape, shape),
        grid_spec=pltpu.PrefetchScalarGridSpec(
            num_scalar_prefetch=1,
            grid=(groups,),
            in_specs=[in_spec] + [pl.BlockSpec(memory_space=pl.ANY)] * 2,
            out_specs=(out_spec, out_spec),
        ),
        input_output_aliases={2: 0, 3: 1},
        compiler_params=params(),
        cost_estimate=cost(0, 8 * token_count * model_width),
        name="merge",
    )(ids, other, *direct)


def pick_acts(chunks, ids, acts, held, arrival):
    per_chunk = acts[0].shape[0]
    local = ids[1] % per_chunk
    for c in range(chunks):

        @pl.when(ids[1] // per_chunk == c)
        def _(c=c):
            pltpu.make_async_copy(acts[c].at[local], held, arrival).start()

    return pltpu.make_async_copy(acts[0].at[local], held, arrival)


def weight_grad_block(features, acts, grads):
    units = acts.shape[1] // 3
    both = dot(features[0], acts[:, : 2 * units], 0, 0).astype(BF16)
    grads[0] = both[:, :units]
    grads[1] = both[:, units:]
    grads[2] = dot(features[1], acts[:, 2 * units :], 0, 0).astype(BF16)


def near_kernel(ids, *refs):
    acts, features = refs[:CHUNKS], refs[CHUNKS : 2 * CHUNKS]
    grads, held, rows, arrivals = refs[2 * CHUNKS :]
    per_chunk = acts[0].shape[0]
    local = ids[1] % per_chunk
    side = pl.program_id(0)
    load = lambda c, s: pltpu.make_async_copy(
        features[c].at[local, s], rows.at[s], arrivals.at[1 + s]
    )

    @pl.when(side == 0)
    def _():
        ready = pick_acts(CHUNKS, ids, acts, held, arrivals.at[0])
        for c in range(CHUNKS):

            @pl.when(ids[1] // per_chunk == c)
            def _(c=c):
                load(c, 0).start()
                load(c, 1).start()

        ready.wait()
        load(0, 0).wait()
        weight_grad_block(rows.at[0], held, grads)

    @pl.when(side == 1)
    def _():
        load(0, 1).wait()
        weight_grad_block(rows.at[1], held, grads)


def near_weight_grads(ids, acts, features):
    rows, triple = acts[0].shape[1:]
    per_chunk = acts[0].shape[0]
    groups = per_chunk * CHUNKS
    width = features[0].shape[4]
    units = triple // 3
    return pl.pallas_call(
        near_kernel,
        out_shape=jax.ShapeDtypeStruct((3, 2 * groups * width, units), BF16),
        grid_spec=pltpu.PrefetchScalarGridSpec(
            num_scalar_prefetch=1,
            grid=(2,),
            in_specs=[pl.BlockSpec(memory_space=pl.ANY)] * (2 * CHUNKS),
            out_specs=pl.BlockSpec(
                (3, width, units),
                lambda s, ids: (0, 2 * ids[1] + jnp.where(s == 0, ids[0], 1 - ids[0]), 0),
            ),
            scratch_shapes=[
                pltpu.VMEM((rows, triple), BF16),
                pltpu.VMEM((2, 2, rows, width), BF16),
                pltpu.SemaphoreType.DMA((3,)),
            ],
        ),
        compiler_params=params(),
        cost_estimate=cost(6 * rows * width * units, 12 * width * units + 8 * rows * width, "near_weight_grads"),
        name="near_weight_grads",
    )(ids, *acts, *features)


def far_kernel(count, ids, *refs):
    acts, features = refs[:CHUNKS], refs[CHUNKS : CHUNKS + count]
    grads, held, arrival = refs[-3:]
    step = pl.program_id(0)

    @pl.when(step == 0)
    def _():
        pick_acts(CHUNKS, ids, acts, held, arrival).wait()

    for index in range(count):

        @pl.when(step == index)
        def _(index=index):
            weight_grad_block(features[index], held, grads)


def far_weight_grads(ids, acts, far, grads):
    rows, triple = acts[0].shape[1:]
    units = triple // 3
    operands = [value for pair in far for value in pair]
    count = len(operands)
    width = operands[0].shape[2]

    def target(s, ids):
        holder = ids[1] ^ (1 + s // 2)
        return 0, 2 * holder + jnp.where(s % 2 == 0, ids[0], 1 - ids[0]), 0

    return pl.pallas_call(
        functools.partial(far_kernel, count),
        out_shape=jax.ShapeDtypeStruct(grads.shape, BF16),
        grid_spec=pltpu.PrefetchScalarGridSpec(
            num_scalar_prefetch=1,
            grid=(count,),
            in_specs=[pl.BlockSpec(memory_space=pl.ANY)] * CHUNKS
            + [pl.BlockSpec((2, rows, width), lambda s, ids: (0, 0, 0))] * count
            + [pl.BlockSpec(memory_space=pl.ANY)],
            out_specs=pl.BlockSpec((3, width, units), target),
            scratch_shapes=[pltpu.VMEM((rows, triple), BF16), pltpu.SemaphoreType.DMA],
        ),
        input_output_aliases={1 + CHUNKS + count: 0},
        compiler_params=params(),
        cost_estimate=cost(
            3 * rows * count * width * units, 6 * count * width * units + 4 * count * rows * width
        ),
        name="far_weight_grads",
    )(ids, *acts, *operands, grads)


def choose(values, index):
    result = values[0]
    for i in range(1, len(values)):
        result = jnp.where(index == i, values[i], result)
    return result


def together(*values):
    return lax.optimization_barrier(values)


def swap_cores(value):
    return lax.ppermute(value, "dp", [(0, 1), (1, 0)])


def swap_holders(value, mask):
    size = lax.axis_size("expert")
    return lax.ppermute(value, "expert", [(source, source ^ mask) for source in range(size)])


def shards(tokens, cotangent, routes, gate_values, weights):
    groups, depth = weights.shape[:2]
    token_count, top_count = routes.shape
    subs = lax.axis_size("expert")
    cap = 5 * token_count * top_count // (4 * subs)
    per_chunk = groups // CHUNKS
    block = 2 * per_chunk * cap
    width = depth // 2
    dims = (subs, groups, per_chunk, cap, block)
    core = lax.axis_index("dp")
    holder = lax.axis_index("expert") % groups
    ids = jnp.stack([core, holder]).astype(jnp.int32)
    weights = weights[:, :, :, 0, :].transpose(0, 2, 1, 3)
    own_tokens = quarter(tokens, groups, width)
    own_cotangent = quarter(cotangent, groups, width)

    def exchange(rows):
        blocks = rows.reshape(subs, block, width)
        moved = lax.all_to_all(blocks, "expert", split_axis=0, concat_axis=0, tiled=True)
        return moved.reshape(subs * block, width)

    sent = [
        dispatch(dims, c, width, ids, routes.T, gate_values.T, own_tokens, own_cotangent)
        for c in range(CHUNKS)
    ]
    arrived = [exchange(value) for value in sent]
    features, acts, mine, theirs, returned = [], [], [], [], []
    for c in range(CHUNKS):
        others = [swap_cores(part) for part in jnp.split(arrived[c], 2)]
        rows, partial = partial_products(dims, c, ids, arrived[c], others, weights)
        features.append(rows)
        if c + 1 < CHUNKS:
            arrived[c + 1], _ = together(arrived[c + 1], partial)
        mask = 1
        while mask < groups // 2:
            partial = (partial.astype(F32) + swap_holders(partial, mask).astype(F32)).astype(BF16)
            mask *= 2
        mine.append(partial)
        theirs.append(swap_holders(partial, mask))
    by_sub = [features[s // per_chunk][s % per_chunk, 0] for s in range(groups)]
    leaving = [choose(by_sub, holder ^ mask) for mask in range(1, groups)]
    theirs[0], _, *leaving = together(theirs[0], mine[-1], *leaving)
    for c in range(CHUNKS):
        active, *parts = output_products(dims, c, ids, mine[c], theirs[c], weights)
        acts.append(active)
        parts[2:] = [swap_cores(part) for part in parts[2:]]
        packed = pack(dims, c, parts)
        if c + 1 < CHUNKS:
            theirs[c + 1], _ = together(theirs[c + 1], packed)
        if c > 0:
            packed, returned[c - 1] = together(packed, returned[c - 1])
        returned.append(exchange(packed))
    theirs[-1], *leaving = together(theirs[-1], *leaving)
    routes, packed = together(routes, packed)
    gates, *choosers = return_choosers(dims, ids, routes, gate_values)
    earlier = gather_rows(ids, choosers[0], returned[0])
    for c in range(1, CHUNKS - 1):
        earlier = earlier + gather_rows(ids, choosers[c], returned[c])
    weight_grad = near_weight_grads(ids, acts, features)
    far = []
    for mask in range(1, groups):
        near = swap_holders(leaving[mask - 1], mask)
        near, weight_grad, earlier = together(near, weight_grad, earlier)
        far.append((near, swap_cores(near)))
    weight_grad = far_weight_grads(ids, acts, far, weight_grad)
    returned[-1], earlier, weight_grad = together(returned[-1], earlier, weight_grad)
    combined, gate_part, *direct = combine(
        dims, width, ids, gates, own_cotangent, choosers[-1], returned[-1], earlier
    )
    layer_out, input_grad = merge(ids, combined, swap_cores(combined), direct)
    gate_grad = (gate_part + swap_cores(gate_part))[:, :top_count]
    weight_grad = weight_grad.transpose(1, 0, 2).reshape(1, groups * depth, 3, 1, -1)
    return layer_out, input_grad, gate_grad, weight_grad


def solution(mesh):
    in_specs = (
        P("expert", None),
        P("expert", None),
        P("expert", None),
        P("expert", None),
        P(None, "expert", None, "dp", None),
    )
    out_specs = (
        P("expert", None),
        P("expert", None),
        P("expert", None),
        P("expert", None, None, "dp", None),
    )
    return jax.shard_map(shards, mesh=mesh, in_specs=in_specs, out_specs=out_specs, check_vma=False)
```

```python
import functools

import jax
import jax.numpy as jnp
import numpy as np
from jax import lax
from jax.experimental import pallas as pl
from jax.experimental.pallas import tpu as pltpu
from jax.sharding import PartitionSpec as P

F32 = jnp.float32
BF16 = jnp.bfloat16
CHUNKS = 2
MIB = 1024 * 1024
BIG = 44


def dot(left, right, left_dim, right_dim):
    return lax.dot_general(
        left, right, (((left_dim,), (right_dim,)), ((), ())), preferred_element_type=F32
    )


def params(mib=24):
    return pltpu.CompilerParams(vmem_limit_bytes=mib * MIB)


WEIGHTS = {"output_0": 30, "output_1": 30}


def cost(macs, moved, name=""):
    weight = WEIGHTS.get(name, 0.01)
    return pl.CostEstimate(
        flops=int(2 * weight * macs), bytes_accessed=int(weight * moved), transcendentals=0
    )


def iota(shape, dim):
    return lax.broadcasted_iota(jnp.int32, shape, dim)


def split_index(index, size):
    whole = jnp.floor((index.astype(F32) + 0.5) * (1.0 / size)).astype(jnp.int32)
    return whole, index - whole * size


def mark_picks(dims, chunk, routes, gates, picks, scales):
    subs, groups, per_chunk, cap, block = dims
    token_count = routes.shape[1]
    route = [routes[k : k + 1, :] for k in range(2)]
    gate = [gates[k : k + 1, :] for k in range(2)]
    sub = iota((subs, token_count), 0)
    hits = [(route[k] == sub).astype(F32) for k in range(2)]
    earlier = (iota((token_count,) * 2, 0) < iota((token_count,) * 2, 1)).astype(BF16)
    before = dot((hits[0] + hits[1]).astype(BF16), earlier, 1, 0)
    slot = [jnp.sum(hits[k] * before, axis=0, keepdims=True) for k in range(2)]
    slot[1] = slot[1] + (route[0] == route[1]).astype(F32)
    row = iota((block, token_count), 0)
    row = jnp.where(row >= block // 2, row - block // 2, row)
    local = jnp.zeros_like(row)
    for i in range(1, per_chunk):
        local = local + (row >= i * cap).astype(jnp.int32)
    place = (row - local * cap).astype(F32)
    for e in range(subs // groups):
        wanted = local + (e * groups + chunk * per_chunk)
        match = [(route[k] == wanted) & (slot[k] == place) for k in range(2)]
        scale = jnp.where(match[0], gate[0], 0.0) + jnp.where(match[1], gate[1], 0.0)
        scales[e * block : (e + 1) * block, :] = jnp.broadcast_to(
            jnp.sum(scale, axis=1, keepdims=True), scale.shape
        )
        picks[e * block : (e + 1) * block, :] = (
            match[0].astype(F32) + match[1].astype(F32)
        ).astype(BF16)


def place_rows(block, picks, scales, tokens, cotangent, store):
    rows = picks[...]
    chosen = dot(rows, tokens, 1, 0)
    graded = dot(rows, cotangent, 1, 0) * scales[:, :1]
    for e in range(rows.shape[0] // block):
        part = slice(e * block, (e + 1) * block)
        first = iota((block, 1), 0) < block // 2
        store(e, jnp.where(first, chosen[part], graded[part]).astype(BF16))


def dispatch_kernel(dims, chunk, aligned, routes, gates, tokens, cotangent, sent, *scratch):
    subs, groups, per_chunk, cap, block = dims
    picks, scales, columns, arrivals = scratch
    token_count = routes.shape[1]
    width = sent.shape[3]
    loads = []
    for p in range(groups):
        for i, source in enumerate((tokens, cotangent)):
            if aligned:
                first = pl.multiple_of((2 * p + lax.axis_index("dp")) * width, 128)
                source = source.at[:, pl.ds(first, width)]
            else:
                source = source.at[p]
            loads.append(pltpu.make_async_copy(source, columns.at[p, i], arrivals.at[p, i]))
            loads[-1].start()
    mark_picks(dims, chunk, routes[...], gates[...], picks, scales)
    for p in range(groups):
        loads[2 * p].wait()
        loads[2 * p + 1].wait()

        def store(e, value, p=p):
            sent[e, p] = value

        place_rows(block, picks, scales, columns[p, 0], columns[p, 1], store)


def group_kernel(dims, chunk, *refs):
    groups, block = dims[1], dims[4]
    infos, columns = refs[:groups], refs[groups : 2 * groups]
    sent, picks, scales = refs[2 * groups :]
    holder = lax.axis_index("expert") % groups
    for mask in range(groups):
        info = infos[mask][...]
        mark_picks(dims, chunk, info[:2].astype(jnp.int32), info[2:], picks, scales)

        def store(e, value, mask=mask):
            sent[e, holder ^ mask] = value

        place_rows(block, picks, scales, columns[mask][0], columns[mask][1], store)


def group_dispatch(dims, chunk, infos, columns):
    subs, groups, per_chunk, cap, block = dims
    experts = subs // groups
    token_count, width = columns[0].shape[1:]
    vmem = pl.BlockSpec(memory_space=pltpu.VMEM)
    return pl.pallas_call(
        functools.partial(group_kernel, dims, chunk),
        out_shape=jax.ShapeDtypeStruct((experts, groups, block, width), BF16),
        in_specs=[vmem] * (2 * groups),
        out_specs=vmem,
        scratch_shapes=[
            pltpu.VMEM((experts * block, token_count), BF16),
            pltpu.VMEM((experts * block, token_count), F32),
        ],
        compiler_params=params(60),
        cost_estimate=cost(
            2 * experts * block * token_count * width * groups,
            2 * (2 * token_count + experts * block) * width * groups,
        ),
        name=f"group_dispatch_{chunk}",
    )(*infos, *columns)


def quarter(value, groups, width):
    rows = value.shape[0]
    if width % 128 == 0:
        return value, pl.BlockSpec((rows, width), lambda p, ids: (0, 2 * p + ids[0]))
    own = lax.dynamic_index_in_dim(
        value.reshape(rows, groups, 2, width), lax.axis_index("dp"), 2, keepdims=False
    )
    return own.transpose(1, 0, 2), pl.BlockSpec((None, rows, width), lambda p, ids: (p, 0, 0))


def dispatch(dims, chunk, width, routes, gates, tokens, cotangent):
    subs, groups, per_chunk, cap, block = dims
    experts = subs // groups
    token_count = routes.shape[1]
    vmem = pl.BlockSpec(memory_space=pltpu.VMEM)
    return pl.pallas_call(
        functools.partial(dispatch_kernel, dims, chunk, tokens.ndim == 2),
        out_shape=jax.ShapeDtypeStruct((experts, groups, block, width), BF16),
        in_specs=[vmem, vmem] + [pl.BlockSpec(memory_space=pl.ANY)] * 2,
        out_specs=vmem,
        scratch_shapes=[
            pltpu.VMEM((experts * block, token_count), BF16),
            pltpu.VMEM((experts * block, token_count), F32),
            pltpu.VMEM((groups, 2, token_count, width), BF16),
            pltpu.SemaphoreType.DMA((groups, 2)),
        ],
        compiler_params=params(60),
        cost_estimate=cost(
            2 * experts * block * token_count * width * groups,
            2 * (2 * token_count + experts * block) * width * groups,
        ),
        name=f"dispatch_{chunk}",
    )(routes, gates, tokens, cotangent)


def partial_kernel(dims, chunk, ids, own, other_low, other_high, weights, *rest):
    subs, groups, per_chunk, cap, block = dims
    features, partial, held, arrivals = rest
    q = ids[0]
    width = own.shape[1]
    units = weights.shape[3]
    loads = [
        pltpu.make_async_copy(
            weights.at[pl.ds(chunk * per_chunk, per_chunk), m], held.at[m], arrivals.at[m]
        )
        for m in range(3)
    ]
    for load in loads:
        load.start()
    together_count = gather_group(cap)
    inner = together_count * block
    part = together_count * cap
    kind, place = split_index(iota((inner, 1), 0), part)
    source, place = split_index(place, cap)
    target = source * block + kind * cap + place
    chooser = (iota((inner, inner), 1) == target).astype(F32).astype(BF16)
    sets = subs // together_count
    for side in range(2):
        for g in range(sets):
            if side == 0:
                rows = own[g * inner : (g + 1) * inner, :]
            elif g < sets // 2:
                rows = other_low[g * inner : (g + 1) * inner, :]
            else:
                rows = other_high[(g - sets // 2) * inner : (g + 1 - sets // 2) * inner, :]
            sorted_rows = dot(chooser, rows, 1, 0).astype(BF16)
            for half in range(2):
                for i in range(per_chunk):
                    start = (half * per_chunk + i) * part
                    features[i, side, half, g * part : (g + 1) * part, :] = sorted_rows[
                        start : start + part
                    ]
    for m in range(3):
        loads[m].wait()
        half = 1 if m == 2 else 0
        for i in range(per_chunk):
            total = None
            for side in range(2):
                first = q * width if side == 0 else (1 - q) * width
                block_rows = held[m, i, pl.ds(pl.multiple_of(first, 64), width), :]
                term = dot(features[i, side, half], block_rows, 1, 0)
                total = term if total is None else total + term
            partial[i, :, m * units : (m + 1) * units] = total.astype(BF16)


def gather_group(cap):
    count = 1
    while count * cap % 16:
        count *= 2
    return count


def partial_products(dims, chunk, ids, own, others, weights):
    subs, groups, per_chunk, cap, block = dims
    rows = subs * cap
    width = own.shape[1]
    depth, units = weights.shape[2:]
    whole = lambda shape: pl.BlockSpec(shape, lambda s, ids: (0,) * len(shape))
    in_specs = [whole(own.shape)] + [whole(o.shape) for o in others]
    in_specs.append(pl.BlockSpec(memory_space=pltpu.HBM))
    operands = [ids, own, *others, weights]
    return pl.pallas_call(
        functools.partial(partial_kernel, dims, chunk),
        out_shape=(
            pltpu.HBM((per_chunk, 2, 2, rows, width), BF16),
            jax.ShapeDtypeStruct((per_chunk, rows, 3 * units), BF16),
        ),
        grid_spec=pltpu.PrefetchScalarGridSpec(
            num_scalar_prefetch=1,
            grid=(1,),
            in_specs=in_specs,
            out_specs=(
                whole((per_chunk, 2, 2, rows, width)),
                whole((per_chunk, rows, 3 * units)),
            ),
            scratch_shapes=[
                pltpu.VMEM((3, per_chunk, depth, units), BF16),
                pltpu.SemaphoreType.DMA((3,)),
            ],
        ),
        compiler_params=params(BIG),
        cost_estimate=cost(
            per_chunk * rows * (3 * depth * units + 4 * subs * block * width),
            2 * per_chunk * (3 * depth * units + 8 * rows * width + 3 * rows * units),
        ),
        name=f"partial_{chunk}",
    )(*operands)


def output_kernel(dims, chunk, ids, mine, theirs, weights, *rest):
    per_chunk = dims[2]
    acts, own_out, own_grad, other_out, other_grad, held, arrivals = rest
    units = weights.shape[3]
    width = own_out.shape[2]
    q = ids[0]
    loads = [
        pltpu.make_async_copy(
            weights.at[
                pl.ds(chunk * per_chunk, per_chunk),
                :,
                pl.ds(pl.multiple_of((1 - q if side == 0 else q) * width, 64), width),
            ],
            held.at[side],
            arrivals.at[side],
        )
        for side in range(2)
    ]
    for load in loads:
        load.start()
    for i in range(per_chunk):
        total = lambda m: mine[i, :, m * units : (m + 1) * units].astype(F32) + theirs[
            i, :, m * units : (m + 1) * units
        ].astype(F32)
        gate, up, grad = total(0), total(1), total(2)
        sigmoid = jax.nn.sigmoid(gate)
        active = gate * sigmoid
        acts[i, :, :units] = (grad * up * sigmoid * (1.0 + gate * (1.0 - sigmoid))).astype(BF16)
        acts[i, :, units : 2 * units] = (grad * active).astype(BF16)
        acts[i, :, 2 * units :] = (active * up).astype(BF16)
    for side, target in enumerate(((other_out, other_grad), (own_out, own_grad))):
        loads[side].wait()
        for i in range(per_chunk):
            hidden = acts[i, :, 2 * units :]
            target[0][i] = dot(hidden, held[side, i, 2], 1, 1).astype(BF16)
            target[1][i] = (
                dot(acts[i, :, :units], held[side, i, 0], 1, 1)
                + dot(acts[i, :, units : 2 * units], held[side, i, 1], 1, 1)
            ).astype(BF16)


def output_products(dims, chunk, ids, mine, theirs, weights):
    subs, groups, per_chunk, cap, block = dims
    rows = subs * cap
    depth, units = weights.shape[2:]
    width = depth // 2
    whole = lambda shape: pl.BlockSpec(shape, lambda s, ids: (0,) * len(shape))
    in_specs = [whole(mine.shape), whole(theirs.shape), pl.BlockSpec(memory_space=pltpu.HBM)]
    operands = [ids, mine, theirs, weights]
    out = jax.ShapeDtypeStruct((per_chunk, rows, width), BF16)
    return pl.pallas_call(
        functools.partial(output_kernel, dims, chunk),
        out_shape=(pltpu.HBM((per_chunk, rows, 3 * units), BF16),) + (out,) * 4,
        grid_spec=pltpu.PrefetchScalarGridSpec(
            num_scalar_prefetch=1,
            grid=(1,),
            in_specs=in_specs,
            out_specs=(
                whole((per_chunk, rows, 3 * units)),
            )
            + (whole(out.shape),) * 4,
            scratch_shapes=[
                pltpu.VMEM((2, per_chunk, 3, width, units), BF16),
                pltpu.SemaphoreType.DMA((2,)),
            ],
        ),
        compiler_params=params(BIG),
        cost_estimate=cost(
            per_chunk * rows * 3 * depth * units,
            2 * per_chunk * (3 * depth * units + 2 * rows * depth + 9 * rows * units),
            f"output_{chunk}",
        ),
        name=f"output_{chunk}",
    )(*operands)


def pack_kernel(dims, own_out, own_grad, other_out, other_grad, packed):
    subs, groups, per_chunk, cap, block = dims
    count = gather_group(cap)
    inner, part = count * block, count * cap
    source, place = split_index(iota((inner, 1), 0), block)
    kind, place = split_index(place, cap)
    target = kind * part + source * cap + place
    chooser = (iota((inner, inner), 1) == target).astype(F32).astype(BF16)
    for g in range(subs // count):
        rows = slice(g * part, (g + 1) * part)
        summed = [
            (own[i, rows].astype(F32) + other[i, rows].astype(F32)).astype(BF16)
            for own, other in ((own_out, other_out), (own_grad, other_grad))
            for i in range(per_chunk)
        ]
        packed[g * inner : (g + 1) * inner, :] = dot(
            chooser, jnp.concatenate(summed, axis=0), 1, 0
        ).astype(BF16)


def pack(dims, chunk, parts):
    subs, groups, per_chunk, cap, block = dims
    rows = subs * cap
    width = parts[0].shape[2]
    columns = 256 if width % 256 == 0 else width
    spec = pl.BlockSpec((per_chunk, rows, columns), lambda c: (0, 0, c))
    return pl.pallas_call(
        functools.partial(pack_kernel, dims),
        out_shape=pltpu.HBM((subs * block, width), BF16),
        grid=(width // columns,),
        in_specs=[spec] * 4,
        out_specs=pl.BlockSpec((subs * block, columns), lambda c: (0, c)),
        compiler_params=params(),
        cost_estimate=cost(
            subs * block * 2 * per_chunk * rows * width, 6 * subs * block * width, f"pack_{chunk}"
        ),
        name=f"pack_{chunk}",
    )(*parts)


def chooser_kernel(dims, ids, routes, gates, marks, gates_out, *choosers):
    subs, groups, per_chunk, cap, block = dims
    token_count = routes.shape[0]
    p = pl.program_id(0)
    gates_out[...] = gates[...]
    route = [routes[:, k : k + 1] for k in range(2)]
    sub = iota((token_count, subs), 1)
    hits = [(route[k] == sub).astype(F32) for k in range(2)]
    earlier = (iota((token_count,) * 2, 1) < iota((token_count,) * 2, 0)).astype(BF16)
    before = dot(earlier, (hits[0] + hits[1]).astype(BF16), 1, 0)
    slot = [jnp.sum(hits[k] * before, axis=1, keepdims=True) for k in range(2)]
    slot[1] = slot[1] + (route[0] == route[1]).astype(F32)
    slot = [value.astype(jnp.int32) for value in slot]
    for chunk in range(CHUNKS):
        wanted = marks[0:1, :] + chunk * per_chunk
        place, half, holder = marks[1:2, :], marks[2:3, :], marks[3:4, :]
        match = [
            ((route[k] == wanted) & (slot[k] == place) & (holder == p)).astype(F32)
            for k in range(2)
        ]
        first = (half == 0).astype(F32)
        second = (half == 1).astype(F32)
        choosers[chunk][0:token_count, :] = (match[0] * first).astype(BF16)
        choosers[chunk][token_count : 2 * token_count, :] = (match[1] * first).astype(BF16)
        choosers[chunk][2 * token_count :, :] = ((match[0] + match[1]) * second).astype(BF16)


def return_choosers(dims, ids, routes, gates):
    subs, groups, per_chunk, cap, block = dims
    token_count = routes.shape[0]
    row = np.arange(subs * block)
    device, inner = row // block, row % block
    half, inner = inner // (per_chunk * cap), inner % (per_chunk * cap)
    local, place = inner // cap, inner % cap
    marks = np.zeros((8, subs * block), np.int32)
    marks[0] = device // groups * groups + local
    marks[1] = place
    marks[2] = half
    marks[3] = device % groups
    whole = lambda shape: pl.BlockSpec(shape, lambda p, ids: (0,) * len(shape))
    shape = pltpu.HBM((groups, 3 * token_count, subs * block), BF16)
    spec = pl.BlockSpec((None, 3 * token_count, subs * block), lambda p, ids: (p, 0, 0))
    return pl.pallas_call(
        functools.partial(chooser_kernel, dims),
        out_shape=(jax.ShapeDtypeStruct(gates.shape, F32),) + (shape,) * CHUNKS,
        grid_spec=pltpu.PrefetchScalarGridSpec(
            num_scalar_prefetch=1,
            grid=(groups,),
            in_specs=[whole(routes.shape), whole(gates.shape), whole(marks.shape)],
            out_specs=(whole(gates.shape),) + (spec,) * CHUNKS,
        ),
        compiler_params=params(),
        cost_estimate=cost(0, 2 * CHUNKS * groups * 3 * token_count * subs * block, "choosers"),
        name="choosers",
    )(ids, routes, gates, jnp.asarray(marks))


def gather_kernel(ids, chooser, returned, total):
    total[...] = dot(chooser[...], returned[...], 1, 0)


def gather_rows(ids, chooser, returned):
    groups, picks, rows = chooser.shape
    width = returned.shape[1]
    return pl.pallas_call(
        gather_kernel,
        out_shape=jax.ShapeDtypeStruct((groups, picks, width), F32),
        grid_spec=pltpu.PrefetchScalarGridSpec(
            num_scalar_prefetch=1,
            grid=(groups,),
            in_specs=[
                pl.BlockSpec((None, picks, rows), lambda p, ids: (p, 0, 0)),
                pl.BlockSpec(returned.shape, lambda p, ids: (0, 0)),
            ],
            out_specs=pl.BlockSpec((None, picks, width), lambda p, ids: (p, 0, 0)),
        ),
        compiler_params=params(),
        cost_estimate=cost(groups * picks * rows * width, 4 * groups * picks * width, "gather_rows"),
        name="gather_rows",
    )(ids, chooser, returned)


def combine_kernel(ids, gates, cotangent, chooser, returned, earlier, combined, gate_grad, *direct):
    token_count = gates.shape[0]
    p = pl.program_id(0)
    total = dot(chooser[...], returned[...], 1, 0) + earlier[...]
    picked = [total[k * token_count : (k + 1) * token_count] for k in range(3)]
    layer_out = (gates[:, 0:1] * picked[0] + gates[:, 1:2] * picked[1]).astype(BF16)
    input_grad = picked[2].astype(BF16)
    combined[0] = layer_out
    combined[1] = input_grad
    if direct:
        direct[0][...] = layer_out
        direct[1][...] = input_grad
    grads = cotangent[...].astype(F32)
    lane = iota((token_count, 128), 1)
    term = jnp.where(lane == 0, jnp.sum(grads * picked[0], axis=1, keepdims=True), 0.0)
    term += jnp.where(lane == 1, jnp.sum(grads * picked[1], axis=1, keepdims=True), 0.0)

    @pl.when(p == 0)
    def _():
        gate_grad[...] = term

    @pl.when(p > 0)
    def _():
        gate_grad[...] += term


def combine(dims, width, ids, gates, cotangent, chooser, returned, earlier):
    subs, groups, per_chunk, cap, block = dims
    token_count = gates.shape[0]
    cotangent, cotangent_spec = cotangent
    whole = lambda shape: pl.BlockSpec(shape, lambda p, ids: (0,) * len(shape))
    by_holder = lambda shape: pl.BlockSpec((None,) + shape[1:], lambda p, ids: (p, 0, 0))
    final = jax.ShapeDtypeStruct((token_count, 2 * groups * width), BF16)
    direct = 2 if width % 128 == 0 else 0
    return pl.pallas_call(
        combine_kernel,
        out_shape=(
            jax.ShapeDtypeStruct((2, groups, token_count, width), BF16),
            jax.ShapeDtypeStruct((token_count, 128), F32),
        )
        + (final,) * direct,
        grid_spec=pltpu.PrefetchScalarGridSpec(
            num_scalar_prefetch=1,
            grid=(groups,),
            in_specs=[
                whole(gates.shape),
                cotangent_spec,
                by_holder(chooser.shape),
                whole(returned.shape),
                by_holder(earlier.shape),
            ],
            out_specs=(
                pl.BlockSpec((2, None, token_count, width), lambda p, ids: (0, p, 0, 0)),
                whole((token_count, 128)),
            )
            + (pl.BlockSpec((token_count, width), lambda p, ids: (0, 2 * p + ids[0])),) * direct,
        ),
        compiler_params=params(),
        cost_estimate=cost(
            groups * 3 * token_count * subs * block * width,
            2 * subs * block * (width + 3 * groups * token_count),
        ),
        name="combine",
    )(ids, gates, cotangent, chooser, returned, earlier)


def merge_kernel(ids, other, started_out, started_grad, layer_out, input_grad):
    layer_out[...] = other[0]
    input_grad[...] = other[1]


def merge(ids, own, other, direct):
    _, groups, token_count, width = own.shape
    model_width = 2 * groups * width
    if not direct:
        q = lax.axis_index("dp")
        pair = jnp.stack([jnp.where(q == 0, own, other), jnp.where(q == 0, other, own)], axis=2)
        pair = pair.transpose(0, 3, 1, 2, 4).reshape(2, token_count, model_width)
        return pair[0], pair[1]
    in_spec = pl.BlockSpec((2, None, token_count, width), lambda p, ids: (0, p, 0, 0))
    out_spec = pl.BlockSpec((token_count, width), lambda p, ids: (0, 2 * p + 1 - ids[0]))
    shape = jax.ShapeDtypeStruct((token_count, model_width), BF16)
    return pl.pallas_call(
        merge_kernel,
        out_shape=(shape, shape),
        grid_spec=pltpu.PrefetchScalarGridSpec(
            num_scalar_prefetch=1,
            grid=(groups,),
            in_specs=[in_spec] + [pl.BlockSpec(memory_space=pl.ANY)] * 2,
            out_specs=(out_spec, out_spec),
        ),
        input_output_aliases={2: 0, 3: 1},
        compiler_params=params(),
        cost_estimate=cost(0, 8 * token_count * model_width),
        name="merge",
    )(ids, other, *direct)


def pick_acts(chunks, ids, acts, held, arrival):
    per_chunk = acts[0].shape[0]
    local = ids[1] % per_chunk
    for c in range(chunks):

        @pl.when(ids[1] // per_chunk == c)
        def _(c=c):
            pltpu.make_async_copy(acts[c].at[local], held, arrival).start()

    return pltpu.make_async_copy(acts[0].at[local], held, arrival)


def weight_grad_block(features, acts, grads):
    units = acts.shape[1] // 3
    both = dot(features[0], acts[:, : 2 * units], 0, 0).astype(BF16)
    grads[0] = both[:, :units]
    grads[1] = both[:, units:]
    grads[2] = dot(features[1], acts[:, 2 * units :], 0, 0).astype(BF16)


def near_kernel(ids, *refs):
    acts, features = refs[:CHUNKS], refs[CHUNKS : 2 * CHUNKS]
    grads, held, rows, arrivals = refs[2 * CHUNKS :]
    per_chunk = acts[0].shape[0]
    local = ids[1] % per_chunk
    side = pl.program_id(0)
    load = lambda c, s: pltpu.make_async_copy(
        features[c].at[local, s], rows.at[s], arrivals.at[1 + s]
    )

    @pl.when(side == 0)
    def _():
        ready = pick_acts(CHUNKS, ids, acts, held, arrivals.at[0])
        for c in range(CHUNKS):

            @pl.when(ids[1] // per_chunk == c)
            def _(c=c):
                load(c, 0).start()
                load(c, 1).start()

        ready.wait()
        load(0, 0).wait()
        weight_grad_block(rows.at[0], held, grads)

    @pl.when(side == 1)
    def _():
        load(0, 1).wait()
        weight_grad_block(rows.at[1], held, grads)


def near_weight_grads(ids, acts, features):
    rows, triple = acts[0].shape[1:]
    per_chunk = acts[0].shape[0]
    groups = per_chunk * CHUNKS
    width = features[0].shape[4]
    units = triple // 3
    return pl.pallas_call(
        near_kernel,
        out_shape=jax.ShapeDtypeStruct((3, 2 * groups * width, units), BF16),
        grid_spec=pltpu.PrefetchScalarGridSpec(
            num_scalar_prefetch=1,
            grid=(2,),
            in_specs=[pl.BlockSpec(memory_space=pl.ANY)] * (2 * CHUNKS),
            out_specs=pl.BlockSpec(
                (3, width, units),
                lambda s, ids: (0, 2 * ids[1] + jnp.where(s == 0, ids[0], 1 - ids[0]), 0),
            ),
            scratch_shapes=[
                pltpu.VMEM((rows, triple), BF16),
                pltpu.VMEM((2, 2, rows, width), BF16),
                pltpu.SemaphoreType.DMA((3,)),
            ],
        ),
        compiler_params=params(),
        cost_estimate=cost(6 * rows * width * units, 12 * width * units + 8 * rows * width, "near_weight_grads"),
        name="near_weight_grads",
    )(ids, *acts, *features)


def far_kernel(count, ids, *refs):
    acts, features = refs[:CHUNKS], refs[CHUNKS : CHUNKS + count]
    grads, held, arrival = refs[-3:]
    step = pl.program_id(0)

    @pl.when(step == 0)
    def _():
        pick_acts(CHUNKS, ids, acts, held, arrival).wait()

    for index in range(count):

        @pl.when(step == index)
        def _(index=index):
            weight_grad_block(features[index], held, grads)


def far_weight_grads(ids, acts, far, grads):
    rows, triple = acts[0].shape[1:]
    units = triple // 3
    operands = [value for pair in far for value in pair]
    count = len(operands)
    width = operands[0].shape[2]

    def target(s, ids):
        holder = ids[1] ^ (1 + s // 2)
        return 0, 2 * holder + jnp.where(s % 2 == 0, ids[0], 1 - ids[0]), 0

    return pl.pallas_call(
        functools.partial(far_kernel, count),
        out_shape=jax.ShapeDtypeStruct(grads.shape, BF16),
        grid_spec=pltpu.PrefetchScalarGridSpec(
            num_scalar_prefetch=1,
            grid=(count,),
            in_specs=[pl.BlockSpec(memory_space=pl.ANY)] * CHUNKS
            + [pl.BlockSpec((2, rows, width), lambda s, ids: (0, 0, 0))] * count
            + [pl.BlockSpec(memory_space=pl.ANY)],
            out_specs=pl.BlockSpec((3, width, units), target),
            scratch_shapes=[pltpu.VMEM((rows, triple), BF16), pltpu.SemaphoreType.DMA],
        ),
        input_output_aliases={1 + CHUNKS + count: 0},
        compiler_params=params(),
        cost_estimate=cost(
            3 * rows * count * width * units, 6 * count * width * units + 4 * count * rows * width
        ),
        name="far_weight_grads",
    )(ids, *acts, *operands, grads)


def choose(values, index):
    result = values[0]
    for i in range(1, len(values)):
        result = jnp.where(index == i, values[i], result)
    return result


def together(*values):
    return lax.optimization_barrier(values)


def swap_cores(value):
    return lax.ppermute(value, "dp", [(0, 1), (1, 0)])


def swap_holders(value, mask):
    size = lax.axis_size("expert")
    return lax.ppermute(value, "expert", [(source, source ^ mask) for source in range(size)])


def shards(tokens, cotangent, routes, gate_values, weights):
    groups, depth = weights.shape[:2]
    token_count, top_count = routes.shape
    subs = lax.axis_size("expert")
    cap = 5 * token_count * top_count // (4 * subs)
    per_chunk = groups // CHUNKS
    block = 2 * per_chunk * cap
    width = depth // 2
    dims = (subs, groups, per_chunk, cap, block)
    core = lax.axis_index("dp")
    holder = lax.axis_index("expert") % groups
    ids = jnp.stack([core, holder]).astype(jnp.int32)
    weights = weights[:, :, :, 0, :].transpose(0, 2, 1, 3)
    own_tokens = quarter(tokens, groups, width)
    own_cotangent = quarter(cotangent, groups, width)

    aligned = width % 128 == 0
    whole_or_own = (tokens, cotangent) if aligned else (own_tokens[0], own_cotangent[0])

    def exchange(rows):
        blocks = rows.reshape(subs, block, width)
        moved = lax.all_to_all(blocks, "expert", split_axis=0, concat_axis=0, tiled=True)
        return moved.reshape(subs * block, width)

    sent = dispatch(dims, 0, width, routes.T, gate_values.T, *whole_or_own)
    sent, tokens, cotangent = together(sent, tokens, cotangent)
    arrived = [exchange(sent)]

    def columns(mask):
        first = (2 * (holder ^ mask) + core) * width
        parts = [
            lax.dynamic_slice_in_dim(value, first, width, 1) for value in (tokens, cotangent)
        ]
        return jnp.stack(parts)

    info = jnp.concatenate([routes.T.astype(F32), gate_values.T], axis=0)
    infos = [info] + [swap_holders(info, mask) for mask in range(1, groups)]
    parts = [columns(0)] + [swap_holders(columns(mask), mask) for mask in range(1, groups)]
    gates, *choosers = return_choosers(dims, ids, routes, gate_values)
    peers = [list(range(p, subs, groups)) for p in range(groups)]
    for c in range(1, CHUNKS):
        sent = group_dispatch(dims, c, infos, parts)
        sent, gates, *choosers = together(sent, gates, *choosers)
        moved = lax.all_to_all(
            sent.reshape(subs // groups, groups * block, width),
            "expert",
            split_axis=0,
            concat_axis=0,
            tiled=True,
            axis_index_groups=peers,
        )
        arrived.append(moved.reshape(subs * block, width))
    features, acts, mine, theirs, returned = [], [], [], [], []
    for c in range(CHUNKS):
        others = [swap_cores(part) for part in jnp.split(arrived[c], 2)]
        rows, partial = partial_products(dims, c, ids, arrived[c], others, weights)
        features.append(rows)
        if c + 1 < CHUNKS:
            arrived[c + 1], _ = together(arrived[c + 1], partial)
        mask = 1
        while mask < groups // 2:
            partial = (partial.astype(F32) + swap_holders(partial, mask).astype(F32)).astype(BF16)
            mask *= 2
        mine.append(partial)
        theirs.append(swap_holders(partial, mask))
    by_sub = [features[s // per_chunk][s % per_chunk, 0] for s in range(groups)]
    leaving = [choose(by_sub, holder ^ mask) for mask in range(1, groups)]
    theirs[0], _, *leaving = together(theirs[0], mine[-1], *leaving)
    for c in range(CHUNKS):
        active, *parts = output_products(dims, c, ids, mine[c], theirs[c], weights)
        acts.append(active)
        parts[2:] = [swap_cores(part) for part in parts[2:]]
        packed = pack(dims, c, parts)
        if c + 1 < CHUNKS:
            theirs[c + 1], _ = together(theirs[c + 1], packed)
        if c > 0:
            weight_grad = near_weight_grads(ids, acts, features)
            packed, returned[c - 1], weight_grad = together(packed, returned[c - 1], weight_grad)
        returned.append(exchange(packed))
    theirs[-1], *leaving = together(theirs[-1], *leaving)
    earlier = gather_rows(ids, choosers[0], returned[0])
    for c in range(1, CHUNKS - 1):
        earlier = earlier + gather_rows(ids, choosers[c], returned[c])
    far = []
    for mask in range(1, groups):
        near = swap_holders(leaving[mask - 1], mask)
        near, weight_grad, earlier = together(near, weight_grad, earlier)
        far.append((near, swap_cores(near)))
    weight_grad = far_weight_grads(ids, acts, far, weight_grad)
    returned[-1], earlier, weight_grad = together(returned[-1], earlier, weight_grad)
    combined, gate_part, *direct = combine(
        dims, width, ids, gates, own_cotangent, choosers[-1], returned[-1], earlier
    )
    layer_out, input_grad = merge(ids, combined, swap_cores(combined), direct)
    gate_grad = (gate_part + swap_cores(gate_part))[:, :top_count]
    weight_grad = weight_grad.transpose(1, 0, 2).reshape(1, groups * depth, 3, 1, -1)
    return layer_out, input_grad, gate_grad, weight_grad


def solution(mesh):
    in_specs = (
        P("expert", None),
        P("expert", None),
        P("expert", None),
        P("expert", None),
        P(None, "expert", None, "dp", None),
    )
    out_specs = (
        P("expert", None),
        P("expert", None),
        P("expert", None),
        P("expert", None, None, "dp", None),
    )
    return jax.shard_map(shards, mesh=mesh, in_specs=in_specs, out_specs=out_specs, check_vma=False)
```

```python
import functools

import jax
import jax.numpy as jnp
import numpy as np
from jax import lax
from jax.experimental import pallas as pl
from jax.experimental.pallas import tpu as pltpu
from jax.sharding import PartitionSpec as P

F32 = jnp.float32
BF16 = jnp.bfloat16
CHUNKS = 2
MIB = 1024 * 1024
BIG = 44


def dot(left, right, left_dim, right_dim):
    return lax.dot_general(
        left, right, (((left_dim,), (right_dim,)), ((), ())), preferred_element_type=F32
    )


def params(mib=24):
    return pltpu.CompilerParams(vmem_limit_bytes=mib * MIB)


WEIGHTS = {"output_0": 30, "output_1": 30, "far_weight_grads": 4}


def cost(macs, moved, name=""):
    weight = WEIGHTS.get(name, 0.01)
    return pl.CostEstimate(
        flops=int(2 * weight * macs), bytes_accessed=int(weight * moved), transcendentals=0
    )


def iota(shape, dim):
    return lax.broadcasted_iota(jnp.int32, shape, dim)


def split_index(index, size):
    whole = jnp.floor((index.astype(F32) + 0.5) * (1.0 / size)).astype(jnp.int32)
    return whole, index - whole * size


def mark_picks(dims, chunk, routes, gates, picks, scales):
    subs, groups, per_chunk, cap, block = dims
    token_count = routes.shape[1]
    route = [routes[k : k + 1, :] for k in range(2)]
    gate = [gates[k : k + 1, :] for k in range(2)]
    sub = iota((subs, token_count), 0)
    hits = [(route[k] == sub).astype(F32) for k in range(2)]
    earlier = (iota((token_count,) * 2, 0) < iota((token_count,) * 2, 1)).astype(BF16)
    before = dot((hits[0] + hits[1]).astype(BF16), earlier, 1, 0)
    slot = [jnp.sum(hits[k] * before, axis=0, keepdims=True) for k in range(2)]
    slot[1] = slot[1] + (route[0] == route[1]).astype(F32)
    row = iota((block, token_count), 0)
    row = jnp.where(row >= block // 2, row - block // 2, row)
    local = jnp.zeros_like(row)
    for i in range(1, per_chunk):
        local = local + (row >= i * cap).astype(jnp.int32)
    place = (row - local * cap).astype(F32)
    for e in range(subs // groups):
        wanted = local + (e * groups + chunk * per_chunk)
        match = [(route[k] == wanted) & (slot[k] == place) for k in range(2)]
        scale = jnp.where(match[0], gate[0], 0.0) + jnp.where(match[1], gate[1], 0.0)
        scales[e * block : (e + 1) * block, :] = jnp.broadcast_to(
            jnp.sum(scale, axis=1, keepdims=True), scale.shape
        )
        picks[e * block : (e + 1) * block, :] = (
            match[0].astype(F32) + match[1].astype(F32)
        ).astype(BF16)


def place_rows(block, picks, scales, tokens, cotangent, store):
    rows = picks[...]
    chosen = dot(rows, tokens, 1, 0)
    graded = dot(rows, cotangent, 1, 0) * scales[:, :1]
    for e in range(rows.shape[0] // block):
        part = slice(e * block, (e + 1) * block)
        first = iota((block, 1), 0) < block // 2
        store(e, jnp.where(first, chosen[part], graded[part]).astype(BF16))


def dispatch_kernel(dims, chunk, aligned, routes, gates, tokens, cotangent, sent, *scratch):
    subs, groups, per_chunk, cap, block = dims
    picks, scales, columns, arrivals = scratch
    token_count = routes.shape[1]
    width = sent.shape[3]
    loads = []
    for p in range(groups):
        for i, source in enumerate((tokens, cotangent)):
            if aligned:
                first = pl.multiple_of((2 * p + lax.axis_index("dp")) * width, 128)
                source = source.at[:, pl.ds(first, width)]
            else:
                source = source.at[p]
            loads.append(pltpu.make_async_copy(source, columns.at[p, i], arrivals.at[p, i]))
            loads[-1].start()
    mark_picks(dims, chunk, routes[...], gates[...], picks, scales)
    for p in range(groups):
        loads[2 * p].wait()
        loads[2 * p + 1].wait()

        def store(e, value, p=p):
            sent[e, p] = value

        place_rows(block, picks, scales, columns[p, 0], columns[p, 1], store)


def group_kernel(dims, chunk, *refs):
    groups, block = dims[1], dims[4]
    infos, columns = refs[:groups], refs[groups : 2 * groups]
    sent, picks, scales = refs[2 * groups :]
    holder = lax.axis_index("expert") % groups
    for mask in range(groups):
        info = infos[mask][...]
        mark_picks(dims, chunk, info[:2].astype(jnp.int32), info[2:], picks, scales)

        def store(e, value, mask=mask):
            sent[e, holder ^ mask] = value

        place_rows(block, picks, scales, columns[mask][0], columns[mask][1], store)


def group_dispatch(dims, chunk, infos, columns):
    subs, groups, per_chunk, cap, block = dims
    experts = subs // groups
    token_count, width = columns[0].shape[1:]
    vmem = pl.BlockSpec(memory_space=pltpu.VMEM)
    return pl.pallas_call(
        functools.partial(group_kernel, dims, chunk),
        out_shape=jax.ShapeDtypeStruct((experts, groups, block, width), BF16),
        in_specs=[vmem] * (2 * groups),
        out_specs=vmem,
        scratch_shapes=[
            pltpu.VMEM((experts * block, token_count), BF16),
            pltpu.VMEM((experts * block, token_count), F32),
        ],
        compiler_params=params(60),
        cost_estimate=cost(
            2 * experts * block * token_count * width * groups,
            2 * (2 * token_count + experts * block) * width * groups,
        ),
        name=f"group_dispatch_{chunk}",
    )(*infos, *columns)


def quarter(value, groups, width):
    rows = value.shape[0]
    if width % 128 == 0:
        return value, pl.BlockSpec((rows, width), lambda p, ids: (0, 2 * p + ids[0]))
    own = lax.dynamic_index_in_dim(
        value.reshape(rows, groups, 2, width), lax.axis_index("dp"), 2, keepdims=False
    )
    return own.transpose(1, 0, 2), pl.BlockSpec((None, rows, width), lambda p, ids: (p, 0, 0))


def dispatch(dims, chunk, width, routes, gates, tokens, cotangent):
    subs, groups, per_chunk, cap, block = dims
    experts = subs // groups
    token_count = routes.shape[1]
    vmem = pl.BlockSpec(memory_space=pltpu.VMEM)
    return pl.pallas_call(
        functools.partial(dispatch_kernel, dims, chunk, tokens.ndim == 2),
        out_shape=jax.ShapeDtypeStruct((experts, groups, block, width), BF16),
        in_specs=[vmem, vmem] + [pl.BlockSpec(memory_space=pl.ANY)] * 2,
        out_specs=vmem,
        scratch_shapes=[
            pltpu.VMEM((experts * block, token_count), BF16),
            pltpu.VMEM((experts * block, token_count), F32),
            pltpu.VMEM((groups, 2, token_count, width), BF16),
            pltpu.SemaphoreType.DMA((groups, 2)),
        ],
        compiler_params=params(60),
        cost_estimate=cost(
            2 * experts * block * token_count * width * groups,
            2 * (2 * token_count + experts * block) * width * groups,
        ),
        name=f"dispatch_{chunk}",
    )(routes, gates, tokens, cotangent)


def partial_kernel(dims, chunk, ids, own, other_low, other_high, weights, *rest):
    subs, groups, per_chunk, cap, block = dims
    features, partial, held, arrivals = rest
    q = ids[0]
    width = own.shape[1]
    units = weights.shape[3]
    loads = [
        pltpu.make_async_copy(
            weights.at[pl.ds(chunk * per_chunk, per_chunk), m], held.at[m], arrivals.at[m]
        )
        for m in range(3)
    ]
    for load in loads:
        load.start()
    together_count = gather_group(cap)
    inner = together_count * block
    part = together_count * cap
    kind, place = split_index(iota((inner, 1), 0), part)
    source, place = split_index(place, cap)
    target = source * block + kind * cap + place
    chooser = (iota((inner, inner), 1) == target).astype(F32).astype(BF16)
    sets = subs // together_count
    for side in range(2):
        for g in range(sets):
            if side == 0:
                rows = own[g * inner : (g + 1) * inner, :]
            elif g < sets // 2:
                rows = other_low[g * inner : (g + 1) * inner, :]
            else:
                rows = other_high[(g - sets // 2) * inner : (g + 1 - sets // 2) * inner, :]
            sorted_rows = dot(chooser, rows, 1, 0).astype(BF16)
            for half in range(2):
                for i in range(per_chunk):
                    start = (half * per_chunk + i) * part
                    features[i, side, half, g * part : (g + 1) * part, :] = sorted_rows[
                        start : start + part
                    ]
    for m in range(3):
        loads[m].wait()
        half = 1 if m == 2 else 0
        for i in range(per_chunk):
            total = None
            for side in range(2):
                first = q * width if side == 0 else (1 - q) * width
                block_rows = held[m, i, pl.ds(pl.multiple_of(first, 64), width), :]
                term = dot(features[i, side, half], block_rows, 1, 0)
                total = term if total is None else total + term
            partial[i, :, m * units : (m + 1) * units] = total.astype(BF16)


def gather_group(cap):
    count = 1
    while count * cap % 16:
        count *= 2
    return count


def partial_products(dims, chunk, ids, own, others, weights):
    subs, groups, per_chunk, cap, block = dims
    rows = subs * cap
    width = own.shape[1]
    depth, units = weights.shape[2:]
    whole = lambda shape: pl.BlockSpec(shape, lambda s, ids: (0,) * len(shape))
    in_specs = [whole(own.shape)] + [whole(o.shape) for o in others]
    in_specs.append(pl.BlockSpec(memory_space=pltpu.HBM))
    operands = [ids, own, *others, weights]
    return pl.pallas_call(
        functools.partial(partial_kernel, dims, chunk),
        out_shape=(
            pltpu.HBM((per_chunk, 2, 2, rows, width), BF16),
            jax.ShapeDtypeStruct((per_chunk, rows, 3 * units), BF16),
        ),
        grid_spec=pltpu.PrefetchScalarGridSpec(
            num_scalar_prefetch=1,
            grid=(1,),
            in_specs=in_specs,
            out_specs=(
                whole((per_chunk, 2, 2, rows, width)),
                whole((per_chunk, rows, 3 * units)),
            ),
            scratch_shapes=[
                pltpu.VMEM((3, per_chunk, depth, units), BF16),
                pltpu.SemaphoreType.DMA((3,)),
            ],
        ),
        compiler_params=params(BIG),
        cost_estimate=cost(
            per_chunk * rows * (3 * depth * units + 4 * subs * block * width),
            2 * per_chunk * (3 * depth * units + 8 * rows * width + 3 * rows * units),
            f"partial_{chunk}",
        ),
        name=f"partial_{chunk}",
    )(*operands)


def output_kernel(dims, chunk, ids, mine, theirs, weights, *rest):
    per_chunk = dims[2]
    acts, own_out, own_grad, other_out, other_grad, held, arrivals = rest
    units = weights.shape[3]
    width = own_out.shape[2]
    q = ids[0]
    loads = [
        pltpu.make_async_copy(
            weights.at[
                pl.ds(chunk * per_chunk, per_chunk),
                :,
                pl.ds(pl.multiple_of((1 - q if side == 0 else q) * width, 64), width),
            ],
            held.at[side],
            arrivals.at[side],
        )
        for side in range(2)
    ]
    for load in loads:
        load.start()
    for i in range(per_chunk):
        total = lambda m: mine[i, :, m * units : (m + 1) * units].astype(F32) + theirs[
            i, :, m * units : (m + 1) * units
        ].astype(F32)
        gate, up, grad = total(0), total(1), total(2)
        sigmoid = jax.nn.sigmoid(gate)
        active = gate * sigmoid
        acts[i, :, :units] = (grad * up * sigmoid * (1.0 + gate * (1.0 - sigmoid))).astype(BF16)
        acts[i, :, units : 2 * units] = (grad * active).astype(BF16)
        acts[i, :, 2 * units :] = (active * up).astype(BF16)
    for side, target in enumerate(((other_out, other_grad), (own_out, own_grad))):
        loads[side].wait()
        for i in range(per_chunk):
            hidden = acts[i, :, 2 * units :]
            target[0][i] = dot(hidden, held[side, i, 2], 1, 1).astype(BF16)
            target[1][i] = (
                dot(acts[i, :, :units], held[side, i, 0], 1, 1)
                + dot(acts[i, :, units : 2 * units], held[side, i, 1], 1, 1)
            ).astype(BF16)


def output_products(dims, chunk, ids, mine, theirs, weights):
    subs, groups, per_chunk, cap, block = dims
    rows = subs * cap
    depth, units = weights.shape[2:]
    width = depth // 2
    whole = lambda shape: pl.BlockSpec(shape, lambda s, ids: (0,) * len(shape))
    in_specs = [whole(mine.shape), whole(theirs.shape), pl.BlockSpec(memory_space=pltpu.HBM)]
    operands = [ids, mine, theirs, weights]
    out = jax.ShapeDtypeStruct((per_chunk, rows, width), BF16)
    return pl.pallas_call(
        functools.partial(output_kernel, dims, chunk),
        out_shape=(pltpu.HBM((per_chunk, rows, 3 * units), BF16),) + (out,) * 4,
        grid_spec=pltpu.PrefetchScalarGridSpec(
            num_scalar_prefetch=1,
            grid=(1,),
            in_specs=in_specs,
            out_specs=(
                whole((per_chunk, rows, 3 * units)),
            )
            + (whole(out.shape),) * 4,
            scratch_shapes=[
                pltpu.VMEM((2, per_chunk, 3, width, units), BF16),
                pltpu.SemaphoreType.DMA((2,)),
            ],
        ),
        compiler_params=params(BIG),
        cost_estimate=cost(
            per_chunk * rows * 3 * depth * units,
            2 * per_chunk * (3 * depth * units + 2 * rows * depth + 9 * rows * units),
            f"output_{chunk}",
        ),
        name=f"output_{chunk}",
    )(*operands)


def pack_kernel(dims, own_out, own_grad, other_out, other_grad, packed):
    subs, groups, per_chunk, cap, block = dims
    count = gather_group(cap)
    inner, part = count * block, count * cap
    source, place = split_index(iota((inner, 1), 0), block)
    kind, place = split_index(place, cap)
    target = kind * part + source * cap + place
    chooser = (iota((inner, inner), 1) == target).astype(F32).astype(BF16)
    for g in range(subs // count):
        rows = slice(g * part, (g + 1) * part)
        summed = [
            (own[i, rows].astype(F32) + other[i, rows].astype(F32)).astype(BF16)
            for own, other in ((own_out, other_out), (own_grad, other_grad))
            for i in range(per_chunk)
        ]
        packed[g * inner : (g + 1) * inner, :] = dot(
            chooser, jnp.concatenate(summed, axis=0), 1, 0
        ).astype(BF16)


def pack(dims, chunk, parts):
    subs, groups, per_chunk, cap, block = dims
    rows = subs * cap
    width = parts[0].shape[2]
    columns = 256 if width % 256 == 0 else width
    spec = pl.BlockSpec((per_chunk, rows, columns), lambda c: (0, 0, c))
    return pl.pallas_call(
        functools.partial(pack_kernel, dims),
        out_shape=pltpu.HBM((subs * block, width), BF16),
        grid=(width // columns,),
        in_specs=[spec] * 4,
        out_specs=pl.BlockSpec((subs * block, columns), lambda c: (0, c)),
        compiler_params=params(),
        cost_estimate=cost(
            subs * block * 2 * per_chunk * rows * width, 6 * subs * block * width, f"pack_{chunk}"
        ),
        name=f"pack_{chunk}",
    )(*parts)


def chooser_kernel(dims, ids, routes, gates, marks, gates_out, *choosers):
    subs, groups, per_chunk, cap, block = dims
    token_count = routes.shape[0]
    p = pl.program_id(0)
    gates_out[...] = gates[...]
    route = [routes[:, k : k + 1] for k in range(2)]
    sub = iota((token_count, subs), 1)
    hits = [(route[k] == sub).astype(F32) for k in range(2)]
    earlier = (iota((token_count,) * 2, 1) < iota((token_count,) * 2, 0)).astype(BF16)
    before = dot(earlier, (hits[0] + hits[1]).astype(BF16), 1, 0)
    slot = [jnp.sum(hits[k] * before, axis=1, keepdims=True) for k in range(2)]
    slot[1] = slot[1] + (route[0] == route[1]).astype(F32)
    slot = [value.astype(jnp.int32) for value in slot]
    for chunk in range(CHUNKS):
        wanted = marks[0:1, :] + chunk * per_chunk
        place, half, holder = marks[1:2, :], marks[2:3, :], marks[3:4, :]
        match = [
            ((route[k] == wanted) & (slot[k] == place) & (holder == p)).astype(F32)
            for k in range(2)
        ]
        first = (half == 0).astype(F32)
        second = (half == 1).astype(F32)
        choosers[chunk][0:token_count, :] = (match[0] * first).astype(BF16)
        choosers[chunk][token_count : 2 * token_count, :] = (match[1] * first).astype(BF16)
        choosers[chunk][2 * token_count :, :] = ((match[0] + match[1]) * second).astype(BF16)


def return_choosers(dims, ids, routes, gates):
    subs, groups, per_chunk, cap, block = dims
    token_count = routes.shape[0]
    row = np.arange(subs * block)
    device, inner = row // block, row % block
    half, inner = inner // (per_chunk * cap), inner % (per_chunk * cap)
    local, place = inner // cap, inner % cap
    marks = np.zeros((8, subs * block), np.int32)
    marks[0] = device // groups * groups + local
    marks[1] = place
    marks[2] = half
    marks[3] = device % groups
    whole = lambda shape: pl.BlockSpec(shape, lambda p, ids: (0,) * len(shape))
    shape = pltpu.HBM((groups, 3 * token_count, subs * block), BF16)
    spec = pl.BlockSpec((None, 3 * token_count, subs * block), lambda p, ids: (p, 0, 0))
    return pl.pallas_call(
        functools.partial(chooser_kernel, dims),
        out_shape=(jax.ShapeDtypeStruct(gates.shape, F32),) + (shape,) * CHUNKS,
        grid_spec=pltpu.PrefetchScalarGridSpec(
            num_scalar_prefetch=1,
            grid=(groups,),
            in_specs=[whole(routes.shape), whole(gates.shape), whole(marks.shape)],
            out_specs=(whole(gates.shape),) + (spec,) * CHUNKS,
        ),
        compiler_params=params(),
        cost_estimate=cost(0, 2 * CHUNKS * groups * 3 * token_count * subs * block, "choosers"),
        name="choosers",
    )(ids, routes, gates, jnp.asarray(marks))


def gather_kernel(ids, chooser, returned, total):
    total[...] = dot(chooser[...], returned[...], 1, 0)


def gather_rows(ids, chooser, returned):
    groups, picks, rows = chooser.shape
    width = returned.shape[1]
    return pl.pallas_call(
        gather_kernel,
        out_shape=jax.ShapeDtypeStruct((groups, picks, width), F32),
        grid_spec=pltpu.PrefetchScalarGridSpec(
            num_scalar_prefetch=1,
            grid=(groups,),
            in_specs=[
                pl.BlockSpec((None, picks, rows), lambda p, ids: (p, 0, 0)),
                pl.BlockSpec(returned.shape, lambda p, ids: (0, 0)),
            ],
            out_specs=pl.BlockSpec((None, picks, width), lambda p, ids: (p, 0, 0)),
        ),
        compiler_params=params(),
        cost_estimate=cost(groups * picks * rows * width, 4 * groups * picks * width, "gather_rows"),
        name="gather_rows",
    )(ids, chooser, returned)


def combine_kernel(ids, gates, cotangent, chooser, returned, earlier, combined, gate_grad, *direct):
    token_count = gates.shape[0]
    p = pl.program_id(0)
    total = dot(chooser[...], returned[...], 1, 0) + earlier[...]
    picked = [total[k * token_count : (k + 1) * token_count] for k in range(3)]
    layer_out = (gates[:, 0:1] * picked[0] + gates[:, 1:2] * picked[1]).astype(BF16)
    input_grad = picked[2].astype(BF16)
    combined[0] = layer_out
    combined[1] = input_grad
    if direct:
        direct[0][...] = layer_out
        direct[1][...] = input_grad
    grads = cotangent[...].astype(F32)
    lane = iota((token_count, 128), 1)
    term = jnp.where(lane == 0, jnp.sum(grads * picked[0], axis=1, keepdims=True), 0.0)
    term += jnp.where(lane == 1, jnp.sum(grads * picked[1], axis=1, keepdims=True), 0.0)

    @pl.when(p == 0)
    def _():
        gate_grad[...] = term

    @pl.when(p > 0)
    def _():
        gate_grad[...] += term


def combine(dims, width, ids, gates, cotangent, chooser, returned, earlier):
    subs, groups, per_chunk, cap, block = dims
    token_count = gates.shape[0]
    cotangent, cotangent_spec = cotangent
    whole = lambda shape: pl.BlockSpec(shape, lambda p, ids: (0,) * len(shape))
    by_holder = lambda shape: pl.BlockSpec((None,) + shape[1:], lambda p, ids: (p, 0, 0))
    final = jax.ShapeDtypeStruct((token_count, 2 * groups * width), BF16)
    direct = 2 if width % 128 == 0 else 0
    return pl.pallas_call(
        combine_kernel,
        out_shape=(
            jax.ShapeDtypeStruct((2, groups, token_count, width), BF16),
            jax.ShapeDtypeStruct((token_count, 128), F32),
        )
        + (final,) * direct,
        grid_spec=pltpu.PrefetchScalarGridSpec(
            num_scalar_prefetch=1,
            grid=(groups,),
            in_specs=[
                whole(gates.shape),
                cotangent_spec,
                by_holder(chooser.shape),
                whole(returned.shape),
                by_holder(earlier.shape),
            ],
            out_specs=(
                pl.BlockSpec((2, None, token_count, width), lambda p, ids: (0, p, 0, 0)),
                whole((token_count, 128)),
            )
            + (pl.BlockSpec((token_count, width), lambda p, ids: (0, 2 * p + ids[0])),) * direct,
        ),
        compiler_params=params(),
        cost_estimate=cost(
            groups * 3 * token_count * subs * block * width,
            2 * subs * block * (width + 3 * groups * token_count),
        ),
        name="combine",
    )(ids, gates, cotangent, chooser, returned, earlier)


def merge_kernel(ids, other, started_out, started_grad, layer_out, input_grad, moved):
    width = other.shape[3]
    copies = []
    for p in range(other.shape[1]):
        columns = pl.ds(pl.multiple_of((2 * p + 1 - ids[0]) * width, 128), width)
        for i, target in enumerate((layer_out, input_grad)):
            copies.append(
                pltpu.make_async_copy(other.at[i, p], target.at[:, columns], moved.at[p, i])
            )
            copies[-1].start()
    for copy in copies:
        copy.wait()


def merge(ids, own, other, direct):
    _, groups, token_count, width = own.shape
    model_width = 2 * groups * width
    if not direct:
        q = lax.axis_index("dp")
        pair = jnp.stack([jnp.where(q == 0, own, other), jnp.where(q == 0, other, own)], axis=2)
        pair = pair.transpose(0, 3, 1, 2, 4).reshape(2, token_count, model_width)
        return pair[0], pair[1]
    shape = jax.ShapeDtypeStruct((token_count, model_width), BF16)
    free = pl.BlockSpec(memory_space=pl.ANY)
    return pl.pallas_call(
        merge_kernel,
        out_shape=(shape, shape),
        grid_spec=pltpu.PrefetchScalarGridSpec(
            num_scalar_prefetch=1,
            grid=(1,),
            in_specs=[free] * 3,
            out_specs=(free, free),
            scratch_shapes=[pltpu.SemaphoreType.DMA((groups, 2))],
        ),
        input_output_aliases={2: 0, 3: 1},
        compiler_params=params(),
        cost_estimate=cost(0, 8 * token_count * model_width),
        name="merge",
    )(ids, other, *direct)


def pick_acts(chunks, ids, acts, held, arrival):
    per_chunk = acts[0].shape[0]
    local = ids[1] % per_chunk
    for c in range(chunks):

        @pl.when(ids[1] // per_chunk == c)
        def _(c=c):
            pltpu.make_async_copy(acts[c].at[local], held, arrival).start()

    return pltpu.make_async_copy(acts[0].at[local], held, arrival)


def weight_grad_block(features, acts, grads):
    units = acts.shape[1] // 3
    both = dot(features[0], acts[:, : 2 * units], 0, 0).astype(BF16)
    grads[0] = both[:, :units]
    grads[1] = both[:, units:]
    grads[2] = dot(features[1], acts[:, 2 * units :], 0, 0).astype(BF16)


def near_kernel(ids, *refs):
    acts, features = refs[:CHUNKS], refs[CHUNKS : 2 * CHUNKS]
    grads, held, rows, arrivals = refs[2 * CHUNKS :]
    per_chunk = acts[0].shape[0]
    local = ids[1] % per_chunk
    side = pl.program_id(0)
    load = lambda c, s: pltpu.make_async_copy(
        features[c].at[local, s], rows.at[s], arrivals.at[1 + s]
    )

    @pl.when(side == 0)
    def _():
        ready = pick_acts(CHUNKS, ids, acts, held, arrivals.at[0])
        for c in range(CHUNKS):

            @pl.when(ids[1] // per_chunk == c)
            def _(c=c):
                load(c, 0).start()
                load(c, 1).start()

        ready.wait()
        load(0, 0).wait()
        weight_grad_block(rows.at[0], held, grads)

    @pl.when(side == 1)
    def _():
        load(0, 1).wait()
        weight_grad_block(rows.at[1], held, grads)


def near_weight_grads(ids, acts, features):
    rows, triple = acts[0].shape[1:]
    per_chunk = acts[0].shape[0]
    groups = per_chunk * CHUNKS
    width = features[0].shape[4]
    units = triple // 3
    return pl.pallas_call(
        near_kernel,
        out_shape=jax.ShapeDtypeStruct((3, 2 * groups * width, units), BF16),
        grid_spec=pltpu.PrefetchScalarGridSpec(
            num_scalar_prefetch=1,
            grid=(2,),
            in_specs=[pl.BlockSpec(memory_space=pl.ANY)] * (2 * CHUNKS),
            out_specs=pl.BlockSpec(
                (3, width, units),
                lambda s, ids: (0, 2 * ids[1] + jnp.where(s == 0, ids[0], 1 - ids[0]), 0),
            ),
            scratch_shapes=[
                pltpu.VMEM((rows, triple), BF16),
                pltpu.VMEM((2, 2, rows, width), BF16),
                pltpu.SemaphoreType.DMA((3,)),
            ],
        ),
        compiler_params=params(),
        cost_estimate=cost(6 * rows * width * units, 12 * width * units + 8 * rows * width, "near_weight_grads"),
        name="near_weight_grads",
    )(ids, *acts, *features)


def far_kernel(count, ids, *refs):
    acts, features = refs[:CHUNKS], refs[CHUNKS : CHUNKS + count]
    grads, held, arrival = refs[-3:]
    step = pl.program_id(0)

    @pl.when(step == 0)
    def _():
        pick_acts(CHUNKS, ids, acts, held, arrival).wait()

    for index in range(count):

        @pl.when(step == index)
        def _(index=index):
            weight_grad_block(features[index], held, grads)


def far_weight_grads(ids, acts, far, grads):
    rows, triple = acts[0].shape[1:]
    units = triple // 3
    operands = [value for pair in far for value in pair]
    count = len(operands)
    width = operands[0].shape[2]

    def target(s, ids):
        holder = ids[1] ^ (1 + s // 2)
        return 0, 2 * holder + jnp.where(s % 2 == 0, ids[0], 1 - ids[0]), 0

    return pl.pallas_call(
        functools.partial(far_kernel, count),
        out_shape=jax.ShapeDtypeStruct(grads.shape, BF16),
        grid_spec=pltpu.PrefetchScalarGridSpec(
            num_scalar_prefetch=1,
            grid=(count,),
            in_specs=[pl.BlockSpec(memory_space=pl.ANY)] * CHUNKS
            + [pl.BlockSpec((2, rows, width), lambda s, ids: (0, 0, 0))] * count
            + [pl.BlockSpec(memory_space=pl.ANY)],
            out_specs=pl.BlockSpec((3, width, units), target),
            scratch_shapes=[pltpu.VMEM((rows, triple), BF16), pltpu.SemaphoreType.DMA],
        ),
        input_output_aliases={1 + CHUNKS + count: 0},
        compiler_params=params(),
        cost_estimate=cost(
            3 * rows * count * width * units, 6 * count * width * units + 4 * count * rows * width,
            "far_weight_grads",
        ),
        name="far_weight_grads",
    )(ids, *acts, *operands, grads)


def choose(values, index):
    result = values[0]
    for i in range(1, len(values)):
        result = jnp.where(index == i, values[i], result)
    return result


def together(*values):
    return lax.optimization_barrier(values)


def swap_cores(value):
    return lax.ppermute(value, "dp", [(0, 1), (1, 0)])


def swap_holders(value, mask):
    size = lax.axis_size("expert")
    return lax.ppermute(value, "expert", [(source, source ^ mask) for source in range(size)])


def shards(tokens, cotangent, routes, gate_values, weights):
    groups, depth = weights.shape[:2]
    token_count, top_count = routes.shape
    subs = lax.axis_size("expert")
    cap = 5 * token_count * top_count // (4 * subs)
    per_chunk = groups // CHUNKS
    block = 2 * per_chunk * cap
    width = depth // 2
    dims = (subs, groups, per_chunk, cap, block)
    core = lax.axis_index("dp")
    holder = lax.axis_index("expert") % groups
    ids = jnp.stack([core, holder]).astype(jnp.int32)
    weights = weights[:, :, :, 0, :].transpose(0, 2, 1, 3)
    own_tokens = quarter(tokens, groups, width)
    own_cotangent = quarter(cotangent, groups, width)

    aligned = width % 128 == 0
    whole_or_own = (tokens, cotangent) if aligned else (own_tokens[0], own_cotangent[0])

    def exchange(rows):
        blocks = rows.reshape(subs, block, width)
        moved = lax.all_to_all(blocks, "expert", split_axis=0, concat_axis=0, tiled=True)
        return moved.reshape(subs * block, width)

    sent = dispatch(dims, 0, width, routes.T, gate_values.T, *whole_or_own)
    sent, tokens, cotangent = together(sent, tokens, cotangent)
    arrived = [exchange(sent)]

    def columns(mask):
        first = (2 * (holder ^ mask) + core) * width
        parts = [
            lax.dynamic_slice_in_dim(value, first, width, 1) for value in (tokens, cotangent)
        ]
        return jnp.stack(parts)

    info = jnp.concatenate([routes.T.astype(F32), gate_values.T], axis=0)
    infos = [info] + [swap_holders(info, mask) for mask in range(1, groups)]
    parts = [columns(0)] + [swap_holders(columns(mask), mask) for mask in range(1, groups)]
    gates, *choosers = return_choosers(dims, ids, routes, gate_values)
    peers = [list(range(p, subs, groups)) for p in range(groups)]
    for c in range(1, CHUNKS):
        sent = group_dispatch(dims, c, infos, parts)
        sent, gates, *choosers = together(sent, gates, *choosers)
        if c == 1:
            arrived[0], _ = together(arrived[0], sent)
        moved = lax.all_to_all(
            sent.reshape(subs // groups, groups * block, width),
            "expert",
            split_axis=0,
            concat_axis=0,
            tiled=True,
            axis_index_groups=peers,
        )
        arrived.append(moved.reshape(subs * block, width))
    features, acts, mine, theirs, returned = [], [], [], [], []
    for c in range(CHUNKS):
        others = [swap_cores(part) for part in jnp.split(arrived[c], 2)]
        rows, partial = partial_products(dims, c, ids, arrived[c], others, weights)
        features.append(rows)
        if c + 1 < CHUNKS:
            arrived[c + 1], _ = together(arrived[c + 1], partial)
        mask = 1
        while mask < groups // 2:
            partial = (partial.astype(F32) + swap_holders(partial, mask).astype(F32)).astype(BF16)
            mask *= 2
        mine.append(partial)
        theirs.append(swap_holders(partial, mask))
    by_sub = [features[s // per_chunk][s % per_chunk, 0] for s in range(groups)]
    leaving = [choose(by_sub, holder ^ mask) for mask in range(1, groups)]
    theirs[0], _, *leaving = together(theirs[0], mine[-1], *leaving)
    for c in range(CHUNKS):
        active, *parts = output_products(dims, c, ids, mine[c], theirs[c], weights)
        acts.append(active)
        parts[2:] = [swap_cores(part) for part in parts[2:]]
        packed = pack(dims, c, parts)
        if c + 1 < CHUNKS:
            theirs[c + 1], _ = together(theirs[c + 1], packed)
        if c > 0:
            packed, returned[c - 1] = together(packed, returned[c - 1])
            weight_grad = near_weight_grads(ids, acts, features)
        returned.append(exchange(packed))
    theirs[-1], *leaving = together(theirs[-1], *leaving)
    earlier = gather_rows(ids, choosers[0], returned[0])
    for c in range(1, CHUNKS - 1):
        earlier = earlier + gather_rows(ids, choosers[c], returned[c])
    far = []
    for mask in range(1, groups):
        near = swap_holders(leaving[mask - 1], mask)
        near, weight_grad, earlier = together(near, weight_grad, earlier)
        far.append((near, swap_cores(near)))
    weight_grad = far_weight_grads(ids, acts, far, weight_grad)
    returned[-1], earlier, weight_grad = together(returned[-1], earlier, weight_grad)
    combined, gate_part, *direct = combine(
        dims, width, ids, gates, own_cotangent, choosers[-1], returned[-1], earlier
    )
    layer_out, input_grad = merge(ids, combined, swap_cores(combined), direct)
    gate_grad = (gate_part + swap_cores(gate_part))[:, :top_count]
    weight_grad = weight_grad.transpose(1, 0, 2).reshape(1, groups * depth, 3, 1, -1)
    return layer_out, input_grad, gate_grad, weight_grad


def solution(mesh):
    in_specs = (
        P("expert", None),
        P("expert", None),
        P("expert", None),
        P("expert", None),
        P(None, "expert", None, "dp", None),
    )
    out_specs = (
        P("expert", None),
        P("expert", None),
        P("expert", None),
        P("expert", None, None, "dp", None),
    )
    return jax.shard_map(shards, mesh=mesh, in_specs=in_specs, out_specs=out_specs, check_vma=False)
```

```python
import functools

import jax
import jax.numpy as jnp
import numpy as np
from jax import lax
from jax.experimental import pallas as pl
from jax.experimental.pallas import tpu as pltpu
from jax.sharding import PartitionSpec as P

F32 = jnp.float32
BF16 = jnp.bfloat16
CHUNKS = 2
MIB = 1024 * 1024
BIG = 44


def dot(left, right, left_dim, right_dim):
    return lax.dot_general(
        left, right, (((left_dim,), (right_dim,)), ((), ())), preferred_element_type=F32
    )


def params(mib=24):
    return pltpu.CompilerParams(vmem_limit_bytes=mib * MIB)


WEIGHTS = {"output_0": 30, "output_1": 30, "far_weight_grads": 4}


def cost(macs, moved, name=""):
    weight = WEIGHTS.get(name, 0.01)
    return pl.CostEstimate(
        flops=int(2 * weight * macs), bytes_accessed=int(weight * moved), transcendentals=0
    )


def iota(shape, dim):
    return lax.broadcasted_iota(jnp.int32, shape, dim)


def split_index(index, size):
    whole = jnp.floor((index.astype(F32) + 0.5) * (1.0 / size)).astype(jnp.int32)
    return whole, index - whole * size


def mark_picks(dims, chunk, routes, gates, picks, scales):
    subs, groups, per_chunk, cap, block = dims
    token_count = routes.shape[1]
    route = [routes[k : k + 1, :] for k in range(2)]
    gate = [gates[k : k + 1, :] for k in range(2)]
    sub = iota((subs, token_count), 0)
    hits = [(route[k] == sub).astype(F32) for k in range(2)]
    earlier = (iota((token_count,) * 2, 0) < iota((token_count,) * 2, 1)).astype(BF16)
    before = dot((hits[0] + hits[1]).astype(BF16), earlier, 1, 0)
    slot = [jnp.sum(hits[k] * before, axis=0, keepdims=True) for k in range(2)]
    slot[1] = slot[1] + (route[0] == route[1]).astype(F32)
    row = iota((block, token_count), 0)
    row = jnp.where(row >= block // 2, row - block // 2, row)
    local = jnp.zeros_like(row)
    for i in range(1, per_chunk):
        local = local + (row >= i * cap).astype(jnp.int32)
    place = (row - local * cap).astype(F32)
    for e in range(subs // groups):
        wanted = local + (e * groups + chunk * per_chunk)
        match = [(route[k] == wanted) & (slot[k] == place) for k in range(2)]
        scale = jnp.where(match[0], gate[0], 0.0) + jnp.where(match[1], gate[1], 0.0)
        scales[e * block : (e + 1) * block, :] = jnp.broadcast_to(
            jnp.sum(scale, axis=1, keepdims=True), scale.shape
        )
        picks[e * block : (e + 1) * block, :] = (
            match[0].astype(F32) + match[1].astype(F32)
        ).astype(BF16)


def place_rows(block, picks, scales, tokens, cotangent, store):
    rows = picks[...]
    chosen = dot(rows, tokens, 1, 0)
    graded = dot(rows, cotangent, 1, 0) * scales[:, :1]
    for e in range(rows.shape[0] // block):
        part = slice(e * block, (e + 1) * block)
        first = iota((block, 1), 0) < block // 2
        store(e, jnp.where(first, chosen[part], graded[part]).astype(BF16))


def dispatch_kernel(dims, chunk, aligned, routes, gates, tokens, cotangent, sent, *scratch):
    subs, groups, per_chunk, cap, block = dims
    picks, scales, columns, arrivals = scratch
    token_count = routes.shape[1]
    width = sent.shape[3]
    loads = []
    for p in range(groups):
        for i, source in enumerate((tokens, cotangent)):
            if aligned:
                first = pl.multiple_of((2 * p + lax.axis_index("dp")) * width, 128)
                source = source.at[:, pl.ds(first, width)]
            else:
                source = source.at[p]
            loads.append(pltpu.make_async_copy(source, columns.at[p, i], arrivals.at[p, i]))
            loads[-1].start()
    mark_picks(dims, chunk, routes[...], gates[...], picks, scales)
    for p in range(groups):
        loads[2 * p].wait()
        loads[2 * p + 1].wait()

        def store(e, value, p=p):
            sent[e, p] = value

        place_rows(block, picks, scales, columns[p, 0], columns[p, 1], store)


def group_kernel(dims, chunk, *refs):
    groups, block = dims[1], dims[4]
    infos, columns = refs[:groups], refs[groups : 2 * groups]
    sent, picks, scales = refs[2 * groups :]
    holder = lax.axis_index("expert") % groups
    for mask in range(groups):
        info = infos[mask][...]
        mark_picks(dims, chunk, info[:2].astype(jnp.int32), info[2:], picks, scales)

        def store(e, value, mask=mask):
            sent[e, holder ^ mask] = value

        place_rows(block, picks, scales, columns[mask][0], columns[mask][1], store)


def group_dispatch(dims, chunk, infos, columns):
    subs, groups, per_chunk, cap, block = dims
    experts = subs // groups
    token_count, width = columns[0].shape[1:]
    vmem = pl.BlockSpec(memory_space=pltpu.VMEM)
    return pl.pallas_call(
        functools.partial(group_kernel, dims, chunk),
        out_shape=jax.ShapeDtypeStruct((experts, groups, block, width), BF16),
        in_specs=[vmem] * (2 * groups),
        out_specs=vmem,
        scratch_shapes=[
            pltpu.VMEM((experts * block, token_count), BF16),
            pltpu.VMEM((experts * block, token_count), F32),
        ],
        compiler_params=params(60),
        cost_estimate=cost(
            2 * experts * block * token_count * width * groups,
            2 * (2 * token_count + experts * block) * width * groups,
        ),
        name=f"group_dispatch_{chunk}",
    )(*infos, *columns)


def quarter(value, groups, width):
    rows = value.shape[0]
    if width % 128 == 0:
        return value, pl.BlockSpec((rows, width), lambda p, ids: (0, 2 * p + ids[0]))
    own = lax.dynamic_index_in_dim(
        value.reshape(rows, groups, 2, width), lax.axis_index("dp"), 2, keepdims=False
    )
    return own.transpose(1, 0, 2), pl.BlockSpec((None, rows, width), lambda p, ids: (p, 0, 0))


def dispatch(dims, chunk, width, routes, gates, tokens, cotangent):
    subs, groups, per_chunk, cap, block = dims
    experts = subs // groups
    token_count = routes.shape[1]
    vmem = pl.BlockSpec(memory_space=pltpu.VMEM)
    return pl.pallas_call(
        functools.partial(dispatch_kernel, dims, chunk, tokens.ndim == 2),
        out_shape=jax.ShapeDtypeStruct((experts, groups, block, width), BF16),
        in_specs=[vmem, vmem] + [pl.BlockSpec(memory_space=pl.ANY)] * 2,
        out_specs=vmem,
        scratch_shapes=[
            pltpu.VMEM((experts * block, token_count), BF16),
            pltpu.VMEM((experts * block, token_count), F32),
            pltpu.VMEM((groups, 2, token_count, width), BF16),
            pltpu.SemaphoreType.DMA((groups, 2)),
        ],
        compiler_params=params(60),
        cost_estimate=cost(
            2 * experts * block * token_count * width * groups,
            2 * (2 * token_count + experts * block) * width * groups,
        ),
        name=f"dispatch_{chunk}",
    )(routes, gates, tokens, cotangent)


def partial_kernel(dims, chunk, pick, ids, own, other_low, other_high, weights, *rest):
    subs, groups, per_chunk, cap, block = dims
    if pick:
        features, partial, leaving, held, arrivals, departure = rest[chunk:]
    else:
        features, partial, held, arrivals = rest
    q = ids[0]
    width = own.shape[1]
    units = weights.shape[3]
    loads = [
        pltpu.make_async_copy(
            weights.at[pl.ds(chunk * per_chunk, per_chunk), m], held.at[m], arrivals.at[m]
        )
        for m in range(3)
    ]
    for load in loads:
        load.start()
    together_count = gather_group(cap)
    inner = together_count * block
    part = together_count * cap
    kind, place = split_index(iota((inner, 1), 0), part)
    source, place = split_index(place, cap)
    target = source * block + kind * cap + place
    chooser = (iota((inner, inner), 1) == target).astype(F32).astype(BF16)
    sets = subs // together_count
    for side in range(2):
        for g in range(sets):
            if side == 0:
                rows = own[g * inner : (g + 1) * inner, :]
            elif g < sets // 2:
                rows = other_low[g * inner : (g + 1) * inner, :]
            else:
                rows = other_high[(g - sets // 2) * inner : (g + 1 - sets // 2) * inner, :]
            sorted_rows = dot(chooser, rows, 1, 0).astype(BF16)
            for half in range(2):
                for i in range(per_chunk):
                    start = (half * per_chunk + i) * part
                    features[i, side, half, g * part : (g + 1) * part, :] = sorted_rows[
                        start : start + part
                    ]
    if pick:

        @pl.when(ids[1] != chunk)
        def _():
            pltpu.make_async_copy(features.at[0, 0], leaving, departure).start()

    for m in range(3):
        loads[m].wait()
        half = 1 if m == 2 else 0
        for i in range(per_chunk):
            total = None
            for side in range(2):
                first = q * width if side == 0 else (1 - q) * width
                block_rows = held[m, i, pl.ds(pl.multiple_of(first, 64), width), :]
                term = dot(features[i, side, half], block_rows, 1, 0)
                total = term if total is None else total + term
            partial[i, :, m * units : (m + 1) * units] = total.astype(BF16)
    if pick:

        @pl.when(ids[1] != chunk)
        def _():
            pltpu.make_async_copy(features.at[0, 0], leaving, departure).wait()


def gather_group(cap):
    count = 1
    while count * cap % 16:
        count *= 2
    return count


def partial_products(dims, chunk, ids, own, others, weights, leaving):
    subs, groups, per_chunk, cap, block = dims
    rows = subs * cap
    width = own.shape[1]
    depth, units = weights.shape[2:]
    whole = lambda shape: pl.BlockSpec(shape, lambda s, ids: (0,) * len(shape))
    in_specs = [whole(own.shape)] + [whole(o.shape) for o in others]
    in_specs.append(pl.BlockSpec(memory_space=pltpu.HBM))
    operands = [ids, own, *others, weights]
    pick = groups == 2
    leaving_shape, leaving_spec, departure, aliases = (), (), [], {}
    if pick:
        leaving_shape = (pltpu.HBM((2, rows, width), BF16),)
        leaving_spec = (pl.BlockSpec(memory_space=pl.ANY),)
        departure = [pltpu.SemaphoreType.DMA]
        if chunk:
            in_specs.append(pl.BlockSpec(memory_space=pl.ANY))
            aliases = {len(operands): 2}
            operands.append(leaving)
    return pl.pallas_call(
        functools.partial(partial_kernel, dims, chunk, pick),
        out_shape=(
            pltpu.HBM((per_chunk, 2, 2, rows, width), BF16),
            jax.ShapeDtypeStruct((per_chunk, rows, 3 * units), BF16),
        )
        + leaving_shape,
        input_output_aliases=aliases,
        grid_spec=pltpu.PrefetchScalarGridSpec(
            num_scalar_prefetch=1,
            grid=(1,),
            in_specs=in_specs,
            out_specs=(
                whole((per_chunk, 2, 2, rows, width)),
                whole((per_chunk, rows, 3 * units)),
            )
            + leaving_spec,
            scratch_shapes=[
                pltpu.VMEM((3, per_chunk, depth, units), BF16),
                pltpu.SemaphoreType.DMA((3,)),
            ]
            + departure,
        ),
        compiler_params=params(BIG),
        cost_estimate=cost(
            per_chunk * rows * (3 * depth * units + 4 * subs * block * width),
            2 * per_chunk * (3 * depth * units + 8 * rows * width + 3 * rows * units),
            f"partial_{chunk}",
        ),
        name=f"partial_{chunk}",
    )(*operands)


def output_kernel(dims, chunk, ids, mine, theirs, weights, *rest):
    per_chunk = dims[2]
    acts, own_out, own_grad, other_out, other_grad, held, arrivals = rest
    units = weights.shape[3]
    width = own_out.shape[2]
    q = ids[0]
    loads = [
        pltpu.make_async_copy(
            weights.at[
                pl.ds(chunk * per_chunk, per_chunk),
                :,
                pl.ds(pl.multiple_of((1 - q if side == 0 else q) * width, 64), width),
            ],
            held.at[side],
            arrivals.at[side],
        )
        for side in range(2)
    ]
    for load in loads:
        load.start()
    for i in range(per_chunk):
        total = lambda m: mine[i, :, m * units : (m + 1) * units].astype(F32) + theirs[
            i, :, m * units : (m + 1) * units
        ].astype(F32)
        gate, up, grad = total(0), total(1), total(2)
        sigmoid = jax.nn.sigmoid(gate)
        active = gate * sigmoid
        acts[i, :, :units] = (grad * up * sigmoid * (1.0 + gate * (1.0 - sigmoid))).astype(BF16)
        acts[i, :, units : 2 * units] = (grad * active).astype(BF16)
        acts[i, :, 2 * units :] = (active * up).astype(BF16)
    for side, target in enumerate(((other_out, other_grad), (own_out, own_grad))):
        loads[side].wait()
        for i in range(per_chunk):
            hidden = acts[i, :, 2 * units :]
            target[0][i] = dot(hidden, held[side, i, 2], 1, 1).astype(BF16)
            target[1][i] = (
                dot(acts[i, :, :units], held[side, i, 0], 1, 1)
                + dot(acts[i, :, units : 2 * units], held[side, i, 1], 1, 1)
            ).astype(BF16)


def output_products(dims, chunk, ids, mine, theirs, weights):
    subs, groups, per_chunk, cap, block = dims
    rows = subs * cap
    depth, units = weights.shape[2:]
    width = depth // 2
    whole = lambda shape: pl.BlockSpec(shape, lambda s, ids: (0,) * len(shape))
    in_specs = [whole(mine.shape), whole(theirs.shape), pl.BlockSpec(memory_space=pltpu.HBM)]
    operands = [ids, mine, theirs, weights]
    out = jax.ShapeDtypeStruct((per_chunk, rows, width), BF16)
    return pl.pallas_call(
        functools.partial(output_kernel, dims, chunk),
        out_shape=(pltpu.HBM((per_chunk, rows, 3 * units), BF16),) + (out,) * 4,
        grid_spec=pltpu.PrefetchScalarGridSpec(
            num_scalar_prefetch=1,
            grid=(1,),
            in_specs=in_specs,
            out_specs=(
                whole((per_chunk, rows, 3 * units)),
            )
            + (whole(out.shape),) * 4,
            scratch_shapes=[
                pltpu.VMEM((2, per_chunk, 3, width, units), BF16),
                pltpu.SemaphoreType.DMA((2,)),
            ],
        ),
        compiler_params=params(BIG),
        cost_estimate=cost(
            per_chunk * rows * 3 * depth * units,
            2 * per_chunk * (3 * depth * units + 2 * rows * depth + 9 * rows * units),
            f"output_{chunk}",
        ),
        name=f"output_{chunk}",
    )(*operands)


def pack_kernel(dims, own_out, own_grad, other_out, other_grad, packed):
    subs, groups, per_chunk, cap, block = dims
    count = gather_group(cap)
    inner, part = count * block, count * cap
    source, place = split_index(iota((inner, 1), 0), block)
    kind, place = split_index(place, cap)
    target = kind * part + source * cap + place
    chooser = (iota((inner, inner), 1) == target).astype(F32).astype(BF16)
    for g in range(subs // count):
        rows = slice(g * part, (g + 1) * part)
        summed = [
            (own[i, rows].astype(F32) + other[i, rows].astype(F32)).astype(BF16)
            for own, other in ((own_out, other_out), (own_grad, other_grad))
            for i in range(per_chunk)
        ]
        packed[g * inner : (g + 1) * inner, :] = dot(
            chooser, jnp.concatenate(summed, axis=0), 1, 0
        ).astype(BF16)


def pack(dims, chunk, parts):
    subs, groups, per_chunk, cap, block = dims
    rows = subs * cap
    width = parts[0].shape[2]
    columns = 256 if width % 256 == 0 else width
    spec = pl.BlockSpec((per_chunk, rows, columns), lambda c: (0, 0, c))
    return pl.pallas_call(
        functools.partial(pack_kernel, dims),
        out_shape=pltpu.HBM((subs * block, width), BF16),
        grid=(width // columns,),
        in_specs=[spec] * 4,
        out_specs=pl.BlockSpec((subs * block, columns), lambda c: (0, c)),
        compiler_params=params(),
        cost_estimate=cost(
            subs * block * 2 * per_chunk * rows * width, 6 * subs * block * width, f"pack_{chunk}"
        ),
        name=f"pack_{chunk}",
    )(*parts)


def chooser_kernel(dims, ids, routes, gates, marks, gates_out, *choosers):
    subs, groups, per_chunk, cap, block = dims
    token_count = routes.shape[0]
    p = pl.program_id(0)
    gates_out[...] = gates[...]
    route = [routes[:, k : k + 1] for k in range(2)]
    sub = iota((token_count, subs), 1)
    hits = [(route[k] == sub).astype(F32) for k in range(2)]
    earlier = (iota((token_count,) * 2, 1) < iota((token_count,) * 2, 0)).astype(BF16)
    before = dot(earlier, (hits[0] + hits[1]).astype(BF16), 1, 0)
    slot = [jnp.sum(hits[k] * before, axis=1, keepdims=True) for k in range(2)]
    slot[1] = slot[1] + (route[0] == route[1]).astype(F32)
    slot = [value.astype(jnp.int32) for value in slot]
    for chunk in range(CHUNKS):
        wanted = marks[0:1, :] + chunk * per_chunk
        place, half, holder = marks[1:2, :], marks[2:3, :], marks[3:4, :]
        match = [
            ((route[k] == wanted) & (slot[k] == place) & (holder == p)).astype(F32)
            for k in range(2)
        ]
        first = (half == 0).astype(F32)
        second = (half == 1).astype(F32)
        choosers[chunk][0:token_count, :] = (match[0] * first).astype(BF16)
        choosers[chunk][token_count : 2 * token_count, :] = (match[1] * first).astype(BF16)
        choosers[chunk][2 * token_count :, :] = ((match[0] + match[1]) * second).astype(BF16)


def return_choosers(dims, ids, routes, gates):
    subs, groups, per_chunk, cap, block = dims
    token_count = routes.shape[0]
    row = np.arange(subs * block)
    device, inner = row // block, row % block
    half, inner = inner // (per_chunk * cap), inner % (per_chunk * cap)
    local, place = inner // cap, inner % cap
    marks = np.zeros((8, subs * block), np.int32)
    marks[0] = device // groups * groups + local
    marks[1] = place
    marks[2] = half
    marks[3] = device % groups
    whole = lambda shape: pl.BlockSpec(shape, lambda p, ids: (0,) * len(shape))
    shape = pltpu.HBM((groups, 3 * token_count, subs * block), BF16)
    spec = pl.BlockSpec((None, 3 * token_count, subs * block), lambda p, ids: (p, 0, 0))
    return pl.pallas_call(
        functools.partial(chooser_kernel, dims),
        out_shape=(jax.ShapeDtypeStruct(gates.shape, F32),) + (shape,) * CHUNKS,
        grid_spec=pltpu.PrefetchScalarGridSpec(
            num_scalar_prefetch=1,
            grid=(groups,),
            in_specs=[whole(routes.shape), whole(gates.shape), whole(marks.shape)],
            out_specs=(whole(gates.shape),) + (spec,) * CHUNKS,
        ),
        compiler_params=params(),
        cost_estimate=cost(0, 2 * CHUNKS * groups * 3 * token_count * subs * block, "choosers"),
        name="choosers",
    )(ids, routes, gates, jnp.asarray(marks))


def gather_kernel(ids, chooser, returned, total):
    total[...] = dot(chooser[...], returned[...], 1, 0)


def gather_rows(ids, chooser, returned):
    groups, picks, rows = chooser.shape
    width = returned.shape[1]
    return pl.pallas_call(
        gather_kernel,
        out_shape=jax.ShapeDtypeStruct((groups, picks, width), F32),
        grid_spec=pltpu.PrefetchScalarGridSpec(
            num_scalar_prefetch=1,
            grid=(groups,),
            in_specs=[
                pl.BlockSpec((None, picks, rows), lambda p, ids: (p, 0, 0)),
                pl.BlockSpec(returned.shape, lambda p, ids: (0, 0)),
            ],
            out_specs=pl.BlockSpec((None, picks, width), lambda p, ids: (p, 0, 0)),
        ),
        compiler_params=params(),
        cost_estimate=cost(groups * picks * rows * width, 4 * groups * picks * width, "gather_rows"),
        name="gather_rows",
    )(ids, chooser, returned)


def combine_kernel(ids, gates, cotangent, chooser, returned, earlier, combined, gate_grad, *direct):
    token_count = gates.shape[0]
    p = pl.program_id(0)
    total = dot(chooser[...], returned[...], 1, 0) + earlier[...]
    picked = [total[k * token_count : (k + 1) * token_count] for k in range(3)]
    layer_out = (gates[:, 0:1] * picked[0] + gates[:, 1:2] * picked[1]).astype(BF16)
    input_grad = picked[2].astype(BF16)
    combined[0] = layer_out
    combined[1] = input_grad
    if direct:
        direct[0][...] = layer_out
        direct[1][...] = input_grad
    grads = cotangent[...].astype(F32)
    lane = iota((token_count, 128), 1)
    term = jnp.where(lane == 0, jnp.sum(grads * picked[0], axis=1, keepdims=True), 0.0)
    term += jnp.where(lane == 1, jnp.sum(grads * picked[1], axis=1, keepdims=True), 0.0)

    @pl.when(p == 0)
    def _():
        gate_grad[...] = term

    @pl.when(p > 0)
    def _():
        gate_grad[...] += term


def combine(dims, width, ids, gates, cotangent, chooser, returned, earlier):
    subs, groups, per_chunk, cap, block = dims
    token_count = gates.shape[0]
    cotangent, cotangent_spec = cotangent
    whole = lambda shape: pl.BlockSpec(shape, lambda p, ids: (0,) * len(shape))
    by_holder = lambda shape: pl.BlockSpec((None,) + shape[1:], lambda p, ids: (p, 0, 0))
    final = jax.ShapeDtypeStruct((token_count, 2 * groups * width), BF16)
    direct = 2 if width % 128 == 0 else 0
    return pl.pallas_call(
        combine_kernel,
        out_shape=(
            jax.ShapeDtypeStruct((2, groups, token_count, width), BF16),
            jax.ShapeDtypeStruct((token_count, 128), F32),
        )
        + (final,) * direct,
        grid_spec=pltpu.PrefetchScalarGridSpec(
            num_scalar_prefetch=1,
            grid=(groups,),
            in_specs=[
                whole(gates.shape),
                cotangent_spec,
                by_holder(chooser.shape),
                whole(returned.shape),
                by_holder(earlier.shape),
            ],
            out_specs=(
                pl.BlockSpec((2, None, token_count, width), lambda p, ids: (0, p, 0, 0)),
                whole((token_count, 128)),
            )
            + (pl.BlockSpec((token_count, width), lambda p, ids: (0, 2 * p + ids[0])),) * direct,
        ),
        compiler_params=params(),
        cost_estimate=cost(
            groups * 3 * token_count * subs * block * width,
            2 * subs * block * (width + 3 * groups * token_count),
        ),
        name="combine",
    )(ids, gates, cotangent, chooser, returned, earlier)


def merge_kernel(ids, other, started_out, started_grad, layer_out, input_grad, moved):
    width = other.shape[3]
    copies = []
    for p in range(other.shape[1]):
        columns = pl.ds(pl.multiple_of((2 * p + 1 - ids[0]) * width, 128), width)
        for i, target in enumerate((layer_out, input_grad)):
            copies.append(
                pltpu.make_async_copy(other.at[i, p], target.at[:, columns], moved.at[p, i])
            )
            copies[-1].start()
    for copy in copies:
        copy.wait()


def merge(ids, own, other, direct):
    _, groups, token_count, width = own.shape
    model_width = 2 * groups * width
    if not direct:
        q = lax.axis_index("dp")
        pair = jnp.stack([jnp.where(q == 0, own, other), jnp.where(q == 0, other, own)], axis=2)
        pair = pair.transpose(0, 3, 1, 2, 4).reshape(2, token_count, model_width)
        return pair[0], pair[1]
    shape = jax.ShapeDtypeStruct((token_count, model_width), BF16)
    free = pl.BlockSpec(memory_space=pl.ANY)
    return pl.pallas_call(
        merge_kernel,
        out_shape=(shape, shape),
        grid_spec=pltpu.PrefetchScalarGridSpec(
            num_scalar_prefetch=1,
            grid=(1,),
            in_specs=[free] * 3,
            out_specs=(free, free),
            scratch_shapes=[pltpu.SemaphoreType.DMA((groups, 2))],
        ),
        input_output_aliases={2: 0, 3: 1},
        compiler_params=params(),
        cost_estimate=cost(0, 8 * token_count * model_width),
        name="merge",
    )(ids, other, *direct)


def pick_acts(chunks, ids, acts, held, arrival):
    per_chunk = acts[0].shape[0]
    local = ids[1] % per_chunk
    for c in range(chunks):

        @pl.when(ids[1] // per_chunk == c)
        def _(c=c):
            pltpu.make_async_copy(acts[c].at[local], held, arrival).start()

    return pltpu.make_async_copy(acts[0].at[local], held, arrival)


def weight_grad_block(features, acts, grads):
    units = acts.shape[1] // 3
    both = dot(features[0], acts[:, : 2 * units], 0, 0).astype(BF16)
    grads[0] = both[:, :units]
    grads[1] = both[:, units:]
    grads[2] = dot(features[1], acts[:, 2 * units :], 0, 0).astype(BF16)


def near_kernel(ids, *refs):
    acts, features = refs[:CHUNKS], refs[CHUNKS : 2 * CHUNKS]
    grads, held, rows, arrivals = refs[2 * CHUNKS :]
    per_chunk = acts[0].shape[0]
    local = ids[1] % per_chunk
    side = pl.program_id(0)
    load = lambda c, s: pltpu.make_async_copy(
        features[c].at[local, s], rows.at[s], arrivals.at[1 + s]
    )

    @pl.when(side == 0)
    def _():
        ready = pick_acts(CHUNKS, ids, acts, held, arrivals.at[0])
        for c in range(CHUNKS):

            @pl.when(ids[1] // per_chunk == c)
            def _(c=c):
                load(c, 0).start()
                load(c, 1).start()

        ready.wait()
        load(0, 0).wait()
        weight_grad_block(rows.at[0], held, grads)

    @pl.when(side == 1)
    def _():
        load(0, 1).wait()
        weight_grad_block(rows.at[1], held, grads)


def near_weight_grads(ids, acts, features):
    rows, triple = acts[0].shape[1:]
    per_chunk = acts[0].shape[0]
    groups = per_chunk * CHUNKS
    width = features[0].shape[4]
    units = triple // 3
    return pl.pallas_call(
        near_kernel,
        out_shape=jax.ShapeDtypeStruct((3, 2 * groups * width, units), BF16),
        grid_spec=pltpu.PrefetchScalarGridSpec(
            num_scalar_prefetch=1,
            grid=(2,),
            in_specs=[pl.BlockSpec(memory_space=pl.ANY)] * (2 * CHUNKS),
            out_specs=pl.BlockSpec(
                (3, width, units),
                lambda s, ids: (0, 2 * ids[1] + jnp.where(s == 0, ids[0], 1 - ids[0]), 0),
            ),
            scratch_shapes=[
                pltpu.VMEM((rows, triple), BF16),
                pltpu.VMEM((2, 2, rows, width), BF16),
                pltpu.SemaphoreType.DMA((3,)),
            ],
        ),
        compiler_params=params(),
        cost_estimate=cost(6 * rows * width * units, 12 * width * units + 8 * rows * width, "near_weight_grads"),
        name="near_weight_grads",
    )(ids, *acts, *features)


def far_kernel(count, ids, *refs):
    acts, features = refs[:CHUNKS], refs[CHUNKS : CHUNKS + count]
    grads, held, arrival = refs[-3:]
    step = pl.program_id(0)

    @pl.when(step == 0)
    def _():
        pick_acts(CHUNKS, ids, acts, held, arrival).wait()

    for index in range(count):

        @pl.when(step == index)
        def _(index=index):
            weight_grad_block(features[index], held, grads)


def far_weight_grads(ids, acts, far, grads):
    rows, triple = acts[0].shape[1:]
    units = triple // 3
    operands = [value for pair in far for value in pair]
    count = len(operands)
    width = operands[0].shape[2]

    def target(s, ids):
        holder = ids[1] ^ (1 + s // 2)
        return 0, 2 * holder + jnp.where(s % 2 == 0, ids[0], 1 - ids[0]), 0

    return pl.pallas_call(
        functools.partial(far_kernel, count),
        out_shape=jax.ShapeDtypeStruct(grads.shape, BF16),
        grid_spec=pltpu.PrefetchScalarGridSpec(
            num_scalar_prefetch=1,
            grid=(count,),
            in_specs=[pl.BlockSpec(memory_space=pl.ANY)] * CHUNKS
            + [pl.BlockSpec((2, rows, width), lambda s, ids: (0, 0, 0))] * count
            + [pl.BlockSpec(memory_space=pl.ANY)],
            out_specs=pl.BlockSpec((3, width, units), target),
            scratch_shapes=[pltpu.VMEM((rows, triple), BF16), pltpu.SemaphoreType.DMA],
        ),
        input_output_aliases={1 + CHUNKS + count: 0},
        compiler_params=params(),
        cost_estimate=cost(
            3 * rows * count * width * units, 6 * count * width * units + 4 * count * rows * width,
            "far_weight_grads",
        ),
        name="far_weight_grads",
    )(ids, *acts, *operands, grads)


def choose(values, index):
    result = values[0]
    for i in range(1, len(values)):
        result = jnp.where(index == i, values[i], result)
    return result


def together(*values):
    return lax.optimization_barrier(values)


def swap_cores(value):
    return lax.ppermute(value, "dp", [(0, 1), (1, 0)])


def swap_holders(value, mask):
    size = lax.axis_size("expert")
    return lax.ppermute(value, "expert", [(source, source ^ mask) for source in range(size)])


def shards(tokens, cotangent, routes, gate_values, weights):
    groups, depth = weights.shape[:2]
    token_count, top_count = routes.shape
    subs = lax.axis_size("expert")
    cap = 5 * token_count * top_count // (4 * subs)
    per_chunk = groups // CHUNKS
    block = 2 * per_chunk * cap
    width = depth // 2
    dims = (subs, groups, per_chunk, cap, block)
    core = lax.axis_index("dp")
    holder = lax.axis_index("expert") % groups
    ids = jnp.stack([core, holder]).astype(jnp.int32)
    weights = weights[:, :, :, 0, :].transpose(0, 2, 1, 3)
    own_tokens = quarter(tokens, groups, width)
    own_cotangent = quarter(cotangent, groups, width)

    aligned = width % 128 == 0
    whole_or_own = (tokens, cotangent) if aligned else (own_tokens[0], own_cotangent[0])

    def exchange(rows):
        blocks = rows.reshape(subs, block, width)
        moved = lax.all_to_all(blocks, "expert", split_axis=0, concat_axis=0, tiled=True)
        return moved.reshape(subs * block, width)

    sent = dispatch(dims, 0, width, routes.T, gate_values.T, *whole_or_own)
    sent, tokens, cotangent = together(sent, tokens, cotangent)
    arrived = [exchange(sent)]

    def columns(mask):
        first = (2 * (holder ^ mask) + core) * width
        parts = [
            lax.dynamic_slice_in_dim(value, first, width, 1) for value in (tokens, cotangent)
        ]
        return jnp.stack(parts)

    info = jnp.concatenate([routes.T.astype(F32), gate_values.T], axis=0)
    infos = [info] + [swap_holders(info, mask) for mask in range(1, groups)]
    parts = [columns(0)] + [swap_holders(columns(mask), mask) for mask in range(1, groups)]
    gates, *choosers = return_choosers(dims, ids, routes, gate_values)
    peers = [list(range(p, subs, groups)) for p in range(groups)]
    for c in range(1, CHUNKS):
        sent = group_dispatch(dims, c, infos, parts)
        sent, gates, *choosers = together(sent, gates, *choosers)
        if c == 1:
            arrived[0], _ = together(arrived[0], sent)
        moved = lax.all_to_all(
            sent.reshape(subs // groups, groups * block, width),
            "expert",
            split_axis=0,
            concat_axis=0,
            tiled=True,
            axis_index_groups=peers,
        )
        arrived.append(moved.reshape(subs * block, width))
    features, acts, mine, theirs, returned, leaving = [], [], [], [], [], []
    for c in range(CHUNKS):
        others = [swap_cores(part) for part in jnp.split(arrived[c], 2)]
        rows, partial, *leaving = partial_products(
            dims, c, ids, arrived[c], others, weights, leaving[0] if leaving else None
        )
        features.append(rows)
        if c + 1 < CHUNKS:
            arrived[c + 1], _ = together(arrived[c + 1], partial)
        mask = 1
        while mask < groups // 2:
            partial = (partial.astype(F32) + swap_holders(partial, mask).astype(F32)).astype(BF16)
            mask *= 2
        mine.append(partial)
        theirs.append(swap_holders(partial, mask))
    if not leaving:
        by_sub = [features[s // per_chunk][s % per_chunk, 0] for s in range(groups)]
        leaving = [choose(by_sub, holder ^ mask) for mask in range(1, groups)]
    theirs[0], _, *leaving = together(theirs[0], mine[-1], *leaving)
    for c in range(CHUNKS):
        active, *parts = output_products(dims, c, ids, mine[c], theirs[c], weights)
        acts.append(active)
        parts[2:] = [swap_cores(part) for part in parts[2:]]
        packed = pack(dims, c, parts)
        if c + 1 < CHUNKS:
            theirs[c + 1], _ = together(theirs[c + 1], packed)
        if c > 0:
            packed, returned[c - 1] = together(packed, returned[c - 1])
            weight_grad = near_weight_grads(ids, acts, features)
        returned.append(exchange(packed))
    theirs[-1], *leaving = together(theirs[-1], *leaving)
    earlier = gather_rows(ids, choosers[0], returned[0])
    for c in range(1, CHUNKS - 1):
        earlier = earlier + gather_rows(ids, choosers[c], returned[c])
    far = []
    for mask in range(1, groups):
        near = swap_holders(leaving[mask - 1], mask)
        near, weight_grad, earlier = together(near, weight_grad, earlier)
        far.append((near, swap_cores(near)))
    weight_grad = far_weight_grads(ids, acts, far, weight_grad)
    returned[-1], earlier, weight_grad = together(returned[-1], earlier, weight_grad)
    combined, gate_part, *direct = combine(
        dims, width, ids, gates, own_cotangent, choosers[-1], returned[-1], earlier
    )
    layer_out, input_grad = merge(ids, combined, swap_cores(combined), direct)
    gate_grad = (gate_part + swap_cores(gate_part))[:, :top_count]
    weight_grad = weight_grad.transpose(1, 0, 2).reshape(1, groups * depth, 3, 1, -1)
    return layer_out, input_grad, gate_grad, weight_grad


def solution(mesh):
    in_specs = (
        P("expert", None),
        P("expert", None),
        P("expert", None),
        P("expert", None),
        P(None, "expert", None, "dp", None),
    )
    out_specs = (
        P("expert", None),
        P("expert", None),
        P("expert", None),
        P("expert", None, None, "dp", None),
    )
    return jax.shard_map(shards, mesh=mesh, in_specs=in_specs, out_specs=out_specs, check_vma=False)
```

```python
import functools

import jax
import jax.numpy as jnp
import numpy as np
from jax import lax
from jax.experimental import pallas as pl
from jax.experimental.pallas import tpu as pltpu
from jax.sharding import PartitionSpec as P

F32 = jnp.float32
BF16 = jnp.bfloat16
CHUNKS = 2
MIB = 1024 * 1024
BIG = 44


def dot(left, right, left_dim, right_dim):
    return lax.dot_general(
        left, right, (((left_dim,), (right_dim,)), ((), ())), preferred_element_type=F32
    )


def params(mib=24):
    return pltpu.CompilerParams(vmem_limit_bytes=mib * MIB)


WEIGHTS = {"output_0": 30, "output_1": 30, "far_weight_grads": 4}


def cost(macs, moved, name=""):
    weight = WEIGHTS.get(name, 0.01)
    return pl.CostEstimate(
        flops=int(2 * weight * macs), bytes_accessed=int(weight * moved), transcendentals=0
    )


def iota(shape, dim):
    return lax.broadcasted_iota(jnp.int32, shape, dim)


def split_index(index, size):
    whole = jnp.floor((index.astype(F32) + 0.5) * (1.0 / size)).astype(jnp.int32)
    return whole, index - whole * size


def mark_picks(dims, chunk, routes, gates, picks, scales):
    subs, groups, per_chunk, cap, block = dims
    token_count = routes.shape[1]
    route = [routes[k : k + 1, :] for k in range(2)]
    gate = [gates[k : k + 1, :] for k in range(2)]
    sub = iota((subs, token_count), 0)
    hits = [(route[k] == sub).astype(F32) for k in range(2)]
    earlier = (iota((token_count,) * 2, 0) < iota((token_count,) * 2, 1)).astype(BF16)
    before = dot((hits[0] + hits[1]).astype(BF16), earlier, 1, 0)
    slot = [jnp.sum(hits[k] * before, axis=0, keepdims=True) for k in range(2)]
    slot[1] = slot[1] + (route[0] == route[1]).astype(F32)
    row = iota((block, token_count), 0)
    row = jnp.where(row >= block // 2, row - block // 2, row)
    local = jnp.zeros_like(row)
    for i in range(1, per_chunk):
        local = local + (row >= i * cap).astype(jnp.int32)
    place = (row - local * cap).astype(F32)
    for e in range(subs // groups):
        wanted = local + (e * groups + chunk * per_chunk)
        match = [(route[k] == wanted) & (slot[k] == place) for k in range(2)]
        scale = jnp.where(match[0], gate[0], 0.0) + jnp.where(match[1], gate[1], 0.0)
        scales[e * block : (e + 1) * block, :] = jnp.broadcast_to(
            jnp.sum(scale, axis=1, keepdims=True), scale.shape
        )
        picks[e * block : (e + 1) * block, :] = (
            match[0].astype(F32) + match[1].astype(F32)
        ).astype(BF16)


def place_rows(block, picks, scales, tokens, cotangent, store):
    rows = picks[...]
    chosen = dot(rows, tokens, 1, 0)
    graded = dot(rows, cotangent, 1, 0) * scales[:, :1]
    for e in range(rows.shape[0] // block):
        part = slice(e * block, (e + 1) * block)
        first = iota((block, 1), 0) < block // 2
        store(e, jnp.where(first, chosen[part], graded[part]).astype(BF16))


def dispatch_kernel(dims, chunk, aligned, routes, gates, tokens, cotangent, sent, *scratch):
    subs, groups, per_chunk, cap, block = dims
    picks, scales, columns, arrivals = scratch
    token_count = routes.shape[1]
    width = sent.shape[3]
    loads = []
    for p in range(groups):
        for i, source in enumerate((tokens, cotangent)):
            if aligned:
                first = pl.multiple_of((2 * p + lax.axis_index("dp")) * width, 128)
                source = source.at[:, pl.ds(first, width)]
            else:
                source = source.at[p]
            loads.append(pltpu.make_async_copy(source, columns.at[p, i], arrivals.at[p, i]))
            loads[-1].start()
    mark_picks(dims, chunk, routes[...], gates[...], picks, scales)
    for p in range(groups):
        loads[2 * p].wait()
        loads[2 * p + 1].wait()

        def store(e, value, p=p):
            sent[e, p] = value

        place_rows(block, picks, scales, columns[p, 0], columns[p, 1], store)


def group_kernel(dims, chunk, *refs):
    groups, block = dims[1], dims[4]
    infos, columns = refs[:groups], refs[groups : 2 * groups]
    sent, picks, scales = refs[2 * groups :]
    holder = lax.axis_index("expert") % groups
    for mask in range(groups):
        info = infos[mask][...]
        mark_picks(dims, chunk, info[:2].astype(jnp.int32), info[2:], picks, scales)

        def store(e, value, mask=mask):
            sent[e, holder ^ mask] = value

        place_rows(block, picks, scales, columns[mask][0], columns[mask][1], store)


def group_dispatch(dims, chunk, infos, columns):
    subs, groups, per_chunk, cap, block = dims
    experts = subs // groups
    token_count, width = columns[0].shape[1:]
    vmem = pl.BlockSpec(memory_space=pltpu.VMEM)
    return pl.pallas_call(
        functools.partial(group_kernel, dims, chunk),
        out_shape=jax.ShapeDtypeStruct((experts, groups, block, width), BF16),
        in_specs=[vmem] * (2 * groups),
        out_specs=vmem,
        scratch_shapes=[
            pltpu.VMEM((experts * block, token_count), BF16),
            pltpu.VMEM((experts * block, token_count), F32),
        ],
        compiler_params=params(60),
        cost_estimate=cost(
            2 * experts * block * token_count * width * groups,
            2 * (2 * token_count + experts * block) * width * groups,
        ),
        name=f"group_dispatch_{chunk}",
    )(*infos, *columns)


def quarter(value, groups, width):
    rows = value.shape[0]
    if width % 128 == 0:
        return value, pl.BlockSpec((rows, width), lambda p, ids: (0, 2 * p + ids[0]))
    own = lax.dynamic_index_in_dim(
        value.reshape(rows, groups, 2, width), lax.axis_index("dp"), 2, keepdims=False
    )
    return own.transpose(1, 0, 2), pl.BlockSpec((None, rows, width), lambda p, ids: (p, 0, 0))


def dispatch(dims, chunk, width, routes, gates, tokens, cotangent):
    subs, groups, per_chunk, cap, block = dims
    experts = subs // groups
    token_count = routes.shape[1]
    vmem = pl.BlockSpec(memory_space=pltpu.VMEM)
    return pl.pallas_call(
        functools.partial(dispatch_kernel, dims, chunk, tokens.ndim == 2),
        out_shape=jax.ShapeDtypeStruct((experts, groups, block, width), BF16),
        in_specs=[vmem, vmem] + [pl.BlockSpec(memory_space=pl.ANY)] * 2,
        out_specs=vmem,
        scratch_shapes=[
            pltpu.VMEM((experts * block, token_count), BF16),
            pltpu.VMEM((experts * block, token_count), F32),
            pltpu.VMEM((groups, 2, token_count, width), BF16),
            pltpu.SemaphoreType.DMA((groups, 2)),
        ],
        compiler_params=params(60),
        cost_estimate=cost(
            2 * experts * block * token_count * width * groups,
            2 * (2 * token_count + experts * block) * width * groups,
        ),
        name=f"dispatch_{chunk}",
    )(routes, gates, tokens, cotangent)


def partial_kernel(dims, chunk, pick, ids, own, other_low, other_high, weights, *rest):
    subs, groups, per_chunk, cap, block = dims
    if pick:
        features, partial, leaving, held, arrivals, departure = rest[chunk:]
    else:
        features, partial, held, arrivals = rest
    q = ids[0]
    width = own.shape[1]
    units = weights.shape[3]
    loads = [
        pltpu.make_async_copy(
            weights.at[pl.ds(chunk * per_chunk, per_chunk), m], held.at[m], arrivals.at[m]
        )
        for m in range(3)
    ]
    for load in loads:
        load.start()
    together_count = gather_group(cap)
    inner = together_count * block
    part = together_count * cap
    kind, place = split_index(iota((inner, 1), 0), part)
    source, place = split_index(place, cap)
    target = source * block + kind * cap + place
    chooser = (iota((inner, inner), 1) == target).astype(F32).astype(BF16)
    sets = subs // together_count
    for side in range(2):
        for g in range(sets):
            if side == 0:
                rows = own[g * inner : (g + 1) * inner, :]
            elif g < sets // 2:
                rows = other_low[g * inner : (g + 1) * inner, :]
            else:
                rows = other_high[(g - sets // 2) * inner : (g + 1 - sets // 2) * inner, :]
            sorted_rows = dot(chooser, rows, 1, 0).astype(BF16)
            for half in range(2):
                for i in range(per_chunk):
                    start = (half * per_chunk + i) * part
                    features[i, side, half, g * part : (g + 1) * part, :] = sorted_rows[
                        start : start + part
                    ]
    if pick:

        @pl.when(ids[1] != chunk)
        def _():
            pltpu.make_async_copy(features.at[0, 0], leaving, departure).start()

    for m in range(3):
        loads[m].wait()
        half = 1 if m == 2 else 0
        for i in range(per_chunk):
            total = None
            for side in range(2):
                first = q * width if side == 0 else (1 - q) * width
                block_rows = held[m, i, pl.ds(pl.multiple_of(first, 64), width), :]
                term = dot(features[i, side, half], block_rows, 1, 0)
                total = term if total is None else total + term
            partial[i, :, m * units : (m + 1) * units] = total.astype(BF16)
    if pick:

        @pl.when(ids[1] != chunk)
        def _():
            pltpu.make_async_copy(features.at[0, 0], leaving, departure).wait()


def gather_group(cap):
    count = 1
    while count * cap % 16:
        count *= 2
    return count


def partial_products(dims, chunk, ids, own, others, weights, leaving):
    subs, groups, per_chunk, cap, block = dims
    rows = subs * cap
    width = own.shape[1]
    depth, units = weights.shape[2:]
    whole = lambda shape: pl.BlockSpec(shape, lambda s, ids: (0,) * len(shape))
    in_specs = [whole(own.shape)] + [whole(o.shape) for o in others]
    in_specs.append(pl.BlockSpec(memory_space=pltpu.HBM))
    operands = [ids, own, *others, weights]
    pick = groups == 2
    leaving_shape, leaving_spec, departure, aliases = (), (), [], {}
    if pick:
        leaving_shape = (pltpu.HBM((2, rows, width), BF16),)
        leaving_spec = (pl.BlockSpec(memory_space=pl.ANY),)
        departure = [pltpu.SemaphoreType.DMA]
        if chunk:
            in_specs.append(pl.BlockSpec(memory_space=pl.ANY))
            aliases = {len(operands): 2}
            operands.append(leaving)
    return pl.pallas_call(
        functools.partial(partial_kernel, dims, chunk, pick),
        out_shape=(
            pltpu.HBM((per_chunk, 2, 2, rows, width), BF16),
            jax.ShapeDtypeStruct((per_chunk, rows, 3 * units), BF16),
        )
        + leaving_shape,
        input_output_aliases=aliases,
        grid_spec=pltpu.PrefetchScalarGridSpec(
            num_scalar_prefetch=1,
            grid=(1,),
            in_specs=in_specs,
            out_specs=(
                whole((per_chunk, 2, 2, rows, width)),
                whole((per_chunk, rows, 3 * units)),
            )
            + leaving_spec,
            scratch_shapes=[
                pltpu.VMEM((3, per_chunk, depth, units), BF16),
                pltpu.SemaphoreType.DMA((3,)),
            ]
            + departure,
        ),
        compiler_params=params(BIG),
        cost_estimate=cost(
            per_chunk * rows * (3 * depth * units + 4 * subs * block * width),
            2 * per_chunk * (3 * depth * units + 8 * rows * width + 3 * rows * units),
            f"partial_{chunk}",
        ),
        name=f"partial_{chunk}",
    )(*operands)


def output_kernel(dims, chunk, ids, mine, theirs, weights, *rest):
    per_chunk = dims[2]
    acts, own_out, own_grad, other_out, other_grad, held, arrivals = rest
    units = weights.shape[3]
    width = own_out.shape[2]
    q = ids[0]
    loads = [
        pltpu.make_async_copy(
            weights.at[
                pl.ds(chunk * per_chunk, per_chunk),
                :,
                pl.ds(pl.multiple_of((1 - q if side == 0 else q) * width, 64), width),
            ],
            held.at[side],
            arrivals.at[side],
        )
        for side in range(2)
    ]
    for load in loads:
        load.start()
    for i in range(per_chunk):
        total = lambda m: mine[i, :, m * units : (m + 1) * units].astype(F32) + theirs[
            i, :, m * units : (m + 1) * units
        ].astype(F32)
        gate, up, grad = total(0), total(1), total(2)
        sigmoid = jax.nn.sigmoid(gate)
        active = gate * sigmoid
        acts[i, :, :units] = (grad * up * sigmoid * (1.0 + gate * (1.0 - sigmoid))).astype(BF16)
        acts[i, :, units : 2 * units] = (grad * active).astype(BF16)
        acts[i, :, 2 * units :] = (active * up).astype(BF16)
    for side, target in enumerate(((other_out, other_grad), (own_out, own_grad))):
        loads[side].wait()
        for i in range(per_chunk):
            hidden = acts[i, :, 2 * units :]
            target[0][i] = dot(hidden, held[side, i, 2], 1, 1).astype(BF16)
            target[1][i] = (
                dot(acts[i, :, :units], held[side, i, 0], 1, 1)
                + dot(acts[i, :, units : 2 * units], held[side, i, 1], 1, 1)
            ).astype(BF16)


def output_products(dims, chunk, ids, mine, theirs, weights):
    subs, groups, per_chunk, cap, block = dims
    rows = subs * cap
    depth, units = weights.shape[2:]
    width = depth // 2
    whole = lambda shape: pl.BlockSpec(shape, lambda s, ids: (0,) * len(shape))
    in_specs = [whole(mine.shape), whole(theirs.shape), pl.BlockSpec(memory_space=pltpu.HBM)]
    operands = [ids, mine, theirs, weights]
    out = jax.ShapeDtypeStruct((per_chunk, rows, width), BF16)
    return pl.pallas_call(
        functools.partial(output_kernel, dims, chunk),
        out_shape=(pltpu.HBM((per_chunk, rows, 3 * units), BF16),) + (out,) * 4,
        grid_spec=pltpu.PrefetchScalarGridSpec(
            num_scalar_prefetch=1,
            grid=(1,),
            in_specs=in_specs,
            out_specs=(
                whole((per_chunk, rows, 3 * units)),
            )
            + (whole(out.shape),) * 4,
            scratch_shapes=[
                pltpu.VMEM((2, per_chunk, 3, width, units), BF16),
                pltpu.SemaphoreType.DMA((2,)),
            ],
        ),
        compiler_params=params(BIG),
        cost_estimate=cost(
            per_chunk * rows * 3 * depth * units,
            2 * per_chunk * (3 * depth * units + 2 * rows * depth + 9 * rows * units),
            f"output_{chunk}",
        ),
        name=f"output_{chunk}",
    )(*operands)


def pack_kernel(dims, own_out, own_grad, other_out, other_grad, packed):
    subs, groups, per_chunk, cap, block = dims
    count = gather_group(cap)
    inner, part = count * block, count * cap
    source, place = split_index(iota((inner, 1), 0), block)
    kind, place = split_index(place, cap)
    target = kind * part + source * cap + place
    chooser = (iota((inner, inner), 1) == target).astype(F32).astype(BF16)
    for g in range(subs // count):
        rows = slice(g * part, (g + 1) * part)
        summed = [
            (own[i, rows].astype(F32) + other[i, rows].astype(F32)).astype(BF16)
            for own, other in ((own_out, other_out), (own_grad, other_grad))
            for i in range(per_chunk)
        ]
        packed[g * inner : (g + 1) * inner, :] = dot(
            chooser, jnp.concatenate(summed, axis=0), 1, 0
        ).astype(BF16)


def pack(dims, chunk, parts):
    subs, groups, per_chunk, cap, block = dims
    rows = subs * cap
    width = parts[0].shape[2]
    columns = 384 if width % 384 == 0 else width
    spec = pl.BlockSpec((per_chunk, rows, columns), lambda c: (0, 0, c))
    return pl.pallas_call(
        functools.partial(pack_kernel, dims),
        out_shape=pltpu.HBM((subs * block, width), BF16),
        grid=(width // columns,),
        in_specs=[spec] * 4,
        out_specs=pl.BlockSpec((subs * block, columns), lambda c: (0, c)),
        compiler_params=params(),
        cost_estimate=cost(
            subs * block * 2 * per_chunk * rows * width, 6 * subs * block * width, f"pack_{chunk}"
        ),
        name=f"pack_{chunk}",
    )(*parts)


def chooser_kernel(dims, ids, routes, gates, marks, gates_out, *choosers):
    subs, groups, per_chunk, cap, block = dims
    token_count = routes.shape[0]
    p = pl.program_id(0)
    gates_out[...] = gates[...]
    route = [routes[:, k : k + 1] for k in range(2)]
    sub = iota((token_count, subs), 1)
    hits = [(route[k] == sub).astype(F32) for k in range(2)]
    earlier = (iota((token_count,) * 2, 1) < iota((token_count,) * 2, 0)).astype(BF16)
    before = dot(earlier, (hits[0] + hits[1]).astype(BF16), 1, 0)
    slot = [jnp.sum(hits[k] * before, axis=1, keepdims=True) for k in range(2)]
    slot[1] = slot[1] + (route[0] == route[1]).astype(F32)
    slot = [value.astype(jnp.int32) for value in slot]
    for chunk in range(CHUNKS):
        wanted = marks[0:1, :] + chunk * per_chunk
        place, half, holder = marks[1:2, :], marks[2:3, :], marks[3:4, :]
        match = [
            ((route[k] == wanted) & (slot[k] == place) & (holder == p)).astype(F32)
            for k in range(2)
        ]
        first = (half == 0).astype(F32)
        second = (half == 1).astype(F32)
        choosers[chunk][0:token_count, :] = (match[0] * first).astype(BF16)
        choosers[chunk][token_count : 2 * token_count, :] = (match[1] * first).astype(BF16)
        choosers[chunk][2 * token_count :, :] = ((match[0] + match[1]) * second).astype(BF16)


def return_choosers(dims, ids, routes, gates):
    subs, groups, per_chunk, cap, block = dims
    token_count = routes.shape[0]
    row = np.arange(subs * block)
    device, inner = row // block, row % block
    half, inner = inner // (per_chunk * cap), inner % (per_chunk * cap)
    local, place = inner // cap, inner % cap
    marks = np.zeros((8, subs * block), np.int32)
    marks[0] = device // groups * groups + local
    marks[1] = place
    marks[2] = half
    marks[3] = device % groups
    whole = lambda shape: pl.BlockSpec(shape, lambda p, ids: (0,) * len(shape))
    shape = pltpu.HBM((groups, 3 * token_count, subs * block), BF16)
    spec = pl.BlockSpec((None, 3 * token_count, subs * block), lambda p, ids: (p, 0, 0))
    return pl.pallas_call(
        functools.partial(chooser_kernel, dims),
        out_shape=(jax.ShapeDtypeStruct(gates.shape, F32),) + (shape,) * CHUNKS,
        grid_spec=pltpu.PrefetchScalarGridSpec(
            num_scalar_prefetch=1,
            grid=(groups,),
            in_specs=[whole(routes.shape), whole(gates.shape), whole(marks.shape)],
            out_specs=(whole(gates.shape),) + (spec,) * CHUNKS,
        ),
        compiler_params=params(),
        cost_estimate=cost(0, 2 * CHUNKS * groups * 3 * token_count * subs * block, "choosers"),
        name="choosers",
    )(ids, routes, gates, jnp.asarray(marks))


def gather_kernel(ids, chooser, returned, total):
    total[...] = dot(chooser[...], returned[...], 1, 0)


def gather_rows(ids, chooser, returned):
    groups, picks, rows = chooser.shape
    width = returned.shape[1]
    return pl.pallas_call(
        gather_kernel,
        out_shape=jax.ShapeDtypeStruct((groups, picks, width), F32),
        grid_spec=pltpu.PrefetchScalarGridSpec(
            num_scalar_prefetch=1,
            grid=(groups,),
            in_specs=[
                pl.BlockSpec((None, picks, rows), lambda p, ids: (p, 0, 0)),
                pl.BlockSpec(returned.shape, lambda p, ids: (0, 0)),
            ],
            out_specs=pl.BlockSpec((None, picks, width), lambda p, ids: (p, 0, 0)),
        ),
        compiler_params=params(),
        cost_estimate=cost(groups * picks * rows * width, 4 * groups * picks * width, "gather_rows"),
        name="gather_rows",
    )(ids, chooser, returned)


def combine_kernel(ids, gates, cotangent, chooser, returned, earlier, combined, gate_grad, *direct):
    token_count = gates.shape[0]
    p = pl.program_id(0)
    total = dot(chooser[...], returned[...], 1, 0) + earlier[...]
    picked = [total[k * token_count : (k + 1) * token_count] for k in range(3)]
    layer_out = (gates[:, 0:1] * picked[0] + gates[:, 1:2] * picked[1]).astype(BF16)
    input_grad = picked[2].astype(BF16)
    combined[0] = layer_out
    combined[1] = input_grad
    if direct:
        direct[0][...] = layer_out
        direct[1][...] = input_grad
    grads = cotangent[...].astype(F32)
    lane = iota((token_count, 128), 1)
    term = jnp.where(lane == 0, jnp.sum(grads * picked[0], axis=1, keepdims=True), 0.0)
    term += jnp.where(lane == 1, jnp.sum(grads * picked[1], axis=1, keepdims=True), 0.0)

    @pl.when(p == 0)
    def _():
        gate_grad[...] = term

    @pl.when(p > 0)
    def _():
        gate_grad[...] += term


def combine(dims, width, ids, gates, cotangent, chooser, returned, earlier):
    subs, groups, per_chunk, cap, block = dims
    token_count = gates.shape[0]
    cotangent, cotangent_spec = cotangent
    whole = lambda shape: pl.BlockSpec(shape, lambda p, ids: (0,) * len(shape))
    by_holder = lambda shape: pl.BlockSpec((None,) + shape[1:], lambda p, ids: (p, 0, 0))
    final = jax.ShapeDtypeStruct((token_count, 2 * groups * width), BF16)
    direct = 2 if width % 128 == 0 else 0
    return pl.pallas_call(
        combine_kernel,
        out_shape=(
            jax.ShapeDtypeStruct((2, groups, token_count, width), BF16),
            jax.ShapeDtypeStruct((token_count, 128), F32),
        )
        + (final,) * direct,
        grid_spec=pltpu.PrefetchScalarGridSpec(
            num_scalar_prefetch=1,
            grid=(groups,),
            in_specs=[
                whole(gates.shape),
                cotangent_spec,
                by_holder(chooser.shape),
                whole(returned.shape),
                by_holder(earlier.shape),
            ],
            out_specs=(
                pl.BlockSpec((2, None, token_count, width), lambda p, ids: (0, p, 0, 0)),
                whole((token_count, 128)),
            )
            + (pl.BlockSpec((token_count, width), lambda p, ids: (0, 2 * p + ids[0])),) * direct,
        ),
        compiler_params=params(),
        cost_estimate=cost(
            groups * 3 * token_count * subs * block * width,
            2 * subs * block * (width + 3 * groups * token_count),
        ),
        name="combine",
    )(ids, gates, cotangent, chooser, returned, earlier)


def merge_kernel(ids, other, started_out, started_grad, layer_out, input_grad, moved):
    width = other.shape[3]
    copies = []
    for p in range(other.shape[1]):
        columns = pl.ds(pl.multiple_of((2 * p + 1 - ids[0]) * width, 128), width)
        for i, target in enumerate((layer_out, input_grad)):
            copies.append(
                pltpu.make_async_copy(other.at[i, p], target.at[:, columns], moved.at[p, i])
            )
            copies[-1].start()
    for copy in copies:
        copy.wait()


def merge(ids, own, other, direct):
    _, groups, token_count, width = own.shape
    model_width = 2 * groups * width
    if not direct:
        q = lax.axis_index("dp")
        pair = jnp.stack([jnp.where(q == 0, own, other), jnp.where(q == 0, other, own)], axis=2)
        pair = pair.transpose(0, 3, 1, 2, 4).reshape(2, token_count, model_width)
        return pair[0], pair[1]
    shape = jax.ShapeDtypeStruct((token_count, model_width), BF16)
    free = pl.BlockSpec(memory_space=pl.ANY)
    return pl.pallas_call(
        merge_kernel,
        out_shape=(shape, shape),
        grid_spec=pltpu.PrefetchScalarGridSpec(
            num_scalar_prefetch=1,
            grid=(1,),
            in_specs=[free] * 3,
            out_specs=(free, free),
            scratch_shapes=[pltpu.SemaphoreType.DMA((groups, 2))],
        ),
        input_output_aliases={2: 0, 3: 1},
        compiler_params=params(),
        cost_estimate=cost(0, 8 * token_count * model_width),
        name="merge",
    )(ids, other, *direct)


def pick_acts(chunks, ids, acts, held, arrival):
    per_chunk = acts[0].shape[0]
    local = ids[1] % per_chunk
    for c in range(chunks):

        @pl.when(ids[1] // per_chunk == c)
        def _(c=c):
            pltpu.make_async_copy(acts[c].at[local], held, arrival).start()

    return pltpu.make_async_copy(acts[0].at[local], held, arrival)


def weight_grad_block(features, acts, grads):
    units = acts.shape[1] // 3
    both = dot(features[0], acts[:, : 2 * units], 0, 0).astype(BF16)
    grads[0] = both[:, :units]
    grads[1] = both[:, units:]
    grads[2] = dot(features[1], acts[:, 2 * units :], 0, 0).astype(BF16)


def near_kernel(ids, *refs):
    acts, features = refs[:CHUNKS], refs[CHUNKS : 2 * CHUNKS]
    grads, held, rows, arrivals = refs[2 * CHUNKS :]
    per_chunk = acts[0].shape[0]
    local = ids[1] % per_chunk
    side = pl.program_id(0)
    load = lambda c, s: pltpu.make_async_copy(
        features[c].at[local, s], rows.at[s], arrivals.at[1 + s]
    )

    @pl.when(side == 0)
    def _():
        ready = pick_acts(CHUNKS, ids, acts, held, arrivals.at[0])
        for c in range(CHUNKS):

            @pl.when(ids[1] // per_chunk == c)
            def _(c=c):
                load(c, 0).start()
                load(c, 1).start()

        ready.wait()
        load(0, 0).wait()
        weight_grad_block(rows.at[0], held, grads)

    @pl.when(side == 1)
    def _():
        load(0, 1).wait()
        weight_grad_block(rows.at[1], held, grads)


def near_weight_grads(ids, acts, features):
    rows, triple = acts[0].shape[1:]
    per_chunk = acts[0].shape[0]
    groups = per_chunk * CHUNKS
    width = features[0].shape[4]
    units = triple // 3
    return pl.pallas_call(
        near_kernel,
        out_shape=jax.ShapeDtypeStruct((3, 2 * groups * width, units), BF16),
        grid_spec=pltpu.PrefetchScalarGridSpec(
            num_scalar_prefetch=1,
            grid=(2,),
            in_specs=[pl.BlockSpec(memory_space=pl.ANY)] * (2 * CHUNKS),
            out_specs=pl.BlockSpec(
                (3, width, units),
                lambda s, ids: (0, 2 * ids[1] + jnp.where(s == 0, ids[0], 1 - ids[0]), 0),
            ),
            scratch_shapes=[
                pltpu.VMEM((rows, triple), BF16),
                pltpu.VMEM((2, 2, rows, width), BF16),
                pltpu.SemaphoreType.DMA((3,)),
            ],
        ),
        compiler_params=params(),
        cost_estimate=cost(6 * rows * width * units, 12 * width * units + 8 * rows * width, "near_weight_grads"),
        name="near_weight_grads",
    )(ids, *acts, *features)


def far_kernel(count, ids, *refs):
    acts, features = refs[:CHUNKS], refs[CHUNKS : CHUNKS + count]
    grads, held, arrival = refs[-3:]
    step = pl.program_id(0)

    @pl.when(step == 0)
    def _():
        pick_acts(CHUNKS, ids, acts, held, arrival).wait()

    for index in range(count):

        @pl.when(step == index)
        def _(index=index):
            weight_grad_block(features[index], held, grads)


def far_weight_grads(ids, acts, far, grads):
    rows, triple = acts[0].shape[1:]
    units = triple // 3
    operands = [value for pair in far for value in pair]
    count = len(operands)
    width = operands[0].shape[2]

    def target(s, ids):
        holder = ids[1] ^ (1 + s // 2)
        return 0, 2 * holder + jnp.where(s % 2 == 0, ids[0], 1 - ids[0]), 0

    return pl.pallas_call(
        functools.partial(far_kernel, count),
        out_shape=jax.ShapeDtypeStruct(grads.shape, BF16),
        grid_spec=pltpu.PrefetchScalarGridSpec(
            num_scalar_prefetch=1,
            grid=(count,),
            in_specs=[pl.BlockSpec(memory_space=pl.ANY)] * CHUNKS
            + [pl.BlockSpec((2, rows, width), lambda s, ids: (0, 0, 0))] * count
            + [pl.BlockSpec(memory_space=pl.ANY)],
            out_specs=pl.BlockSpec((3, width, units), target),
            scratch_shapes=[pltpu.VMEM((rows, triple), BF16), pltpu.SemaphoreType.DMA],
        ),
        input_output_aliases={1 + CHUNKS + count: 0},
        compiler_params=params(),
        cost_estimate=cost(
            3 * rows * count * width * units, 6 * count * width * units + 4 * count * rows * width,
            "far_weight_grads",
        ),
        name="far_weight_grads",
    )(ids, *acts, *operands, grads)


def choose(values, index):
    result = values[0]
    for i in range(1, len(values)):
        result = jnp.where(index == i, values[i], result)
    return result


def together(*values):
    return lax.optimization_barrier(values)


def swap_cores(value):
    return lax.ppermute(value, "dp", [(0, 1), (1, 0)])


def swap_holders(value, mask):
    size = lax.axis_size("expert")
    return lax.ppermute(value, "expert", [(source, source ^ mask) for source in range(size)])


def shards(tokens, cotangent, routes, gate_values, weights):
    groups, depth = weights.shape[:2]
    token_count, top_count = routes.shape
    subs = lax.axis_size("expert")
    cap = 5 * token_count * top_count // (4 * subs)
    per_chunk = groups // CHUNKS
    block = 2 * per_chunk * cap
    width = depth // 2
    dims = (subs, groups, per_chunk, cap, block)
    core = lax.axis_index("dp")
    holder = lax.axis_index("expert") % groups
    ids = jnp.stack([core, holder]).astype(jnp.int32)
    weights = weights[:, :, :, 0, :].transpose(0, 2, 1, 3)
    own_tokens = quarter(tokens, groups, width)
    own_cotangent = quarter(cotangent, groups, width)

    aligned = width % 128 == 0
    whole_or_own = (tokens, cotangent) if aligned else (own_tokens[0], own_cotangent[0])

    def exchange(rows):
        blocks = rows.reshape(subs, block, width)
        moved = lax.all_to_all(blocks, "expert", split_axis=0, concat_axis=0, tiled=True)
        return moved.reshape(subs * block, width)

    sent = dispatch(dims, 0, width, routes.T, gate_values.T, *whole_or_own)
    sent, tokens, cotangent = together(sent, tokens, cotangent)
    arrived = [exchange(sent)]

    def columns(mask):
        first = (2 * (holder ^ mask) + core) * width
        parts = [
            lax.dynamic_slice_in_dim(value, first, width, 1) for value in (tokens, cotangent)
        ]
        return jnp.stack(parts)

    info = jnp.concatenate([routes.T.astype(F32), gate_values.T], axis=0)
    infos = [info] + [swap_holders(info, mask) for mask in range(1, groups)]
    parts = [columns(0)] + [swap_holders(columns(mask), mask) for mask in range(1, groups)]
    gates, *choosers = return_choosers(dims, ids, routes, gate_values)
    peers = [list(range(p, subs, groups)) for p in range(groups)]
    for c in range(1, CHUNKS):
        sent = group_dispatch(dims, c, infos, parts)
        sent, gates, *choosers = together(sent, gates, *choosers)
        if c == 1:
            arrived[0], _ = together(arrived[0], sent)
        moved = lax.all_to_all(
            sent.reshape(subs // groups, groups * block, width),
            "expert",
            split_axis=0,
            concat_axis=0,
            tiled=True,
            axis_index_groups=peers,
        )
        arrived.append(moved.reshape(subs * block, width))
    features, acts, mine, theirs, returned, leaving = [], [], [], [], [], []
    for c in range(CHUNKS):
        others = [swap_cores(part) for part in jnp.split(arrived[c], 2)]
        rows, partial, *leaving = partial_products(
            dims, c, ids, arrived[c], others, weights, leaving[0] if leaving else None
        )
        features.append(rows)
        if c + 1 < CHUNKS:
            arrived[c + 1], _ = together(arrived[c + 1], partial)
        mask = 1
        while mask < groups // 2:
            partial = (partial.astype(F32) + swap_holders(partial, mask).astype(F32)).astype(BF16)
            mask *= 2
        mine.append(partial)
        theirs.append(swap_holders(partial, mask))
    if not leaving:
        by_sub = [features[s // per_chunk][s % per_chunk, 0] for s in range(groups)]
        leaving = [choose(by_sub, holder ^ mask) for mask in range(1, groups)]
    theirs[0], _, *leaving = together(theirs[0], mine[-1], *leaving)
    for c in range(CHUNKS):
        active, *parts = output_products(dims, c, ids, mine[c], theirs[c], weights)
        acts.append(active)
        parts[2:] = [swap_cores(part) for part in parts[2:]]
        packed = pack(dims, c, parts)
        if c + 1 < CHUNKS:
            theirs[c + 1], _ = together(theirs[c + 1], packed)
        if c > 0:
            packed, returned[c - 1] = together(packed, returned[c - 1])
            weight_grad = near_weight_grads(ids, acts, features)
        returned.append(exchange(packed))
    theirs[-1], *leaving = together(theirs[-1], *leaving)
    earlier = gather_rows(ids, choosers[0], returned[0])
    for c in range(1, CHUNKS - 1):
        earlier = earlier + gather_rows(ids, choosers[c], returned[c])
    far = []
    for mask in range(1, groups):
        near = swap_holders(leaving[mask - 1], mask)
        near, weight_grad, earlier = together(near, weight_grad, earlier)
        far.append((near, swap_cores(near)))
    weight_grad = far_weight_grads(ids, acts, far, weight_grad)
    returned[-1], earlier, weight_grad = together(returned[-1], earlier, weight_grad)
    combined, gate_part, *direct = combine(
        dims, width, ids, gates, own_cotangent, choosers[-1], returned[-1], earlier
    )
    layer_out, input_grad = merge(ids, combined, swap_cores(combined), direct)
    gate_grad = (gate_part + swap_cores(gate_part))[:, :top_count]
    weight_grad = weight_grad.transpose(1, 0, 2).reshape(1, groups * depth, 3, 1, -1)
    return layer_out, input_grad, gate_grad, weight_grad


def solution(mesh):
    in_specs = (
        P("expert", None),
        P("expert", None),
        P("expert", None),
        P("expert", None),
        P(None, "expert", None, "dp", None),
    )
    out_specs = (
        P("expert", None),
        P("expert", None),
        P("expert", None),
        P("expert", None, None, "dp", None),
    )
    return jax.shard_map(shards, mesh=mesh, in_specs=in_specs, out_specs=out_specs, check_vma=False)
```
